512 devices in a mesh: pixel: 16 (over x, z_hi), trow: 8 (over y), tcol: 4 (over z_lo, core).
Axes of the slice: x: 4, y: 8, z: 8 (z_hi: 4, z_lo: 2; z = z_hi * 2 + z_lo), core: 2. Of those that a mesh axis runs over, the one named last changes fastest.
Arguments:
- counts: int32 [512, 65536], P(('trow', 'tcol'), 'pixel'), may hold values from 2 to 62
- labels: int32 [65536, 1], P('pixel'), may hold values from 0 to 63, as said below
- pixel_mask: int32 [65536], P('pixel'), may hold values from 0 to 1, as said below
- dark_level: float32 [65536], P('pixel'), may hold values from 0 to 3.5
- flat_field: float32 [65536], P('pixel'), may hold values from 0.3 to 3
Outputs:
- two_time: float32 [64, 512, 512], P('pixel', 'trow', 'tcol')
- lag_means: float32 [64, 512], P('pixel')
The draws below stay inside these ranges and needn't reach their ends.
Inputs may be any that keep to these rules, and one draw needn't show every extreme that they name: `labels`: among the pixels of one index of pixel (aligned blocks of 4096 pixels), no cycle holds more than 128 pixels, and some cycle holds exactly 128; every cycle has pixels in every block. `pixel_mask`: all pixels of one cycle are 0.
All inputs are finite; a program needn't handle non-finite values.
Results may differ from the reference program's by a relative error of at most 0.0003.
Values may be sent and summed in bfloat16 or wider, within the bound.
No kernel may reach another device: no remote copies, remote signals or barrier semaphores. Data moves between devices by JAX's collectives and lax.ppermute only.
A program may use at most 64 MiB of HBM per device.

```python
import math
import jax
import jax.numpy as jnp
from jax import lax

CYCLES = 64
FRAMES = 512
PIX_DEV = 4096
CAP = 128
PIXELS = 65536
N_PIXEL = 16
N_TROW = 8
N_TCOL = 4


def cycle_layout(key):
    half = CAP // 2
    layout_key = jax.random.fold_in(key, 101)

    def one_block(block_key):
        keys = jax.random.split(block_key, 5)
        order = jax.random.permutation(keys[0], CYCLES).astype(jnp.int32)
        first = jax.random.randint(keys[1], (1,), 1, half).astype(jnp.int32)
        second = jax.random.randint(keys[2], (1,), 1, half).astype(jnp.int32)
        split_at = jax.random.randint(keys[3], ((CYCLES - 4) // 2,), 1, 2 * half).astype(jnp.int32)
        leading = jnp.full((1,), 2 * half, jnp.int32)
        quad = jnp.concatenate([leading, first, second, leading - first - second])
        pairs = jnp.stack([split_at, 2 * half - split_at], axis=1).reshape(-1)
        slot_sizes = jnp.concatenate([quad, pairs]).astype(jnp.int32)
        cycle_sizes = jnp.zeros((CYCLES,), jnp.int32).at[order].set(slot_sizes)
        ends = jnp.cumsum(cycle_sizes).astype(jnp.int32)
        positions = jnp.arange(PIX_DEV, dtype=jnp.int32)
        sorted_labels = jnp.sum((ends[None, :] <= positions[:, None]).astype(jnp.int32), axis=1)
        scatter = jax.random.permutation(keys[4], PIX_DEV).astype(jnp.int32)
        return sorted_labels[scatter]
    block_keys = jax.random.split(layout_key, N_PIXEL)
    labels = jax.vmap(one_block)(block_keys).reshape(-1).astype(jnp.int32)
    rate_key = jax.random.fold_in(key, 202)
    steps = jnp.arange(CYCLES, dtype=jnp.int32) * 7 // CYCLES
    rate_table = jnp.right_shift(jnp.full((CYCLES,), 512, jnp.int32), steps)
    cycle_rate = rate_table[jax.random.permutation(rate_key, CYCLES).astype(jnp.int32)]
    dead_cycle = jax.random.randint(jax.random.fold_in(key, 303), (), 0, CYCLES).astype(jnp.int32)
    return (labels, cycle_rate, dead_cycle)


def draw_labels(key, part):
    labels, cycle_rate, dead_cycle = cycle_layout(key)
    return labels.reshape(PIXELS, 1)


def draw_pixel_mask(key, part):
    labels, cycle_rate, dead_cycle = cycle_layout(key)
    key = jax.random.fold_in(key, 11)
    usable = jax.random.randint(key, (PIXELS,), 0, 16) < 15
    return jnp.where(usable & (labels != dead_cycle), 1, 0).astype(jnp.int32)


def draw_counts(key, part):
    labels, cycle_rate, dead_cycle = cycle_layout(key)
    key = jax.random.fold_in(key, 7)
    pixel_rate = cycle_rate[labels]

    def advance(level, frame):
        frame_key = jax.random.fold_in(key, frame)
        keys = jax.random.split(frame_key, 3)
        renew = jax.random.randint(keys[0], (PIXELS,), 0, 1024) < pixel_rate
        fresh = jax.random.randint(keys[1], (PIXELS,), 2, 60).astype(jnp.int32)
        level = jnp.where(renew | (frame == 0), fresh, level)
        noise = jax.random.randint(keys[2], (PIXELS,), 0, 4).astype(jnp.int32)
        return (level, level + noise)
    start = jnp.zeros((PIXELS,), jnp.int32)
    final, frames = lax.scan(advance, start, jnp.arange(FRAMES, dtype=jnp.int32))
    return frames.astype(jnp.int32)


def shard_levels(key, dims, cuts, smallest, high):
    factor_of, own = 1.0, jax.random.fold_in(key, 6)
    for axis_at, parts in cuts:
        draws = jnp.exp(jax.random.uniform(jax.random.fold_in(own, axis_at), (parts,), jnp.float32, smallest / len(cuts), high / len(cuts)))
        factor_of = factor_of * jnp.repeat(draws, dims[axis_at] // parts).reshape([-1 if axis == axis_at else 1 for axis in range(len(dims))])
    return factor_of


def setup_inputs(seed: int = 0) -> dict:
    key_of = jax.random.split(jax.random.key(seed), 6)
    return {
        "counts": draw_counts(jax.random.fold_in(key_of[5], 71), 0),
        "labels": draw_labels(jax.random.fold_in(key_of[5], 71), 0),
        "pixel_mask": draw_pixel_mask(jax.random.fold_in(key_of[5], 71), 0),
        "dark_level": jnp.clip(3.5 * jax.random.uniform(key_of[3], (PIXELS,), jnp.float32) ** shard_levels(key_of[3], (PIXELS,), ((0, 16),), -0.2, 0.2), 0.0, 3.5),
        "flat_field": jnp.clip(jnp.exp(math.log(3.0) - 2.3025851 * jax.random.uniform(key_of[4], (PIXELS,), jnp.float32) ** shard_levels(key_of[4], (PIXELS,), ((0, 16),), -0.2, 0.2)), 0.3, 3.0),
    }


def slot_table(block_labels):
    pixels = block_labels.shape[0]
    ordering = jnp.argsort(block_labels, stable=True).astype(jnp.int32)
    member = block_labels[:, None] == jnp.arange(CYCLES, dtype=jnp.int32)[None, :]
    cycle_sizes = jnp.sum(member.astype(jnp.int32), axis=0)
    starts = jnp.cumsum(cycle_sizes) - cycle_sizes
    offset = jnp.arange(CAP, dtype=jnp.int32)
    places = jnp.minimum(starts[:, None] + offset[None, :], pixels - 1)
    return ordering[places], offset[None, :] < cycle_sizes[:, None]


def reference(counts, labels, pixel_mask, dark_level, flat_field):
    corrected = (flat_field * pixel_mask.astype(jnp.float32) * (counts.astype(jnp.float32) - dark_level)).astype(jnp.bfloat16)
    blocks = labels[:, 0].reshape(N_PIXEL, PIX_DEV)
    table, usable = jax.vmap(slot_table)(blocks)
    table = table + (jnp.arange(N_PIXEL, dtype=jnp.int32) * PIX_DEV)[:, None, None]
    live = jnp.where(usable, pixel_mask[table], 0).astype(jnp.float32)
    sizes_all = jnp.sum(live, axis=(0, 2))
    sub_frames = FRAMES // (N_TROW * N_TCOL)
    column_ids = jnp.arange(FRAMES, dtype=jnp.int32)
    tile_k = column_ids // (N_TROW * sub_frames)
    rest = column_ids % (N_TROW * sub_frames)
    permuted = (rest // sub_frames) * N_TCOL * sub_frames + tile_k * sub_frames + rest % sub_frames
    row_ids = jnp.arange(FRAMES, dtype=jnp.int32)[:, None]
    lag_ids = jnp.arange(FRAMES, dtype=jnp.int32)[None, :]
    upper = row_ids + lag_ids < FRAMES
    zero_value = jnp.zeros((), jnp.bfloat16)

    def one_cycle(cycle_index):
        columns = lax.dynamic_index_in_dim(table, cycle_index, 1, keepdims=False).reshape(-1)
        allowed = lax.dynamic_index_in_dim(usable, cycle_index, 1, keepdims=False).reshape(-1)
        cycle_data = jnp.where(allowed[None, :], corrected[:, columns], zero_value)
        gram = jnp.dot(cycle_data, cycle_data.T, preferred_element_type=jnp.float32)
        cycle_sums = jnp.maximum(jnp.sum(cycle_data, axis=1, dtype=jnp.float32), 1.0)
        correlation = sizes_all[cycle_index] * gram / (cycle_sums[:, None] * cycle_sums[None, :])
        skewed = jnp.pad(correlation.reshape(-1), (0, FRAMES)).reshape(FRAMES, FRAMES + 1)[:, :FRAMES]
        summed = jnp.sum(jnp.where(upper, skewed, 0.0), axis=0)
        lag_means = summed / (FRAMES - jnp.arange(FRAMES)).astype(jnp.float32)
        return correlation[:, permuted], lag_means

    two_time, lag_means = lax.map(one_cycle, jnp.arange(CYCLES, dtype=jnp.int32))
    return two_time, lag_means
```

```python
import jax
import jax.numpy as jnp
from jax import lax
from jax.experimental import pallas as pl
from jax.experimental.pallas import tpu as pltpu
from jax.sharding import PartitionSpec as P

CYCLES = 64
FRAMES = 512
CAP = 128
HALF = CAP // 2
PIX = 4096
N_PIXEL = 16
N_TROW = 8
N_TCOL = 4
SUB = 16
OWNED = CYCLES // N_PIXEL
COLS = N_TROW * SUB
PAIRS = N_PIXEL // 2
ROWS = N_TCOL * SUB
LANES = 128
CHUNK = 512
RANK = 256
F32 = jnp.float32
BF16 = jnp.bfloat16


def dot_t(a, b):
    return lax.dot_general(a, b, (((1,), (1,)), ((), ())), preferred_element_type=F32)


def dot_n(a, b):
    return jnp.dot(a, b, preferred_element_type=F32)


def three_parts(x):
    hi = x.astype(BF16).astype(F32)
    rest = x - hi
    mid = rest.astype(BF16).astype(F32)
    return hi, mid, rest - mid


def slot_kernel(odd_ref, counts_ref, labels_ref, mask_ref, dark_ref, flat_ref, out_ref):
    odd = odd_ref[0] == 1
    live = mask_ref[...].astype(F32)
    frames = (
        flat_ref[...] * live * (counts_ref[...].astype(F32) - dark_ref[...])
    ).astype(BF16)
    labels = labels_ref[...]

    before = lax.broadcasted_iota(jnp.int32, (RANK, RANK + LANES), 0)
    at = lax.broadcasted_iota(jnp.int32, (RANK, RANK + LANES), 1)
    ahead = jnp.where((before < at) | (at >= RANK), 1.0, 0.0).astype(BF16)
    cycle_of_row = lax.broadcasted_iota(jnp.int32, (CYCLES, RANK), 0)
    offset = jnp.zeros((CYCLES, LANES), F32)
    usable = jnp.zeros((CYCLES, LANES), F32)
    ranks = []
    for c in range(PIX // RANK):
        span = slice(c * RANK, (c + 1) * RANK)
        member = jnp.where(labels[:, span] == cycle_of_row, 1.0, 0.0)
        counted = dot_n(member.astype(BF16), ahead)
        place = counted[:, :RANK] + jnp.concatenate([offset] * (RANK // LANES), axis=1)
        ranks.append(jnp.sum(member * place, axis=0, keepdims=True))
        offset = offset + counted[:, RANK:]
        usable = usable + dot_n(
            (member * live[:, span]).astype(BF16), jnp.ones((RANK, LANES), BF16)
        )
    rank = jnp.concatenate(ranks, axis=1).astype(BF16)
    label16 = labels.astype(F32).astype(BF16)

    slots = jnp.zeros((CYCLES * SUB, CAP), F32)
    slot_of_row = lax.broadcasted_iota(jnp.int32, (CAP, CHUNK), 0).astype(F32).astype(BF16)
    one = jnp.ones((CAP, CHUNK), BF16)
    none = jnp.zeros((SUB, CHUNK), BF16)
    for c in range(PIX // CHUNK):
        span = slice(c * CHUNK, (c + 1) * CHUNK)
        here = jnp.broadcast_to(label16[:, span], (SUB, CHUNK))
        chunk = frames[:, span]
        left = jnp.concatenate(
            [jnp.where(here == jnp.array(r, BF16), chunk, none) for r in range(CYCLES)], axis=0
        )
        right = jnp.where(
            jnp.broadcast_to(rank[:, span], (CAP, CHUNK)) == slot_of_row, one, jnp.zeros_like(one)
        )
        slots = slots + dot_t(left, right)

    sums = dot_n(slots.astype(BF16), jnp.ones((CAP, LANES), BF16))
    hi, mid, lo = three_parts(sums)
    lane = lax.broadcasted_iota(jnp.int32, (CYCLES * SUB, LANES), 1)
    first = jnp.where(odd, 0, HALF)
    extra = jnp.where(lane == first, hi, 0.0)
    extra = jnp.where(lane == first + 1, mid, extra)
    extra = jnp.where(lane == first + 2, lo, extra)
    extra = extra.reshape(CYCLES, SUB, LANES)
    lane = lane.reshape(CYCLES, SUB, LANES)
    extra = jnp.where(lane == first + 3, usable[:, None, :], extra)
    turned = pltpu.roll(slots, HALF, axis=1)
    in_place = jnp.where(odd, turned, slots).reshape(CYCLES, SUB, LANES)
    moved = jnp.where(odd, slots, turned).reshape(CYCLES, SUB, LANES)
    data = (lane >= HALF) == odd
    out_ref[:, 0] = jnp.where(data, in_place, extra).astype(BF16)
    out_ref[:, 1] = jnp.where(data, moved, extra).astype(BF16)


def pack_kernel(in_ref, out_ref):
    low = lax.broadcasted_iota(jnp.int32, (N_TROW, SUB, LANES), 2) < HALF
    total = jnp.zeros((COLS, LANES), F32)
    for pair in range(PAIRS):
        even = in_ref[2 * pair].astype(F32)
        odd = in_ref[2 * pair + 1].astype(F32)
        out_ref[pair * COLS : (pair + 1) * COLS] = (
            jnp.where(low, even, odd).reshape(COLS, LANES).astype(BF16)
        )
        total = total + jnp.where(low, odd, even).reshape(COLS, LANES)
    lane = lax.broadcasted_iota(jnp.int32, (COLS, LANES), 1) % HALF
    sums = jnp.sum(jnp.where(lane < 3, total, 0.0), axis=1, keepdims=True)
    usable = jnp.sum(jnp.where(lane == 3, total, 0.0), axis=1, keepdims=True)
    hi, mid, lo = three_parts(jnp.broadcast_to(sums, (COLS, LANES)).T[:SUB])
    n_hi, n_lo, _ = three_parts(jnp.broadcast_to(usable, (COLS, LANES)).T[:SUB])
    row = lax.broadcasted_iota(jnp.int32, (SUB, COLS), 0)
    tail = jnp.where(row == 0, hi, 0.0)
    tail = jnp.where(row == 1, mid, tail)
    tail = jnp.where(row == 2, lo, tail)
    tail = jnp.where(row == 3, n_hi, tail)
    tail = jnp.where(row == 4, n_lo, tail)
    out_ref[PAIRS * COLS :] = tail.astype(BF16)


def gram_kernel(me_ref, x0_ref, x1_ref, x2_ref, x3_ref, out_ref, all_ref, own_ref):
    me = me_ref[0]
    depth = PAIRS * LANES
    t_row = lax.broadcasted_iota(jnp.int32, (COLS, FRAMES), 0)
    t_col = lax.broadcasted_iota(jnp.int32, (COLS, FRAMES), 1)
    stats = jnp.zeros((SUB, FRAMES), F32)
    for d, ref in enumerate((x0_ref, x1_ref, x2_ref, x3_ref)):
        k = me ^ d
        for j in range(N_TROW):
            rows = pl.ds(pl.multiple_of(j * ROWS + k * SUB, SUB), SUB)
            for pair in range(PAIRS):
                at = pair * COLS + j * SUB
                all_ref[rows, pair * LANES : (pair + 1) * LANES] = ref[at : at + SUB]
        goes_to = (t_row // SUB) * ROWS + k * SUB + t_row % SUB
        spread = jnp.where(goes_to == t_col, 1.0, 0.0).astype(BF16)
        stats = stats + dot_n(ref[PAIRS * COLS :], spread)
    for pair in range(PAIRS):
        own_ref[:, pair * LANES : (pair + 1) * LANES] = x0_ref[pair * COLS : (pair + 1) * COLS]

    own = x0_ref[PAIRS * COLS :].astype(F32)
    own_inv = 1.0 / jnp.maximum(own[0:1] + own[1:2] + own[2:3], 1.0)
    usable = (own[3:4] + own[4:5])[:, 0:1]
    inv = 1.0 / jnp.maximum(stats[0:1] + stats[1:2] + stats[2:3], 1.0)
    inv_col = jnp.broadcast_to(inv, (LANES, FRAMES)).T

    tile = dot_t(all_ref[...], own_ref[...])
    tile = tile * (inv_col * (own_inv * usable))

    lags = jnp.zeros((1, FRAMES), F32)
    flip_row = lax.broadcasted_iota(jnp.int32, (LANES, LANES), 0)
    flip_col = lax.broadcasted_iota(jnp.int32, (LANES, LANES), 1)
    flip = jnp.where(flip_row + flip_col == LANES - 1, 1.0, 0.0).astype(BF16)
    for b in range(FRAMES // LANES):
        start = b * LANES
        width = FRAMES - start
        back = dot_n(flip, all_ref[start : start + LANES]).astype(BF16)
        back_stats = dot_n(stats[:, start : start + LANES].astype(BF16), flip)
        back_sums = back_stats[0:1] + back_stats[1:2] + back_stats[2:3]
        back_inv = jnp.broadcast_to(1.0 / jnp.maximum(back_sums, 1.0), (LANES, LANES)).T[:, 0:1]
        block = dot_t(back, all_ref[start:])
        row = lax.broadcasted_iota(jnp.int32, (LANES, width), 0)
        col = lax.broadcasted_iota(jnp.int32, (LANES, width), 1)
        block = jnp.where(row + col >= LANES - 1, block * (back_inv * inv[:, start:]), 0.0)
        block = pltpu.roll(block, width - LANES + 1, axis=1, stride=1, stride_axis=0)
        part = jnp.sum(block, axis=0, keepdims=True)
        if width < FRAMES:
            part = jnp.concatenate([part, jnp.zeros((1, start), F32)], axis=1)
        lags = lags + part
    remaining = (FRAMES - lax.broadcasted_iota(jnp.int32, (1, FRAMES), 1)).astype(F32)
    lags = lags * usable / remaining

    for i in range(N_TROW):
        out_ref[i, :ROWS] = tile[i * ROWS : (i + 1) * ROWS]
        for b in range(FRAMES // LANES):
            out_ref[i, ROWS + b : ROWS + b + 1] = lags[:, b * LANES : (b + 1) * LANES]
        out_ref[i, ROWS + 4 :] = jnp.zeros((4, LANES), F32)


def join_kernel(in_ref, tile_ref, lag_ref):
    for c in range(OWNED):
        both = in_ref[2 * c] + in_ref[2 * c + 1]
        tile_ref[c] = both[:ROWS]
        for b in range(FRAMES // LANES):
            lag_ref[c : c + 1, b * LANES : (b + 1) * LANES] = both[ROWS + b : ROWS + b + 1]


def call(body, out_shape, n_in, scalars=0, scratch=(), flops=0, size=0):
    vmem = pl.BlockSpec(memory_space=pltpu.VMEM)
    smem = pl.BlockSpec(memory_space=pltpu.SMEM)
    many = isinstance(out_shape, tuple)
    return pl.pallas_call(
        body,
        out_shape=out_shape,
        in_specs=[smem] * scalars + [vmem] * n_in,
        out_specs=(vmem,) * len(out_shape) if many else vmem,
        scratch_shapes=list(scratch),
        compiler_params=pltpu.CompilerParams(vmem_limit_bytes=32 * 1024 * 1024),
        cost_estimate=pl.CostEstimate(flops=flops, bytes_accessed=size, transcendentals=0),
    )


def per_device(counts, labels, pixel_mask, dark_level, flat_field):
    odd = (lax.axis_index("pixel") % 2).astype(jnp.int32).reshape(1)
    me = lax.axis_index("tcol").astype(jnp.int32).reshape(1)
    payload = call(
        slot_kernel,
        jax.ShapeDtypeStruct((CYCLES, 2, SUB, LANES), BF16),
        5,
        scalars=1,
        flops=2 * CYCLES * SUB * CAP * PIX,
        size=1 << 20,
    )(
        odd,
        counts,
        labels.reshape(1, PIX),
        pixel_mask.reshape(1, PIX),
        dark_level.reshape(1, PIX),
        flat_field.reshape(1, PIX),
    )
    arrived = lax.all_to_all(
        payload.reshape(2 * CYCLES, SUB, LANES), ("pixel", "trow"), 0, 0, tiled=True
    )
    packed = call(
        pack_kernel,
        jax.ShapeDtypeStruct((PAIRS * COLS + SUB, LANES), BF16),
        1,
        flops=1 << 20,
        size=3 << 18,
    )(arrived.reshape(N_PIXEL, N_TROW, SUB, LANES))
    beside = lax.ppermute(packed, "tcol", [(k, k ^ 1) for k in range(N_TCOL)])
    across = lax.ppermute(packed, "tcol", [(k, k ^ 2) for k in range(N_TCOL)])
    corner = lax.ppermute(across, "tcol", [(k, k ^ 1) for k in range(N_TCOL)])
    depth = PAIRS * LANES
    sends = call(
        gram_kernel,
        jax.ShapeDtypeStruct((N_TROW, ROWS + 8, LANES), F32),
        4,
        scalars=1,
        scratch=[pltpu.VMEM((FRAMES, depth), BF16), pltpu.VMEM((COLS, depth), BF16)],
        flops=2 * FRAMES * FRAMES * depth,
        size=3 << 19,
    )(me, packed, beside, across, corner)
    gets = lax.all_to_all(sends, "trow", 0, 0, tiled=True)
    return call(
        join_kernel,
        (
            jax.ShapeDtypeStruct((OWNED, ROWS, COLS), F32),
            jax.ShapeDtypeStruct((OWNED, FRAMES), F32),
        ),
        1,
        flops=1 << 16,
        size=1 << 19,
    )(gets)


def solution(mesh):
    placed = (P(("trow", "tcol"), "pixel"), P("pixel", None), P("pixel"), P("pixel"), P("pixel"))
    return jax.shard_map(
        per_device,
        mesh=mesh,
        in_specs=placed,
        out_specs=(P("pixel", "trow", "tcol"), P("pixel", None)),
        check_vma=False,
    )
```

```python
import jax
import jax.numpy as jnp
from jax import lax
from jax.experimental import pallas as pl
from jax.experimental.pallas import tpu as pltpu
from jax.sharding import Mesh
from jax.sharding import PartitionSpec as P

CYCLES = 64
FRAMES = 512
CAP = 128
SPLIT = 4
PART = CAP // SPLIT
PIX = 4096
N_PIXEL = 16
N_TROW = 8
N_TCOL = 4
N_Z = 2
SUB = 16
OWNED = CYCLES // N_PIXEL
COLS = N_TROW * SUB
QUADS = N_PIXEL // SPLIT
SEEN = N_TROW * N_Z * SUB
ROWS = N_TCOL * SUB
LANES = 128
CHUNK = 512
RANK = 256
F32 = jnp.float32
BF16 = jnp.bfloat16


def dot_t(a, b):
    return lax.dot_general(a, b, (((1,), (1,)), ((), ())), preferred_element_type=F32)


def dot_n(a, b):
    return jnp.dot(a, b, preferred_element_type=F32)


def three_parts(x):
    hi = x.astype(BF16).astype(F32)
    rest = x - hi
    mid = rest.astype(BF16).astype(F32)
    return hi, mid, rest - mid


def slot_kernel(turn_ref, counts_ref, labels_ref, mask_ref, dark_ref, flat_ref, out_ref):
    turn = turn_ref[0]
    live = mask_ref[...].astype(F32)
    frames = (
        flat_ref[...] * live * (counts_ref[...].astype(F32) - dark_ref[...])
    ).astype(BF16)
    labels = labels_ref[...]

    before = lax.broadcasted_iota(jnp.int32, (RANK, RANK + LANES), 0)
    at = lax.broadcasted_iota(jnp.int32, (RANK, RANK + LANES), 1)
    ahead = jnp.where((before < at) | (at >= RANK), 1.0, 0.0).astype(BF16)
    cycle_of_row = lax.broadcasted_iota(jnp.int32, (CYCLES, RANK), 0)
    offset = jnp.zeros((CYCLES, LANES), F32)
    usable = jnp.zeros((CYCLES, LANES), F32)
    ranks = []
    for c in range(PIX // RANK):
        span = slice(c * RANK, (c + 1) * RANK)
        member = jnp.where(labels[:, span] == cycle_of_row, 1.0, 0.0)
        counted = dot_n(member.astype(BF16), ahead)
        place = counted[:, :RANK] + jnp.concatenate([offset] * (RANK // LANES), axis=1)
        ranks.append(jnp.sum(member * place, axis=0, keepdims=True))
        offset = offset + counted[:, RANK:]
        usable = usable + dot_n(
            (member * live[:, span]).astype(BF16), jnp.ones((RANK, LANES), BF16)
        )
    rank = jnp.concatenate(ranks, axis=1).astype(jnp.int32) + turn * PART
    rank = (rank & (CAP - 1)).astype(F32).astype(BF16)
    label16 = labels.astype(F32).astype(BF16)

    slots = jnp.zeros((CYCLES * SUB, CAP), F32)
    slot_of_row = lax.broadcasted_iota(jnp.int32, (CAP, CHUNK), 0).astype(F32).astype(BF16)
    one = jnp.ones((CAP, CHUNK), BF16)
    none = jnp.zeros((SUB, CHUNK), BF16)
    for c in range(PIX // CHUNK):
        span = slice(c * CHUNK, (c + 1) * CHUNK)
        here = jnp.broadcast_to(label16[:, span], (SUB, CHUNK))
        chunk = frames[:, span]
        left = jnp.concatenate(
            [jnp.where(here == jnp.array(r, BF16), chunk, none) for r in range(CYCLES)], axis=0
        )
        right = jnp.where(
            jnp.broadcast_to(rank[:, span], (CAP, CHUNK)) == slot_of_row, one, jnp.zeros_like(one)
        )
        slots = slots + dot_t(left, right)

    sums = dot_n(slots.astype(BF16), jnp.ones((CAP, LANES), BF16))
    hi, mid, lo = three_parts(sums)
    lane = lax.broadcasted_iota(jnp.int32, (CYCLES * SUB, LANES), 1) % PART
    extra = jnp.where(lane == 0, hi, jnp.where(lane == 1, mid, jnp.where(lane == 2, lo, 0.0)))
    extra = extra.reshape(CYCLES, SUB, LANES)
    extra = jnp.where(lane.reshape(CYCLES, SUB, LANES) == 3, usable[:, None, :], extra)
    slots = slots.reshape(CYCLES, SUB, LANES)
    early, late = slots[:, : SUB // 2], slots[:, SUB // 2 :]
    block = lax.broadcasted_iota(jnp.int32, (CYCLES, SUB // 2, LANES), 2) // PART
    block = (block - turn) & (SPLIT - 1)
    rest = jnp.where(block == 1, extra[:, : SUB // 2], extra[:, SUB // 2 :])
    for part in range(SPLIT):
        first = pltpu.roll(early, (CAP - part * PART) % CAP, axis=2)
        second = pltpu.roll(late, (CAP - part * PART + CAP // 2) % CAP, axis=2)
        tile = jnp.where(block == 0, first, jnp.where(block == 2, second, rest))
        tiles = [tile] if part % 2 == 0 else tiles + [tile]
        if part % 2 == 1:
            rows = slice((part - 1) * SUB // 2, (part + 1) * SUB // 2)
            out_ref[:, rows] = jnp.concatenate(tiles, axis=1).astype(BF16)


def pick(tiles, ahead):
    block = lax.broadcasted_iota(jnp.int32, tiles[0].shape, 2) // PART
    out = tiles[(SPLIT - 1 + ahead) % SPLIT]
    for b in range(SPLIT - 1):
        out = jnp.where(block == b, tiles[(b + ahead) % SPLIT], out)
    return out


def by_frame(early, late):
    half = SUB // 2
    pieces = [x[:, z * half : (z + 1) * half] for z in range(N_Z) for x in (early, late)]
    return jnp.concatenate(pieces, axis=1).reshape(SEEN, LANES)


def pack_kernel(in_ref, out_ref):
    total = jnp.zeros((SEEN, LANES), F32)
    for quad in range(QUADS):
        tiles = [in_ref[SPLIT * quad + s].astype(F32) for s in range(SPLIT)]
        late = pltpu.roll(pick(tiles, 2), CAP // 2, axis=2)
        out_ref[quad * SEEN : (quad + 1) * SEEN] = by_frame(pick(tiles, 0), late).astype(BF16)
        total = total + by_frame(pick(tiles, 3), pick(tiles, 1))
    lane = lax.broadcasted_iota(jnp.int32, (SEEN, LANES), 1) % PART
    sums = jnp.sum(jnp.where(lane < 3, total, 0.0), axis=1, keepdims=True)
    usable = jnp.sum(jnp.where(lane == 3, total, 0.0), axis=1, keepdims=True)
    sums = jnp.broadcast_to(sums, (SEEN, LANES)).T[: SUB // 2]
    usable = jnp.broadcast_to(usable, (SEEN, LANES)).T[: SUB // 2]
    hi, mid, lo = three_parts(sums)
    n_hi, n_lo, _ = three_parts(usable)
    row = lax.broadcasted_iota(jnp.int32, (SUB // 2, SEEN), 0)
    tail = jnp.zeros((SUB // 2, SEEN), F32)
    for i, x in enumerate((hi, mid, lo, n_hi, n_lo)):
        tail = jnp.where(row == i, x, tail)
    tail = jnp.concatenate([tail[:, :LANES], tail[:, LANES:]], axis=0)
    out_ref[QUADS * SEEN :] = tail.astype(BF16)


def gram_kernel(me_ref, x0_ref, x1_ref, out_ref, all_ref, own_ref):
    me = me_ref[0]
    t_row = lax.broadcasted_iota(jnp.int32, (LANES, FRAMES), 0)
    t_col = lax.broadcasted_iota(jnp.int32, (LANES, FRAMES), 1)
    stats = jnp.zeros((SUB // 2, FRAMES), F32)
    for d, ref in enumerate((x0_ref, x1_ref)):
        core = me ^ d
        for j in range(N_TROW):
            for z in range(N_Z):
                first = j * ROWS + z * 2 * SUB + core * SUB
                rows = pl.ds(pl.multiple_of(first, SUB), SUB)
                for quad in range(QUADS):
                    at = quad * SEEN + (j * N_Z + z) * SUB
                    here = ref[at : at + SUB]
                    all_ref[rows, quad * LANES : (quad + 1) * LANES] = here
                    if d == 0:
                        own_ref[z, j * SUB : (j + 1) * SUB, quad * LANES : (quad + 1) * LANES] = here
        tail = ref[QUADS * SEEN :]
        for part in range(SEEN // LANES):
            group = t_row // SUB + part * LANES // SUB
            goes_to = group * 2 * SUB + core * SUB + t_row % SUB
            spread = jnp.where(goes_to == t_col, 1.0, 0.0).astype(BF16)
            stats = stats + dot_n(tail, spread)[part * SUB // 2 : (part + 1) * SUB // 2]

    inv = 1.0 / jnp.maximum(stats[0:1] + stats[1:2] + stats[2:3], 1.0)
    inv_col = jnp.broadcast_to(inv, (LANES, FRAMES)).T
    usable = (stats[3:4] + stats[4:5])[:, 0:1]

    lags = jnp.zeros((1, FRAMES), F32)
    flip_row = lax.broadcasted_iota(jnp.int32, (LANES, LANES), 0)
    flip_col = lax.broadcasted_iota(jnp.int32, (LANES, LANES), 1)
    flip = jnp.where(flip_row + flip_col == LANES - 1, 1.0, 0.0).astype(BF16)
    for b in range(FRAMES // LANES):
        start = b * LANES
        width = FRAMES - start
        back = dot_n(flip, all_ref[start : start + LANES]).astype(BF16)
        back_stats = dot_n(stats[:, start : start + LANES].astype(BF16), flip)
        back_sums = back_stats[0:1] + back_stats[1:2] + back_stats[2:3]
        back_inv = jnp.broadcast_to(1.0 / jnp.maximum(back_sums, 1.0), (LANES, LANES)).T[:, 0:1]
        block = dot_t(back, all_ref[start:])
        row = lax.broadcasted_iota(jnp.int32, (LANES, width), 0)
        col = lax.broadcasted_iota(jnp.int32, (LANES, width), 1)
        block = jnp.where(row + col >= LANES - 1, block * (back_inv * inv[:, start:]), 0.0)
        block = pltpu.roll(block, width - LANES + 1, axis=1, stride=1, stride_axis=0)
        part = jnp.sum(block, axis=0, keepdims=True)
        if width < FRAMES:
            part = jnp.concatenate([part, jnp.zeros((1, start), F32)], axis=1)
        lags = lags + part
    remaining = (FRAMES - lax.broadcasted_iota(jnp.int32, (1, FRAMES), 1)).astype(F32)
    lags = lags * usable / remaining
    tail = jnp.concatenate(
        [lags[:, b * LANES : (b + 1) * LANES] for b in range(FRAMES // LANES)]
        + [jnp.zeros((4, LANES), F32)],
        axis=0,
    )

    own_sums = x0_ref[QUADS * SEEN :].astype(F32)
    for z in range(N_Z):
        pieces = []
        for j in range(N_TROW):
            at = (j * N_Z + z) * SUB
            half = at // LANES * (SUB // 2)
            pieces.append(own_sums[half : half + SUB // 2, at % LANES : at % LANES + SUB])
        own = jnp.concatenate(pieces, axis=1)
        own_inv = usable / jnp.maximum(own[0:1] + own[1:2] + own[2:3], 1.0)
        tile = dot_t(all_ref[...], own_ref[z]) * (inv_col * own_inv)
        for i in range(N_TROW):
            out_ref[i, z, :ROWS] = tile[i * ROWS : (i + 1) * ROWS]
            out_ref[i, z, ROWS:] = tail


def join_kernel(in_ref, tile_ref, lag_ref):
    for c in range(OWNED):
        parts = [in_ref[SPLIT * c + part] for part in range(SPLIT)]
        both = (parts[0] + parts[1]) + (parts[2] + parts[3])
        tile_ref[c] = both[:ROWS]
        for b in range(FRAMES // LANES):
            lag_ref[c : c + 1, b * LANES : (b + 1) * LANES] = both[ROWS + b : ROWS + b + 1]


def call(body, out_shape, n_in, scalars=0, scratch=(), flops=0, size=0):
    vmem = pl.BlockSpec(memory_space=pltpu.VMEM)
    smem = pl.BlockSpec(memory_space=pltpu.SMEM)
    many = isinstance(out_shape, tuple)
    return pl.pallas_call(
        body,
        out_shape=out_shape,
        in_specs=[smem] * scalars + [vmem] * n_in,
        out_specs=(vmem,) * len(out_shape) if many else vmem,
        scratch_shapes=list(scratch),
        compiler_params=pltpu.CompilerParams(vmem_limit_bytes=32 * 1024 * 1024),
        cost_estimate=pl.CostEstimate(flops=flops, bytes_accessed=size, transcendentals=0),
    )


def per_device(counts, labels, pixel_mask, dark_level, flat_field):
    turn = (lax.axis_index("pixel") & (SPLIT - 1)).astype(jnp.int32).reshape(1)
    me = lax.axis_index("core").astype(jnp.int32).reshape(1)
    payload = call(
        slot_kernel,
        jax.ShapeDtypeStruct((CYCLES, SPLIT * SUB // 2, LANES), BF16),
        5,
        scalars=1,
        flops=2 * CYCLES * SUB * CAP * PIX,
        size=1 << 20,
    )(
        turn,
        counts,
        labels.reshape(1, PIX),
        pixel_mask.reshape(1, PIX),
        dark_level.reshape(1, PIX),
        flat_field.reshape(1, PIX),
    )
    arrived = lax.all_to_all(
        payload.reshape(SPLIT * CYCLES, SUB // 2, LANES), ("pixel", "trow", "z"), 0, 0, tiled=True
    )
    packed = call(
        pack_kernel,
        jax.ShapeDtypeStruct((QUADS * SEEN + SUB, LANES), BF16),
        1,
        flops=1 << 20,
        size=3 << 18,
    )(arrived.reshape(N_PIXEL, N_TROW, SUB, LANES))
    beside = lax.ppermute(packed, "core", [(0, 1), (1, 0)])
    depth = QUADS * LANES
    sends = call(
        gram_kernel,
        jax.ShapeDtypeStruct((N_TROW, N_Z, ROWS + 8, LANES), F32),
        2,
        scalars=1,
        scratch=[pltpu.VMEM((FRAMES, depth), BF16), pltpu.VMEM((N_Z, COLS, depth), BF16)],
        flops=2 * FRAMES * FRAMES * depth,
        size=3 << 19,
    )(me, packed, beside)
    gets = lax.all_to_all(
        sends.reshape(N_TROW * N_Z, ROWS + 8, LANES), ("trow", "z"), 0, 0, tiled=True
    )
    return call(
        join_kernel,
        (
            jax.ShapeDtypeStruct((OWNED, ROWS, COLS), F32),
            jax.ShapeDtypeStruct((OWNED, FRAMES), F32),
        ),
        1,
        flops=1 << 16,
        size=1 << 19,
    )(gets)


def solution(mesh):
    fine = Mesh(
        mesh.devices.reshape(N_PIXEL, N_TROW, N_Z, 2), ("pixel", "trow", "z", "core")
    )
    frames = ("trow", "z", "core")
    placed = (P(frames, "pixel"), P("pixel", None), P("pixel"), P("pixel"), P("pixel"))
    return jax.shard_map(
        per_device,
        mesh=fine,
        in_specs=placed,
        out_specs=(P("pixel", "trow", ("z", "core")), P("pixel", None)),
        check_vma=False,
    )
```

```python
import jax
import jax.numpy as jnp
from jax import lax
from jax.experimental import pallas as pl
from jax.experimental.pallas import tpu as pltpu
from jax.sharding import Mesh
from jax.sharding import PartitionSpec as P

CYCLES = 64
FRAMES = 512
CAP = 128
SPLIT = 4
PART = CAP // SPLIT
PIX = 4096
N_PIXEL = 16
N_TROW = 8
N_TCOL = 4
N_Z = 2
SUB = 16
OWNED = CYCLES // N_PIXEL
COLS = N_TROW * SUB
QUADS = N_PIXEL // SPLIT
SEEN = N_TROW * N_Z * SUB
ROWS = N_TCOL * SUB
LANES = 128
CHUNK = 512
RANK = 256
F32 = jnp.float32
BF16 = jnp.bfloat16


def dot_t(a, b):
    return lax.dot_general(a, b, (((1,), (1,)), ((), ())), preferred_element_type=F32)


def dot_n(a, b):
    return jnp.dot(a, b, preferred_element_type=F32)


def three_parts(x):
    hi = x.astype(BF16).astype(F32)
    rest = x - hi
    mid = rest.astype(BF16).astype(F32)
    return hi, mid, rest - mid


def slot_kernel(
    turn_ref,
    labels_hbm,
    mask_hbm,
    dark_hbm,
    flat_hbm,
    counts_hbm,
    out_ref,
    labels_ref,
    mask_ref,
    dark_ref,
    flat_ref,
    counts_ref,
    labels_sem,
    mask_sem,
    dark_sem,
    flat_sem,
    counts_sem,
):
    get_labels = pltpu.make_async_copy(labels_hbm, labels_ref, labels_sem)
    get_mask = pltpu.make_async_copy(mask_hbm, mask_ref, mask_sem)
    get_dark = pltpu.make_async_copy(dark_hbm, dark_ref, dark_sem)
    get_flat = pltpu.make_async_copy(flat_hbm, flat_ref, flat_sem)
    get_counts = pltpu.make_async_copy(counts_hbm, counts_ref, counts_sem)
    for get in (get_labels, get_mask, get_dark, get_flat, get_counts):
        get.start()
    turn = turn_ref[0]
    get_labels.wait()
    get_mask.wait()
    labels = labels_ref[...]
    live = mask_ref[...].astype(F32)

    before = lax.broadcasted_iota(jnp.int32, (RANK, RANK + LANES), 0)
    at = lax.broadcasted_iota(jnp.int32, (RANK, RANK + LANES), 1)
    ahead = jnp.where((before < at) | (at >= RANK), 1.0, 0.0).astype(BF16)
    cycle_of_row = lax.broadcasted_iota(jnp.int32, (CYCLES, RANK), 0)
    offset = jnp.zeros((CYCLES, LANES), F32)
    usable = jnp.zeros((CYCLES, LANES), F32)
    ranks = []
    for c in range(PIX // RANK):
        span = slice(c * RANK, (c + 1) * RANK)
        member = jnp.where(labels[:, span] == cycle_of_row, 1.0, 0.0)
        counted = dot_n(member.astype(BF16), ahead)
        place = counted[:, :RANK] + jnp.concatenate([offset] * (RANK // LANES), axis=1)
        ranks.append(jnp.sum(member * place, axis=0, keepdims=True))
        offset = offset + counted[:, RANK:]
        usable = usable + dot_n(
            (member * live[:, span]).astype(BF16), jnp.ones((RANK, LANES), BF16)
        )
    rank = jnp.concatenate(ranks, axis=1).astype(jnp.int32) + turn * PART
    rank = (rank & (CAP - 1)).astype(F32).astype(BF16)
    label16 = labels.astype(F32).astype(BF16)
    get_dark.wait()
    get_flat.wait()
    get_counts.wait()
    frames = (
        flat_ref[...] * live * (counts_ref[...].astype(F32) - dark_ref[...])
    ).astype(BF16)

    slots = jnp.zeros((CYCLES * SUB, CAP), F32)
    slot_of_row = lax.broadcasted_iota(jnp.int32, (CAP, CHUNK), 0).astype(F32).astype(BF16)
    one = jnp.ones((CAP, CHUNK), BF16)
    none = jnp.zeros((SUB, CHUNK), BF16)
    for c in range(PIX // CHUNK):
        span = slice(c * CHUNK, (c + 1) * CHUNK)
        here = jnp.broadcast_to(label16[:, span], (SUB, CHUNK))
        chunk = frames[:, span]
        left = jnp.concatenate(
            [jnp.where(here == jnp.array(r, BF16), chunk, none) for r in range(CYCLES)], axis=0
        )
        right = jnp.where(
            jnp.broadcast_to(rank[:, span], (CAP, CHUNK)) == slot_of_row, one, jnp.zeros_like(one)
        )
        slots = slots + dot_t(left, right)

    sums = dot_n(slots.astype(BF16), jnp.ones((CAP, LANES), BF16))
    hi, mid, lo = three_parts(sums)
    lane = lax.broadcasted_iota(jnp.int32, (CYCLES * SUB, LANES), 1) % PART
    extra = jnp.where(lane == 0, hi, jnp.where(lane == 1, mid, jnp.where(lane == 2, lo, 0.0)))
    extra = extra.reshape(CYCLES, SUB, LANES)
    extra = jnp.where(lane.reshape(CYCLES, SUB, LANES) == 3, usable[:, None, :], extra)
    slots = slots.reshape(CYCLES, SUB, LANES)
    early, late = slots[:, : SUB // 2], slots[:, SUB // 2 :]
    block = lax.broadcasted_iota(jnp.int32, (CYCLES, SUB // 2, LANES), 2) // PART
    block = (block - turn) & (SPLIT - 1)
    rest = jnp.where(block == 1, extra[:, : SUB // 2], extra[:, SUB // 2 :])
    for part in range(SPLIT):
        first = pltpu.roll(early, (CAP - part * PART) % CAP, axis=2)
        second = pltpu.roll(late, (CAP - part * PART + CAP // 2) % CAP, axis=2)
        tile = jnp.where(block == 0, first, jnp.where(block == 2, second, rest))
        tiles = [tile] if part % 2 == 0 else tiles + [tile]
        if part % 2 == 1:
            rows = slice((part - 1) * SUB // 2, (part + 1) * SUB // 2)
            out_ref[:, rows] = jnp.concatenate(tiles, axis=1).astype(BF16)


def pick(tiles, ahead):
    block = lax.broadcasted_iota(jnp.int32, tiles[0].shape, 2) // PART
    out = tiles[(SPLIT - 1 + ahead) % SPLIT]
    for b in range(SPLIT - 1):
        out = jnp.where(block == b, tiles[(b + ahead) % SPLIT], out)
    return out


def by_frame(early, late):
    half = SUB // 2
    pieces = [x[:, z * half : (z + 1) * half] for z in range(N_Z) for x in (early, late)]
    return jnp.concatenate(pieces, axis=1).reshape(SEEN, LANES)


def pack_kernel(in_ref, out_ref):
    total = jnp.zeros((SEEN, LANES), F32)
    for quad in range(QUADS):
        tiles = [in_ref[SPLIT * quad + s].astype(F32) for s in range(SPLIT)]
        late = pltpu.roll(pick(tiles, 2), CAP // 2, axis=2)
        out_ref[quad * SEEN : (quad + 1) * SEEN] = by_frame(pick(tiles, 0), late).astype(BF16)
        total = total + by_frame(pick(tiles, 3), pick(tiles, 1))
    lane = lax.broadcasted_iota(jnp.int32, (SEEN, LANES), 1) % PART
    sums = jnp.sum(jnp.where(lane < 3, total, 0.0), axis=1, keepdims=True)
    usable = jnp.sum(jnp.where(lane == 3, total, 0.0), axis=1, keepdims=True)
    sums = jnp.broadcast_to(sums, (SEEN, LANES)).T[: SUB // 2]
    usable = jnp.broadcast_to(usable, (SEEN, LANES)).T[: SUB // 2]
    hi, mid, lo = three_parts(sums)
    n_hi, n_lo, _ = three_parts(usable)
    row = lax.broadcasted_iota(jnp.int32, (SUB // 2, SEEN), 0)
    tail = jnp.zeros((SUB // 2, SEEN), F32)
    for i, x in enumerate((hi, mid, lo, n_hi, n_lo)):
        tail = jnp.where(row == i, x, tail)
    tail = jnp.concatenate([tail[:, :LANES], tail[:, LANES:]], axis=0)
    out_ref[QUADS * SEEN :] = tail.astype(BF16)


def gram_kernel(me_ref, x0_ref, x1_ref, out_ref, all_ref, own_ref):
    me = me_ref[0]
    t_row = lax.broadcasted_iota(jnp.int32, (LANES, FRAMES), 0)
    t_col = lax.broadcasted_iota(jnp.int32, (LANES, FRAMES), 1)
    stats = jnp.zeros((SUB // 2, FRAMES), F32)
    for d, ref in enumerate((x0_ref, x1_ref)):
        core = me ^ d
        for j in range(N_TROW):
            for z in range(N_Z):
                first = j * ROWS + z * 2 * SUB + core * SUB
                rows = pl.ds(pl.multiple_of(first, SUB), SUB)
                for quad in range(QUADS):
                    at = quad * SEEN + (j * N_Z + z) * SUB
                    here = ref[at : at + SUB]
                    all_ref[rows, quad * LANES : (quad + 1) * LANES] = here
                    if d == 0:
                        own_ref[z, j * SUB : (j + 1) * SUB, quad * LANES : (quad + 1) * LANES] = here
        tail = ref[QUADS * SEEN :]
        for part in range(SEEN // LANES):
            group = t_row // SUB + part * LANES // SUB
            goes_to = group * 2 * SUB + core * SUB + t_row % SUB
            spread = jnp.where(goes_to == t_col, 1.0, 0.0).astype(BF16)
            stats = stats + dot_n(tail, spread)[part * SUB // 2 : (part + 1) * SUB // 2]

    inv = 1.0 / jnp.maximum(stats[0:1] + stats[1:2] + stats[2:3], 1.0)
    inv_col = jnp.broadcast_to(inv, (LANES, FRAMES)).T
    usable = (stats[3:4] + stats[4:5])[:, 0:1]

    lags = jnp.zeros((1, FRAMES), F32)
    flip_row = lax.broadcasted_iota(jnp.int32, (LANES, LANES), 0)
    flip_col = lax.broadcasted_iota(jnp.int32, (LANES, LANES), 1)
    flip = jnp.where(flip_row + flip_col == LANES - 1, 1.0, 0.0).astype(BF16)
    for b in range(FRAMES // LANES):
        start = b * LANES
        width = FRAMES - start
        back = dot_n(flip, all_ref[start : start + LANES]).astype(BF16)
        back_stats = dot_n(stats[:, start : start + LANES].astype(BF16), flip)
        back_sums = back_stats[0:1] + back_stats[1:2] + back_stats[2:3]
        back_inv = jnp.broadcast_to(1.0 / jnp.maximum(back_sums, 1.0), (LANES, LANES)).T[:, 0:1]
        block = dot_t(back, all_ref[start:])
        row = lax.broadcasted_iota(jnp.int32, (LANES, width), 0)
        col = lax.broadcasted_iota(jnp.int32, (LANES, width), 1)
        block = jnp.where(row + col >= LANES - 1, block * (back_inv * inv[:, start:]), 0.0)
        block = pltpu.roll(block, width - LANES + 1, axis=1, stride=1, stride_axis=0)
        part = jnp.sum(block, axis=0, keepdims=True)
        if width < FRAMES:
            part = jnp.concatenate([part, jnp.zeros((1, start), F32)], axis=1)
        lags = lags + part
    remaining = (FRAMES - lax.broadcasted_iota(jnp.int32, (1, FRAMES), 1)).astype(F32)
    lags = lags * usable / remaining
    tail = jnp.concatenate(
        [lags[:, b * LANES : (b + 1) * LANES] for b in range(FRAMES // LANES)]
        + [jnp.zeros((4, LANES), F32)],
        axis=0,
    )

    own_sums = x0_ref[QUADS * SEEN :].astype(F32)
    for z in range(N_Z):
        pieces = []
        for j in range(N_TROW):
            at = (j * N_Z + z) * SUB
            half = at // LANES * (SUB // 2)
            pieces.append(own_sums[half : half + SUB // 2, at % LANES : at % LANES + SUB])
        own = jnp.concatenate(pieces, axis=1)
        own_inv = usable / jnp.maximum(own[0:1] + own[1:2] + own[2:3], 1.0)
        tile = dot_t(all_ref[...], own_ref[z]) * (inv_col * own_inv)
        for i in range(N_TROW):
            out_ref[i, z, :ROWS] = tile[i * ROWS : (i + 1) * ROWS]
            out_ref[i, z, ROWS:] = tail


def join_kernel(in_ref, tile_ref, lag_ref):
    for c in range(OWNED):
        parts = [in_ref[SPLIT * c + part] for part in range(SPLIT)]
        both = (parts[0] + parts[1]) + (parts[2] + parts[3])
        tile_ref[c] = both[:ROWS]
        for b in range(FRAMES // LANES):
            lag_ref[c : c + 1, b * LANES : (b + 1) * LANES] = both[ROWS + b : ROWS + b + 1]


def call(body, out_shape, n_in, scalars=0, scratch=(), flops=0, size=0, source=pltpu.VMEM, limit=32 << 20):
    vmem = pl.BlockSpec(memory_space=pltpu.VMEM)
    given = pl.BlockSpec(memory_space=source)
    smem = pl.BlockSpec(memory_space=pltpu.SMEM)
    many = isinstance(out_shape, tuple)
    return pl.pallas_call(
        body,
        out_shape=out_shape,
        in_specs=[smem] * scalars + [given] * n_in,
        out_specs=(vmem,) * len(out_shape) if many else vmem,
        scratch_shapes=list(scratch),
        compiler_params=pltpu.CompilerParams(vmem_limit_bytes=limit),
        cost_estimate=pl.CostEstimate(flops=flops, bytes_accessed=size, transcendentals=0),
    )


def per_device(counts, labels, pixel_mask, dark_level, flat_field):
    turn = (lax.axis_index("pixel") & (SPLIT - 1)).astype(jnp.int32).reshape(1)
    me = lax.axis_index("core").astype(jnp.int32).reshape(1)
    payload = call(
        slot_kernel,
        jax.ShapeDtypeStruct((CYCLES, SPLIT * SUB // 2, LANES), BF16),
        5,
        scalars=1,
        scratch=[
            pltpu.VMEM((1, PIX), jnp.int32),
            pltpu.VMEM((1, PIX), jnp.int32),
            pltpu.VMEM((1, PIX), F32),
            pltpu.VMEM((1, PIX), F32),
            pltpu.VMEM((SUB, PIX), jnp.int32),
        ]
        + [pltpu.SemaphoreType.DMA] * 5,
        flops=2 * CYCLES * SUB * CAP * PIX,
        size=1 << 20,
        source=pltpu.HBM,
        limit=63 << 20,
    )(
        turn,
        labels.reshape(1, PIX),
        pixel_mask.reshape(1, PIX),
        dark_level.reshape(1, PIX),
        flat_field.reshape(1, PIX),
        counts,
    )
    arrived = lax.all_to_all(
        payload.reshape(SPLIT * CYCLES, SUB // 2, LANES), ("pixel", "trow", "z"), 0, 0, tiled=True
    )
    packed = call(
        pack_kernel,
        jax.ShapeDtypeStruct((QUADS * SEEN + SUB, LANES), BF16),
        1,
        flops=1 << 20,
        size=3 << 18,
    )(arrived.reshape(N_PIXEL, N_TROW, SUB, LANES))
    beside = lax.ppermute(packed, "core", [(0, 1), (1, 0)])
    depth = QUADS * LANES
    sends = call(
        gram_kernel,
        jax.ShapeDtypeStruct((N_TROW, N_Z, ROWS + 8, LANES), F32),
        2,
        scalars=1,
        scratch=[pltpu.VMEM((FRAMES, depth), BF16), pltpu.VMEM((N_Z, COLS, depth), BF16)],
        flops=2 * FRAMES * FRAMES * depth,
        size=3 << 19,
    )(me, packed, beside)
    gets = lax.all_to_all(
        sends.reshape(N_TROW * N_Z, ROWS + 8, LANES), ("trow", "z"), 0, 0, tiled=True
    )
    return call(
        join_kernel,
        (
            jax.ShapeDtypeStruct((OWNED, ROWS, COLS), F32),
            jax.ShapeDtypeStruct((OWNED, FRAMES), F32),
        ),
        1,
        flops=1 << 16,
        size=1 << 19,
    )(gets)


def solution(mesh):
    fine = Mesh(
        mesh.devices.reshape(N_PIXEL, N_TROW, N_Z, 2), ("pixel", "trow", "z", "core")
    )
    frames = ("trow", "z", "core")
    placed = (P(frames, "pixel"), P("pixel", None), P("pixel"), P("pixel"), P("pixel"))
    return jax.shard_map(
        per_device,
        mesh=fine,
        in_specs=placed,
        out_specs=(P("pixel", "trow", ("z", "core")), P("pixel", None)),
        check_vma=False,
    )
```

```python
import jax
import jax.numpy as jnp
from jax import lax
from jax.experimental import pallas as pl
from jax.experimental.pallas import tpu as pltpu
from jax.sharding import PartitionSpec as P

CYCLES = 64
FRAMES = 512
CAP = 128
HALF = CAP // 2
PIX = 4096
N_PIXEL = 16
N_TROW = 8
N_TCOL = 4
SUB = 16
OWNED = CYCLES // N_PIXEL
COLS = N_TROW * SUB
PAIRS = N_PIXEL // 2
ROWS = N_TCOL * SUB
LANES = 128
MESSAGE = 10
CHUNK = 512
RANK = 256
F32 = jnp.float32
BF16 = jnp.bfloat16


def dot_t(a, b):
    return lax.dot_general(a, b, (((1,), (1,)), ((), ())), preferred_element_type=F32)


def dot_n(a, b):
    return jnp.dot(a, b, preferred_element_type=F32)


def three_parts(x):
    hi = x.astype(BF16).astype(F32)
    rest = x - hi
    mid = rest.astype(BF16).astype(F32)
    return hi, mid, rest - mid


def slot_kernel(
    turn_ref,
    labels_hbm,
    mask_hbm,
    dark_hbm,
    flat_hbm,
    counts_hbm,
    out_ref,
    labels_ref,
    mask_ref,
    dark_ref,
    flat_ref,
    counts_ref,
    labels_sem,
    mask_sem,
    dark_sem,
    flat_sem,
    counts_sem,
):
    get_labels = pltpu.make_async_copy(labels_hbm, labels_ref, labels_sem)
    get_mask = pltpu.make_async_copy(mask_hbm, mask_ref, mask_sem)
    get_dark = pltpu.make_async_copy(dark_hbm, dark_ref, dark_sem)
    get_flat = pltpu.make_async_copy(flat_hbm, flat_ref, flat_sem)
    get_counts = pltpu.make_async_copy(counts_hbm, counts_ref, counts_sem)
    for get in (get_labels, get_mask, get_dark, get_flat, get_counts):
        get.start()
    turn = turn_ref[0]
    get_labels.wait()
    get_mask.wait()
    labels = labels_ref[...]
    live = mask_ref[...].astype(F32)

    before = lax.broadcasted_iota(jnp.int32, (RANK, RANK + LANES), 0)
    at = lax.broadcasted_iota(jnp.int32, (RANK, RANK + LANES), 1)
    ahead = jnp.where((before < at) | (at >= RANK), 1.0, 0.0).astype(BF16)
    cycle_of_row = lax.broadcasted_iota(jnp.int32, (CYCLES, RANK), 0)
    offset = jnp.zeros((CYCLES, LANES), F32)
    ranks = []
    for c in range(PIX // RANK):
        span = slice(c * RANK, (c + 1) * RANK)
        member = jnp.where(labels[:, span] == cycle_of_row, 1.0, 0.0)
        counted = dot_n(member.astype(BF16), ahead)
        place = counted[:, :RANK] + jnp.concatenate([offset] * (RANK // LANES), axis=1)
        ranks.append(jnp.sum(member * place, axis=0, keepdims=True))
        offset = offset + counted[:, RANK:]
    rank = jnp.concatenate(ranks, axis=1).astype(jnp.int32)
    slot = ((rank + turn * HALF) & (CAP - 1)) + (labels & 1) * CAP
    slot16 = slot.astype(F32).astype(BF16)
    label16 = labels.astype(F32).astype(BF16)
    pair16 = (labels >> 1).astype(F32).astype(BF16)

    get_dark.wait()
    get_flat.wait()
    get_counts.wait()
    frames = (
        flat_ref[...] * live * (counts_ref[...].astype(F32) - dark_ref[...])
    ).astype(BF16)
    live16 = jnp.broadcast_to(live, (SUB, PIX)).astype(BF16)

    slots = jnp.zeros((CYCLES // 2 * SUB, 2 * CAP), F32)
    sums = jnp.zeros((CYCLES, LANES), F32)
    slot_of_row = lax.broadcasted_iota(jnp.int32, (2 * CAP, CHUNK), 0).astype(F32).astype(BF16)
    row = lax.broadcasted_iota(jnp.int32, (CYCLES, CHUNK), 0)
    even_first = ((row & (CYCLES // 2 - 1)) * 2 + row // (CYCLES // 2)).astype(F32).astype(BF16)
    one = jnp.ones((2 * CAP, CHUNK), BF16)
    none = jnp.zeros((SUB, CHUNK), BF16)
    for c in range(PIX // CHUNK):
        span = slice(c * CHUNK, (c + 1) * CHUNK)
        here = jnp.broadcast_to(pair16[:, span], (SUB, CHUNK))
        chunk = frames[:, span]
        left = jnp.concatenate(
            [jnp.where(here == jnp.array(r, BF16), chunk, none) for r in range(CYCLES // 2)],
            axis=0,
        )
        right = jnp.where(
            jnp.broadcast_to(slot16[:, span], (2 * CAP, CHUNK)) == slot_of_row,
            one,
            jnp.zeros_like(one),
        )
        slots = slots + dot_t(left, right)
        member = jnp.where(
            jnp.broadcast_to(label16[:, span], (CYCLES, CHUNK)) == even_first,
            one[:CYCLES],
            jnp.zeros_like(one[:CYCLES]),
        )
        stack = jnp.concatenate([chunk, chunk, chunk, live16[:, span]] * 2, axis=0)
        sums = sums + dot_t(member, stack)

    hi, mid, lo = three_parts(sums)
    part = lax.broadcasted_iota(jnp.int32, (CYCLES, LANES), 1) // SUB
    extra = jnp.where(part == 0, hi, jnp.where(part == 1, mid, jnp.where(part == 2, lo, sums)))
    shape = (CYCLES // 2, SUB // 2, LANES)
    extras = [
        jnp.broadcast_to(extra[b * shape[0] : (b + 1) * shape[0]][:, None, :], shape)
        for b in range(2)
    ]
    data = (lax.broadcasted_iota(jnp.int32, shape, 2) >= HALF) == (turn == 1)
    row = lax.broadcasted_iota(jnp.int32, shape, 1)
    slots = slots.reshape(CYCLES // 2, SUB, 2 * CAP)
    tiles = []
    for b in range(2):
        early = slots[:, : SUB // 2, b * CAP : (b + 1) * CAP]
        late = slots[:, SUB // 2 :, b * CAP : (b + 1) * CAP]
        tiles.append(jnp.where(data, early, pltpu.roll(late, HALF, axis=2)))
        tiles.append(jnp.where(data, pltpu.roll(early, HALF, axis=2), late))
    second, third, fourth = (pltpu.roll(tiles[m], 2 * m, axis=1) for m in (1, 2, 3))
    groups = [
        tiles[0],
        jnp.where(row < 2, extras[0], second),
        jnp.where(row < 2, second, jnp.where(row < 4, extras[0], third)),
        jnp.where(row < 4, third, jnp.where(row < 6, extras[1], fourth)),
        jnp.where(row < 6, fourth, extras[1]),
    ]
    out_ref[...] = (
        jnp.concatenate(groups, axis=1).reshape(2 * CYCLES * MESSAGE, LANES).astype(BF16)
    )


def pack_kernel(in_ref, out_ref):
    per_shard = N_TROW * MESSAGE
    shape = (N_TROW, SUB // 2, LANES)
    low = lax.broadcasted_iota(jnp.int32, shape, 2) < HALF
    row = lax.broadcasted_iota(jnp.int32, (SUB // 2, LANES), 0)
    lane = lax.broadcasted_iota(jnp.int32, (SUB // 2, LANES), 1)
    total = jnp.zeros((per_shard, LANES), F32)
    for pair in range(PAIRS):
        halves = []
        for shard in (2 * pair, 2 * pair + 1):
            rows = in_ref[shard * per_shard : (shard + 1) * per_shard].astype(F32)
            total = total + rows
            group = [rows[8 * i : 8 * i + 8] for i in range(per_shard // 8)]
            tiles = []
            for first in (0, 5):
                g = group[first : first + 5]
                tiles.append(g[0])
                tiles.append(pltpu.roll(jnp.where(row < 2, g[2], g[1]), 6, axis=0))
                tiles.append(pltpu.roll(jnp.where(row < 4, g[3], g[2]), 4, axis=0))
                tiles.append(pltpu.roll(jnp.where(row < 6, g[4], g[3]), 2, axis=0))
            halves.append(jnp.concatenate(tiles, axis=0).reshape(shape))
        even, odd = halves
        early = jnp.where(low, even, odd)
        late = pltpu.roll(jnp.where(low, odd, even), HALF, axis=2)
        out_ref[pair * COLS : (pair + 1) * COLS] = (
            jnp.concatenate([early, late], axis=1).reshape(COLS, LANES).astype(BF16)
        )
    sums = jnp.zeros((SUB // 2, LANES), F32)
    usable = jnp.zeros((SUB // 2, LANES), F32)
    for j in range(N_TROW):
        at = j * MESSAGE + SUB // 2
        extra = jnp.broadcast_to(total[at : at + 1], (SUB // 2, LANES))
        added = extra + pltpu.roll(extra, LANES - SUB, axis=1)
        added = added + pltpu.roll(extra, LANES - 2 * SUB, axis=1)
        here = lane // SUB == j
        sums = jnp.where(here, pltpu.roll(added, j * SUB, axis=1), sums)
        count = pltpu.roll(extra, (LANES - 3 * SUB + j * SUB) % LANES, axis=1)
        usable = jnp.where(here, count, usable)
    hi, mid, lo = three_parts(sums)
    n_hi, n_lo, _ = three_parts(usable)
    tail = jnp.zeros((SUB // 2, LANES), F32)
    for i, x in enumerate((hi, mid, lo, n_hi, n_lo)):
        tail = jnp.where(row == i, x, tail)
    out_ref[PAIRS * COLS :] = jnp.concatenate([tail, jnp.zeros_like(tail)], axis=0).astype(BF16)


def gram_kernel(me_ref, x0_ref, x1_ref, x2_ref, x3_ref, out_ref, all_ref, own_ref):
    me = me_ref[0]
    depth = PAIRS * LANES
    t_row = lax.broadcasted_iota(jnp.int32, (COLS, FRAMES), 0)
    t_col = lax.broadcasted_iota(jnp.int32, (COLS, FRAMES), 1)
    stats = jnp.zeros((SUB, FRAMES), F32)
    for d, ref in enumerate((x0_ref, x1_ref, x2_ref, x3_ref)):
        k = me ^ d
        for j in range(N_TROW):
            rows = pl.ds(pl.multiple_of(j * ROWS + k * SUB, SUB), SUB)
            for pair in range(PAIRS):
                at = pair * COLS + j * SUB
                all_ref[rows, pair * LANES : (pair + 1) * LANES] = ref[at : at + SUB]
        goes_to = (t_row // SUB) * ROWS + k * SUB + t_row % SUB
        spread = jnp.where(goes_to == t_col, 1.0, 0.0).astype(BF16)
        stats = stats + dot_n(ref[PAIRS * COLS :], spread)
    for pair in range(PAIRS):
        own_ref[:, pair * LANES : (pair + 1) * LANES] = x0_ref[pair * COLS : (pair + 1) * COLS]

    own = x0_ref[PAIRS * COLS :].astype(F32)
    own_inv = 1.0 / jnp.maximum(own[0:1] + own[1:2] + own[2:3], 1.0)
    usable = (own[3:4] + own[4:5])[:, 0:1]
    inv = 1.0 / jnp.maximum(stats[0:1] + stats[1:2] + stats[2:3], 1.0)
    inv_col = jnp.broadcast_to(inv, (LANES, FRAMES)).T

    tile = dot_t(all_ref[...], own_ref[...])
    tile = tile * (inv_col * (own_inv * usable))

    lags = jnp.zeros((1, FRAMES), F32)
    flip_row = lax.broadcasted_iota(jnp.int32, (LANES, LANES), 0)
    flip_col = lax.broadcasted_iota(jnp.int32, (LANES, LANES), 1)
    flip = jnp.where(flip_row + flip_col == LANES - 1, 1.0, 0.0).astype(BF16)
    for b in range(FRAMES // LANES):
        start = b * LANES
        width = FRAMES - start
        back = dot_n(flip, all_ref[start : start + LANES]).astype(BF16)
        back_stats = dot_n(stats[:, start : start + LANES].astype(BF16), flip)
        back_sums = back_stats[0:1] + back_stats[1:2] + back_stats[2:3]
        back_inv = jnp.broadcast_to(1.0 / jnp.maximum(back_sums, 1.0), (LANES, LANES)).T[:, 0:1]
        block = dot_t(back, all_ref[start:])
        row = lax.broadcasted_iota(jnp.int32, (LANES, width), 0)
        col = lax.broadcasted_iota(jnp.int32, (LANES, width), 1)
        block = jnp.where(row + col >= LANES - 1, block * (back_inv * inv[:, start:]), 0.0)
        block = pltpu.roll(block, width - LANES + 1, axis=1, stride=1, stride_axis=0)
        part = jnp.sum(block, axis=0, keepdims=True)
        if width < FRAMES:
            part = jnp.concatenate([part, jnp.zeros((1, start), F32)], axis=1)
        lags = lags + part
    remaining = (FRAMES - lax.broadcasted_iota(jnp.int32, (1, FRAMES), 1)).astype(F32)
    lags = lags * usable / remaining

    for i in range(N_TROW):
        out_ref[i, :ROWS] = tile[i * ROWS : (i + 1) * ROWS]
        for b in range(FRAMES // LANES):
            out_ref[i, ROWS + b : ROWS + b + 1] = lags[:, b * LANES : (b + 1) * LANES]
        out_ref[i, ROWS + 4 :] = jnp.zeros((4, LANES), F32)


def join_kernel(in_ref, tile_ref, lag_ref):
    for c in range(OWNED):
        both = in_ref[2 * c] + in_ref[2 * c + 1]
        tile_ref[c] = both[:ROWS]
        for b in range(FRAMES // LANES):
            lag_ref[c : c + 1, b * LANES : (b + 1) * LANES] = both[ROWS + b : ROWS + b + 1]


def call(body, out_shape, n_in, scalars=0, scratch=(), flops=0, size=0, source=pltpu.VMEM, limit=32 << 20):
    vmem = pl.BlockSpec(memory_space=pltpu.VMEM)
    given = pl.BlockSpec(memory_space=source)
    smem = pl.BlockSpec(memory_space=pltpu.SMEM)
    many = isinstance(out_shape, tuple)
    return pl.pallas_call(
        body,
        out_shape=out_shape,
        in_specs=[smem] * scalars + [given] * n_in,
        out_specs=(vmem,) * len(out_shape) if many else vmem,
        scratch_shapes=list(scratch),
        compiler_params=pltpu.CompilerParams(vmem_limit_bytes=limit),
        cost_estimate=pl.CostEstimate(flops=flops, bytes_accessed=size, transcendentals=0),
    )


def per_device(counts, labels, pixel_mask, dark_level, flat_field):
    turn = (lax.axis_index("pixel") & 1).astype(jnp.int32).reshape(1)
    me = lax.axis_index("tcol").astype(jnp.int32).reshape(1)
    payload = call(
        slot_kernel,
        jax.ShapeDtypeStruct((2 * CYCLES * MESSAGE, LANES), BF16),
        5,
        scalars=1,
        scratch=[
            pltpu.VMEM((1, PIX), jnp.int32),
            pltpu.VMEM((1, PIX), jnp.int32),
            pltpu.VMEM((1, PIX), F32),
            pltpu.VMEM((1, PIX), F32),
            pltpu.VMEM((SUB, PIX), jnp.int32),
        ]
        + [pltpu.SemaphoreType.DMA] * 5,
        flops=2 * CYCLES * SUB * CAP * PIX,
        size=1 << 20,
        source=pltpu.HBM,
        limit=63 << 20,
    )(
        turn,
        labels.reshape(1, PIX),
        pixel_mask.reshape(1, PIX),
        dark_level.reshape(1, PIX),
        flat_field.reshape(1, PIX),
        counts,
    )
    arrived = lax.all_to_all(
        payload.reshape(2 * CYCLES, MESSAGE // 2, 2, LANES), ("pixel", "trow"), 0, 0, tiled=True
    )
    packed = call(
        pack_kernel,
        jax.ShapeDtypeStruct((PAIRS * COLS + SUB, LANES), BF16),
        1,
        flops=1 << 20,
        size=3 << 18,
    )(arrived.reshape(2 * CYCLES * MESSAGE, LANES))
    beside = lax.ppermute(packed, "tcol", [(k, k ^ 1) for k in range(N_TCOL)])
    across = lax.ppermute(packed, "tcol", [(k, k ^ 2) for k in range(N_TCOL)])
    corner = lax.ppermute(across, "tcol", [(k, k ^ 1) for k in range(N_TCOL)])
    depth = PAIRS * LANES
    sends = call(
        gram_kernel,
        jax.ShapeDtypeStruct((N_TROW, ROWS + 8, LANES), F32),
        4,
        scalars=1,
        scratch=[pltpu.VMEM((FRAMES, depth), BF16), pltpu.VMEM((COLS, depth), BF16)],
        flops=2 * FRAMES * FRAMES * depth,
        size=3 << 19,
    )(me, packed, beside, across, corner)
    gets = lax.all_to_all(sends, "trow", 0, 0, tiled=True)
    return call(
        join_kernel,
        (
            jax.ShapeDtypeStruct((OWNED, ROWS, COLS), F32),
            jax.ShapeDtypeStruct((OWNED, FRAMES), F32),
        ),
        1,
        flops=1 << 16,
        size=1 << 19,
    )(gets)


def solution(mesh):
    placed = (P(("trow", "tcol"), "pixel"), P("pixel", None), P("pixel"), P("pixel"), P("pixel"))
    return jax.shard_map(
        per_device,
        mesh=mesh,
        in_specs=placed,
        out_specs=(P("pixel", "trow", "tcol"), P("pixel", None)),
        check_vma=False,
    )
```

```python
import jax
import jax.numpy as jnp
from jax import lax
from jax.experimental import pallas as pl
from jax.experimental.pallas import tpu as pltpu
from jax.sharding import Mesh
from jax.sharding import PartitionSpec as P

CYCLES = 64
FRAMES = 512
CAP = 128
HALF = CAP // 2
PIX = 4096
N_PIXEL = 16
N_TROW = 8
N_TCOL = 4
N_Z = 2
SUB = 16
OWNED = CYCLES // N_PIXEL
COLS = N_TROW * SUB
PAIRS = N_PIXEL // 2
SEEN = N_TROW * N_Z * SUB
ROWS = N_TCOL * SUB
LANES = 128
MESSAGE = 10
CHUNK = 512
RANK = 256
F32 = jnp.float32
BF16 = jnp.bfloat16


def dot_t(a, b):
    return lax.dot_general(a, b, (((1,), (1,)), ((), ())), preferred_element_type=F32)


def dot_n(a, b):
    return jnp.dot(a, b, preferred_element_type=F32)


def three_parts(x):
    hi = x.astype(BF16).astype(F32)
    rest = x - hi
    mid = rest.astype(BF16).astype(F32)
    return hi, mid, rest - mid


def slot_kernel(
    turn_ref,
    labels_hbm,
    mask_hbm,
    dark_hbm,
    flat_hbm,
    counts_hbm,
    out_ref,
    labels_ref,
    mask_ref,
    dark_ref,
    flat_ref,
    counts_ref,
    labels_sem,
    mask_sem,
    dark_sem,
    flat_sem,
    counts_sem,
):
    get_labels = pltpu.make_async_copy(labels_hbm, labels_ref, labels_sem)
    get_mask = pltpu.make_async_copy(mask_hbm, mask_ref, mask_sem)
    get_dark = pltpu.make_async_copy(dark_hbm, dark_ref, dark_sem)
    get_flat = pltpu.make_async_copy(flat_hbm, flat_ref, flat_sem)
    get_counts = pltpu.make_async_copy(counts_hbm, counts_ref, counts_sem)
    for get in (get_labels, get_mask, get_dark, get_flat, get_counts):
        get.start()
    turn = turn_ref[0]
    get_labels.wait()
    get_mask.wait()
    labels = labels_ref[...]
    live = mask_ref[...].astype(F32)

    before = lax.broadcasted_iota(jnp.int32, (RANK, RANK + LANES), 0)
    at = lax.broadcasted_iota(jnp.int32, (RANK, RANK + LANES), 1)
    ahead = jnp.where((before < at) | (at >= RANK), 1.0, 0.0).astype(BF16)
    cycle_of_row = lax.broadcasted_iota(jnp.int32, (CYCLES, RANK), 0)
    offset = jnp.zeros((CYCLES, LANES), F32)
    ranks = []
    for c in range(PIX // RANK):
        span = slice(c * RANK, (c + 1) * RANK)
        member = jnp.where(labels[:, span] == cycle_of_row, 1.0, 0.0)
        counted = dot_n(member.astype(BF16), ahead)
        place = counted[:, :RANK] + jnp.concatenate([offset] * (RANK // LANES), axis=1)
        ranks.append(jnp.sum(member * place, axis=0, keepdims=True))
        offset = offset + counted[:, RANK:]
    rank = jnp.concatenate(ranks, axis=1).astype(jnp.int32)
    slot = ((rank + turn * HALF) & (CAP - 1)) + (labels & 1) * CAP
    slot16 = slot.astype(F32).astype(BF16)
    label16 = labels.astype(F32).astype(BF16)
    pair16 = (labels >> 1).astype(F32).astype(BF16)

    get_dark.wait()
    get_flat.wait()
    get_counts.wait()
    frames = (
        flat_ref[...] * live * (counts_ref[...].astype(F32) - dark_ref[...])
    ).astype(BF16)
    live16 = jnp.broadcast_to(live, (SUB, PIX)).astype(BF16)

    slots = jnp.zeros((CYCLES // 2 * SUB, 2 * CAP), F32)
    sums = jnp.zeros((CYCLES, LANES), F32)
    slot_of_row = lax.broadcasted_iota(jnp.int32, (2 * CAP, CHUNK), 0).astype(F32).astype(BF16)
    row = lax.broadcasted_iota(jnp.int32, (CYCLES, CHUNK), 0)
    even_first = ((row & (CYCLES // 2 - 1)) * 2 + row // (CYCLES // 2)).astype(F32).astype(BF16)
    one = jnp.ones((2 * CAP, CHUNK), BF16)
    none = jnp.zeros((SUB, CHUNK), BF16)
    for c in range(PIX // CHUNK):
        span = slice(c * CHUNK, (c + 1) * CHUNK)
        here = jnp.broadcast_to(pair16[:, span], (SUB, CHUNK))
        chunk = frames[:, span]
        left = jnp.concatenate(
            [jnp.where(here == jnp.array(r, BF16), chunk, none) for r in range(CYCLES // 2)],
            axis=0,
        )
        right = jnp.where(
            jnp.broadcast_to(slot16[:, span], (2 * CAP, CHUNK)) == slot_of_row,
            one,
            jnp.zeros_like(one),
        )
        slots = slots + dot_t(left, right)
        member = jnp.where(
            jnp.broadcast_to(label16[:, span], (CYCLES, CHUNK)) == even_first,
            one[:CYCLES],
            jnp.zeros_like(one[:CYCLES]),
        )
        stack = jnp.concatenate([chunk, chunk, chunk, live16[:, span]] * 2, axis=0)
        sums = sums + dot_t(member, stack)

    hi, mid, lo = three_parts(sums)
    part = lax.broadcasted_iota(jnp.int32, (CYCLES, LANES), 1) // SUB
    extra = jnp.where(part == 0, hi, jnp.where(part == 1, mid, jnp.where(part == 2, lo, sums)))
    shape = (CYCLES // 2, SUB // 2, LANES)
    extras = [
        jnp.broadcast_to(extra[b * shape[0] : (b + 1) * shape[0]][:, None, :], shape)
        for b in range(2)
    ]
    data = (lax.broadcasted_iota(jnp.int32, shape, 2) >= HALF) == (turn == 1)
    row = lax.broadcasted_iota(jnp.int32, shape, 1)
    slots = slots.reshape(CYCLES // 2, SUB, 2 * CAP)
    tiles = []
    for b in range(2):
        early = slots[:, : SUB // 2, b * CAP : (b + 1) * CAP]
        late = slots[:, SUB // 2 :, b * CAP : (b + 1) * CAP]
        tiles.append(jnp.where(data, early, pltpu.roll(late, HALF, axis=2)))
        tiles.append(jnp.where(data, pltpu.roll(early, HALF, axis=2), late))
    groups = []
    for b in range(2):
        extra, (lower, upper) = extras[b], tiles[2 * b : 2 * b + 2]
        second, third, fourth = (
            pltpu.roll(x, 2 * m, axis=1) for m, x in ((1, lower), (2, upper), (3, upper))
        )
        groups += [
            lower,
            jnp.where(row < 2, extra, second),
            jnp.where(row < 2, second, jnp.where(row < 4, extra, third)),
            jnp.where(row < 4, third, jnp.where(row < 6, extra, fourth)),
            jnp.where(row < 6, fourth, extra),
        ]
    out_ref[...] = (
        jnp.concatenate(groups, axis=1).reshape(4 * CYCLES * MESSAGE, LANES).astype(BF16)
    )


def pack_kernel(in_ref, out_ref):
    per_shard = N_TROW * N_Z * MESSAGE
    shape = (N_TROW * N_Z, SUB // 2, LANES)
    low = lax.broadcasted_iota(jnp.int32, shape, 2) < HALF
    row = lax.broadcasted_iota(jnp.int32, (SUB // 2, LANES), 0)
    lane = lax.broadcasted_iota(jnp.int32, (SUB // 2, LANES), 1)
    total = jnp.zeros((per_shard, LANES), F32)
    for pair in range(PAIRS):
        halves = []
        for shard in (2 * pair, 2 * pair + 1):
            rows = in_ref[shard * per_shard : (shard + 1) * per_shard].astype(F32)
            total = total + rows
            group = [rows[8 * i : 8 * i + 8] for i in range(per_shard // 8)]
            tiles = []
            for first in range(0, len(group), 5):
                g = group[first : first + 5]
                tiles.append(g[0])
                tiles.append(pltpu.roll(jnp.where(row < 2, g[2], g[1]), 6, axis=0))
                tiles.append(pltpu.roll(jnp.where(row < 4, g[3], g[2]), 4, axis=0))
                tiles.append(pltpu.roll(jnp.where(row < 6, g[4], g[3]), 2, axis=0))
            halves.append(jnp.concatenate(tiles, axis=0).reshape(shape))
        even, odd = halves
        early = jnp.where(low, even, odd)
        late = pltpu.roll(jnp.where(low, odd, even), HALF, axis=2)
        out_ref[pair * SEEN : (pair + 1) * SEEN] = (
            jnp.concatenate([early, late], axis=1).reshape(SEEN, LANES).astype(BF16)
        )
    tails = []
    for half in range(SEEN // LANES):
        sums = jnp.zeros((SUB // 2, LANES), F32)
        usable = jnp.zeros((SUB // 2, LANES), F32)
        for i in range(LANES // SUB):
            at = (half * LANES // SUB + i) * MESSAGE + SUB // 2
            extra = jnp.broadcast_to(total[at : at + 1], (SUB // 2, LANES))
            added = extra + pltpu.roll(extra, LANES - SUB, axis=1)
            added = added + pltpu.roll(extra, LANES - 2 * SUB, axis=1)
            here = lane // SUB == i
            sums = jnp.where(here, pltpu.roll(added, i * SUB, axis=1), sums)
            count = pltpu.roll(extra, (LANES - 3 * SUB + i * SUB) % LANES, axis=1)
            usable = jnp.where(here, count, usable)
        hi, mid, lo = three_parts(sums)
        n_hi, n_lo, _ = three_parts(usable)
        tail = jnp.zeros((SUB // 2, LANES), F32)
        for i, x in enumerate((hi, mid, lo, n_hi, n_lo)):
            tail = jnp.where(row == i, x, tail)
        tails.append(tail)
    out_ref[PAIRS * SEEN :] = jnp.concatenate(tails, axis=0).astype(BF16)


def gram_kernel(core_ref, z_ref, x0_ref, x1_ref, out_ref, all_ref, own_ref):
    me = core_ref[0]
    my_z = z_ref[0]
    t_row = lax.broadcasted_iota(jnp.int32, (LANES, FRAMES), 0)
    t_col = lax.broadcasted_iota(jnp.int32, (LANES, FRAMES), 1)
    stats = jnp.zeros((SUB // 2, FRAMES), F32)
    for d, ref in enumerate((x0_ref, x1_ref)):
        core = me ^ d
        for j in range(N_TROW):
            for z in range(N_Z):
                first = j * ROWS + z * 2 * SUB + core * SUB
                rows = pl.ds(pl.multiple_of(first, SUB), SUB)
                for pair in range(PAIRS):
                    at = pair * SEEN + (j * N_Z + z) * SUB
                    here = ref[at : at + SUB]
                    all_ref[rows, pair * LANES : (pair + 1) * LANES] = here
        tail = ref[PAIRS * SEEN :]
        for part in range(SEEN // LANES):
            group = t_row // SUB + part * LANES // SUB
            goes_to = group * 2 * SUB + core * SUB + t_row % SUB
            spread = jnp.where(goes_to == t_col, 1.0, 0.0).astype(BF16)
            stats = stats + dot_n(tail, spread)[part * SUB // 2 : (part + 1) * SUB // 2]

    inv = 1.0 / jnp.maximum(stats[0:1] + stats[1:2] + stats[2:3], 1.0)
    inv_col = jnp.broadcast_to(inv, (LANES, FRAMES)).T
    usable = (stats[3:4] + stats[4:5])[:, 0:1]

    lags = jnp.zeros((1, FRAMES), F32)
    flip_row = lax.broadcasted_iota(jnp.int32, (LANES, LANES), 0)
    flip_col = lax.broadcasted_iota(jnp.int32, (LANES, LANES), 1)
    flip = jnp.where(flip_row + flip_col == LANES - 1, 1.0, 0.0).astype(BF16)
    for b in range(FRAMES // LANES):
        start = b * LANES
        width = FRAMES - start
        back = dot_n(flip, all_ref[start : start + LANES]).astype(BF16)
        back_stats = dot_n(stats[:, start : start + LANES].astype(BF16), flip)
        back_sums = back_stats[0:1] + back_stats[1:2] + back_stats[2:3]
        back_inv = jnp.broadcast_to(1.0 / jnp.maximum(back_sums, 1.0), (LANES, LANES)).T[:, 0:1]
        block = dot_t(back, all_ref[start:])
        row = lax.broadcasted_iota(jnp.int32, (LANES, width), 0)
        col = lax.broadcasted_iota(jnp.int32, (LANES, width), 1)
        block = jnp.where(row + col >= LANES - 1, block * (back_inv * inv[:, start:]), 0.0)
        block = pltpu.roll(block, width - LANES + 1, axis=1, stride=1, stride_axis=0)
        part = jnp.sum(block, axis=0, keepdims=True)
        if width < FRAMES:
            part = jnp.concatenate([part, jnp.zeros((1, start), F32)], axis=1)
        lags = lags + part
    remaining = (FRAMES - lax.broadcasted_iota(jnp.int32, (1, FRAMES), 1)).astype(F32)
    lags = lags * usable / remaining
    tail = jnp.concatenate(
        [lags[:, b * LANES : (b + 1) * LANES] for b in range(FRAMES // LANES)]
        + [jnp.zeros((4, LANES), F32)],
        axis=0,
    )

    own_sums = x0_ref[PAIRS * SEEN :].astype(F32)
    own = jnp.zeros((SUB // 2, LANES), F32)
    for z in range(N_Z):
        pieces = []
        for j in range(N_TROW):
            at = (j * N_Z + z) * SUB
            half = at // LANES * (SUB // 2)
            pieces.append(own_sums[half : half + SUB // 2, at % LANES : at % LANES + SUB])
        own = jnp.where(my_z == z, jnp.concatenate(pieces, axis=1), own)
    own_inv = usable / jnp.maximum(own[0:1] + own[1:2] + own[2:3], 1.0)
    for j in range(N_TROW):
        for pair in range(PAIRS):
            at = pl.ds(pl.multiple_of(pair * SEEN + j * N_Z * SUB + my_z * SUB, SUB), SUB)
            own_ref[j * SUB : (j + 1) * SUB, pair * LANES : (pair + 1) * LANES] = x0_ref[at]
    tile = dot_t(all_ref[...], own_ref[...]) * (inv_col * own_inv)
    for i in range(N_TROW):
        out_ref[i, :ROWS] = tile[i * ROWS : (i + 1) * ROWS]
        out_ref[i, ROWS:] = tail


def join_kernel(in_ref, tile_ref, lag_ref):
    for c in range(OWNED):
        both = in_ref[2 * c] + in_ref[2 * c + 1]
        tile_ref[c] = both[:ROWS]
        for b in range(FRAMES // LANES):
            lag_ref[c : c + 1, b * LANES : (b + 1) * LANES] = both[ROWS + b : ROWS + b + 1]


def call(body, out_shape, n_in, scalars=0, scratch=(), flops=0, size=0, source=pltpu.VMEM, limit=32 << 20):
    vmem = pl.BlockSpec(memory_space=pltpu.VMEM)
    given = pl.BlockSpec(memory_space=source)
    smem = pl.BlockSpec(memory_space=pltpu.SMEM)
    many = isinstance(out_shape, tuple)
    return pl.pallas_call(
        body,
        out_shape=out_shape,
        in_specs=[smem] * scalars + [given] * n_in,
        out_specs=(vmem,) * len(out_shape) if many else vmem,
        scratch_shapes=list(scratch),
        compiler_params=pltpu.CompilerParams(vmem_limit_bytes=limit),
        cost_estimate=pl.CostEstimate(flops=flops, bytes_accessed=size, transcendentals=0),
    )


def per_device(counts, labels, pixel_mask, dark_level, flat_field):
    turn = (lax.axis_index("pixel") & 1).astype(jnp.int32).reshape(1)
    core = lax.axis_index("core").astype(jnp.int32).reshape(1)
    z = lax.axis_index("z").astype(jnp.int32).reshape(1)
    payload = call(
        slot_kernel,
        jax.ShapeDtypeStruct((4 * CYCLES * MESSAGE, LANES), BF16),
        5,
        scalars=1,
        scratch=[
            pltpu.VMEM((1, PIX), jnp.int32),
            pltpu.VMEM((1, PIX), jnp.int32),
            pltpu.VMEM((1, PIX), F32),
            pltpu.VMEM((1, PIX), F32),
            pltpu.VMEM((SUB, PIX), jnp.int32),
        ]
        + [pltpu.SemaphoreType.DMA] * 5,
        flops=2 * CYCLES * SUB * CAP * PIX,
        size=1 << 20,
        source=pltpu.HBM,
        limit=63 << 20,
    )(
        turn,
        labels.reshape(1, PIX),
        pixel_mask.reshape(1, PIX),
        dark_level.reshape(1, PIX),
        flat_field.reshape(1, PIX),
        counts,
    )
    arrived = lax.all_to_all(
        payload.reshape(4 * CYCLES, MESSAGE // 2, 2, LANES),
        ("pixel", "trow", "z"),
        0,
        0,
        tiled=True,
    )
    packed = call(
        pack_kernel,
        jax.ShapeDtypeStruct((PAIRS * SEEN + SUB, LANES), BF16),
        1,
        flops=1 << 20,
        size=3 << 19,
    )(arrived.reshape(4 * CYCLES * MESSAGE, LANES))
    beside = lax.ppermute(packed, "core", [(0, 1), (1, 0)])
    depth = PAIRS * LANES
    sends = call(
        gram_kernel,
        jax.ShapeDtypeStruct((N_TROW, ROWS + 8, LANES), F32),
        2,
        scalars=2,
        scratch=[pltpu.VMEM((FRAMES, depth), BF16), pltpu.VMEM((COLS, depth), BF16)],
        flops=2 * FRAMES * FRAMES * depth,
        size=3 << 19,
    )(core, z, packed, beside)
    gets = lax.all_to_all(sends, "trow", 0, 0, tiled=True)
    return call(
        join_kernel,
        (
            jax.ShapeDtypeStruct((OWNED, ROWS, COLS), F32),
            jax.ShapeDtypeStruct((OWNED, FRAMES), F32),
        ),
        1,
        flops=1 << 16,
        size=1 << 19,
    )(gets)


def solution(mesh):
    fine = Mesh(
        mesh.devices.reshape(N_PIXEL, N_TROW, N_Z, 2), ("pixel", "trow", "z", "core")
    )
    frames = ("trow", "z", "core")
    placed = (P(frames, "pixel"), P("pixel", None), P("pixel"), P("pixel"), P("pixel"))
    return jax.shard_map(
        per_device,
        mesh=fine,
        in_specs=placed,
        out_specs=(P("pixel", "trow", ("z", "core")), P("pixel", None)),
        check_vma=False,
    )
```

```python
import jax
import jax.numpy as jnp
from jax import lax
from jax.experimental import pallas as pl
from jax.experimental.pallas import tpu as pltpu
from jax.sharding import PartitionSpec as P

CYCLES = 64
FRAMES = 512
CAP = 128
HALF = CAP // 2
PIX = 4096
N_PIXEL = 16
N_TROW = 8
N_TCOL = 4
SUB = 16
OWNED = CYCLES // N_PIXEL
COLS = N_TROW * SUB
PAIRS = N_PIXEL // 2
ROWS = N_TCOL * SUB
LANES = 128
MESSAGE = 10
FILLED = CYCLES // 2 * SUB
CHUNK = 512
RANK = 256
F32 = jnp.float32
BF16 = jnp.bfloat16


def dot_t(a, b):
    return lax.dot_general(a, b, (((1,), (1,)), ((), ())), preferred_element_type=F32)


def dot_n(a, b):
    return jnp.dot(a, b, preferred_element_type=F32)


def three_parts(x):
    hi = x.astype(BF16).astype(F32)
    rest = x - hi
    mid = rest.astype(BF16).astype(F32)
    return hi, mid, rest - mid


def slot_kernel(
    turn_ref,
    labels_hbm,
    mask_hbm,
    dark_hbm,
    flat_hbm,
    counts_hbm,
    out_ref,
    labels_ref,
    mask_ref,
    dark_ref,
    flat_ref,
    counts_ref,
    labels_sem,
    mask_sem,
    dark_sem,
    flat_sem,
    counts_sem,
):
    get_labels = pltpu.make_async_copy(labels_hbm, labels_ref, labels_sem)
    get_mask = pltpu.make_async_copy(mask_hbm, mask_ref, mask_sem)
    get_dark = pltpu.make_async_copy(dark_hbm, dark_ref, dark_sem)
    get_flat = pltpu.make_async_copy(flat_hbm, flat_ref, flat_sem)
    get_counts = pltpu.make_async_copy(counts_hbm, counts_ref, counts_sem)
    for get in (get_labels, get_mask, get_dark, get_flat, get_counts):
        get.start()
    turn = turn_ref[0]
    get_labels.wait()
    get_mask.wait()
    labels = labels_ref[...]
    live = mask_ref[...].astype(F32)

    before = lax.broadcasted_iota(jnp.int32, (RANK, RANK + LANES), 0)
    at = lax.broadcasted_iota(jnp.int32, (RANK, RANK + LANES), 1)
    ahead = jnp.where((before < at) | (at >= RANK), 1.0, 0.0).astype(BF16)
    cycle_of_row = lax.broadcasted_iota(jnp.int32, (CYCLES, RANK), 0)
    offset = jnp.zeros((CYCLES, LANES), F32)
    ranks = []
    for c in range(PIX // RANK):
        span = slice(c * RANK, (c + 1) * RANK)
        member = jnp.where(labels[:, span] == cycle_of_row, 1.0, 0.0)
        counted = dot_n(member.astype(BF16), ahead)
        place = counted[:, :RANK] + jnp.concatenate([offset] * (RANK // LANES), axis=1)
        ranks.append(jnp.sum(member * place, axis=0, keepdims=True))
        offset = offset + counted[:, RANK:]
    rank = jnp.concatenate(ranks, axis=1).astype(jnp.int32)
    slot = ((rank + turn * HALF) & (CAP - 1)) + (labels & 1) * CAP
    slot16 = slot.astype(F32).astype(BF16)
    pair16 = (labels >> 1).astype(F32).astype(BF16)

    get_dark.wait()
    get_flat.wait()
    get_counts.wait()
    frames = (
        flat_ref[...] * live * (counts_ref[...].astype(F32) - dark_ref[...])
    ).astype(BF16)
    live16 = live.astype(BF16)

    slots = jnp.zeros((FILLED + CYCLES // 2, 2 * CAP), F32)
    slot_of_row = lax.broadcasted_iota(jnp.int32, (2 * CAP, CHUNK), 0).astype(F32).astype(BF16)
    pairs = lax.broadcasted_iota(jnp.int32, (CYCLES // 2, CHUNK), 0).astype(F32).astype(BF16)
    one = jnp.ones((2 * CAP, CHUNK), BF16)
    none = jnp.zeros((SUB, CHUNK), BF16)
    for c in range(PIX // CHUNK):
        span = slice(c * CHUNK, (c + 1) * CHUNK)
        here = jnp.broadcast_to(pair16[:, span], (SUB, CHUNK))
        chunk = frames[:, span]
        usable = jnp.where(
            jnp.broadcast_to(pair16[:, span], (CYCLES // 2, CHUNK)) == pairs,
            jnp.broadcast_to(live16[:, span], (CYCLES // 2, CHUNK)),
            jnp.zeros((CYCLES // 2, CHUNK), BF16),
        )
        left = jnp.concatenate(
            [jnp.where(here == jnp.array(r, BF16), chunk, none) for r in range(CYCLES // 2)]
            + [usable],
            axis=0,
        )
        right = jnp.where(
            jnp.broadcast_to(slot16[:, span], (2 * CAP, CHUNK)) == slot_of_row,
            one,
            jnp.zeros_like(one),
        )
        slots = slots + dot_t(left, right)

    in_row = lax.broadcasted_iota(jnp.int32, (2 * CAP, 2 * CAP), 0) // CAP
    in_col = lax.broadcasted_iota(jnp.int32, (2 * CAP, 2 * CAP), 1) // CAP
    same = jnp.where(in_row == in_col, 1.0, 0.0).astype(BF16)
    sums = dot_n(slots.astype(BF16), same)
    counted = sums[FILLED:]
    sums = sums[:FILLED].reshape(CYCLES // 2, SUB, 2 * CAP)
    lane = lax.broadcasted_iota(jnp.int32, sums.shape, 2) % SUB
    sums = jnp.where(lane == lax.broadcasted_iota(jnp.int32, sums.shape, 1), sums, 0.0)
    hi, mid, lo = three_parts(jnp.sum(sums, axis=1))
    part = lax.broadcasted_iota(jnp.int32, (CYCLES // 2, 2 * CAP), 1) % CAP // SUB
    extra = jnp.where(part == 0, hi, jnp.where(part == 1, mid, jnp.where(part == 2, lo, counted)))
    shape = (CYCLES // 2, SUB // 2, LANES)
    extras = [
        jnp.broadcast_to(extra[:, b * LANES : (b + 1) * LANES][:, None, :], shape)
        for b in range(2)
    ]
    data = (lax.broadcasted_iota(jnp.int32, shape, 2) >= HALF) == (turn == 1)
    row = lax.broadcasted_iota(jnp.int32, shape, 1)
    slots = slots[:FILLED].reshape(CYCLES // 2, SUB, 2 * CAP)
    tiles = []
    for b in range(2):
        early = slots[:, : SUB // 2, b * CAP : (b + 1) * CAP]
        late = slots[:, SUB // 2 :, b * CAP : (b + 1) * CAP]
        tiles.append(jnp.where(data, early, pltpu.roll(late, HALF, axis=2)))
        tiles.append(jnp.where(data, pltpu.roll(early, HALF, axis=2), late))
    second, third, fourth = (pltpu.roll(tiles[m], 2 * m, axis=1) for m in (1, 2, 3))
    groups = [
        tiles[0],
        jnp.where(row < 2, extras[0], second),
        jnp.where(row < 2, second, jnp.where(row < 4, extras[0], third)),
        jnp.where(row < 4, third, jnp.where(row < 6, extras[1], fourth)),
        jnp.where(row < 6, fourth, extras[1]),
    ]
    out_ref[...] = (
        jnp.concatenate(groups, axis=1).reshape(2 * CYCLES * MESSAGE, LANES).astype(BF16)
    )


def pack_kernel(in_ref, out_ref):
    per_shard = N_TROW * MESSAGE
    shape = (N_TROW, SUB // 2, LANES)
    low = lax.broadcasted_iota(jnp.int32, shape, 2) < HALF
    row = lax.broadcasted_iota(jnp.int32, (SUB // 2, LANES), 0)
    lane = lax.broadcasted_iota(jnp.int32, (SUB // 2, LANES), 1)
    total = jnp.zeros((per_shard, LANES), F32)
    for pair in range(PAIRS):
        halves = []
        for shard in (2 * pair, 2 * pair + 1):
            rows = in_ref[shard * per_shard : (shard + 1) * per_shard].astype(F32)
            total = total + rows
            group = [rows[8 * i : 8 * i + 8] for i in range(per_shard // 8)]
            tiles = []
            for first in (0, 5):
                g = group[first : first + 5]
                tiles.append(g[0])
                tiles.append(pltpu.roll(jnp.where(row < 2, g[2], g[1]), 6, axis=0))
                tiles.append(pltpu.roll(jnp.where(row < 4, g[3], g[2]), 4, axis=0))
                tiles.append(pltpu.roll(jnp.where(row < 6, g[4], g[3]), 2, axis=0))
            halves.append(jnp.concatenate(tiles, axis=0).reshape(shape))
        even, odd = halves
        early = jnp.where(low, even, odd)
        late = pltpu.roll(jnp.where(low, odd, even), HALF, axis=2)
        out_ref[pair * COLS : (pair + 1) * COLS] = (
            jnp.concatenate([early, late], axis=1).reshape(COLS, LANES).astype(BF16)
        )
    sums = jnp.zeros((SUB // 2, LANES), F32)
    usable = jnp.zeros((SUB // 2, LANES), F32)
    for j in range(N_TROW):
        at = j * MESSAGE + SUB // 2
        extra = jnp.broadcast_to(total[at : at + 1], (SUB // 2, LANES))
        added = extra + pltpu.roll(extra, LANES - SUB, axis=1)
        added = added + pltpu.roll(extra, LANES - 2 * SUB, axis=1)
        here = lane // SUB == j
        sums = jnp.where(here, pltpu.roll(added, j * SUB, axis=1), sums)
        count = pltpu.roll(extra, (LANES - 3 * SUB + j * SUB) % LANES, axis=1)
        usable = jnp.where(here, count, usable)
    hi, mid, lo = three_parts(sums)
    n_hi, n_lo, _ = three_parts(usable)
    tail = jnp.zeros((SUB // 2, LANES), F32)
    for i, x in enumerate((hi, mid, lo, n_hi, n_lo)):
        tail = jnp.where(row == i, x, tail)
    out_ref[PAIRS * COLS :] = jnp.concatenate([tail, jnp.zeros_like(tail)], axis=0).astype(BF16)


def gram_kernel(me_ref, x0_ref, x1_ref, x2_ref, x3_ref, out_ref, all_ref, own_ref):
    me = me_ref[0]
    depth = PAIRS * LANES
    t_row = lax.broadcasted_iota(jnp.int32, (COLS, FRAMES), 0)
    t_col = lax.broadcasted_iota(jnp.int32, (COLS, FRAMES), 1)
    stats = jnp.zeros((SUB, FRAMES), F32)
    for d, ref in enumerate((x0_ref, x1_ref, x2_ref, x3_ref)):
        k = me ^ d
        for j in range(N_TROW):
            rows = pl.ds(pl.multiple_of(j * ROWS + k * SUB, SUB), SUB)
            for pair in range(PAIRS):
                at = pair * COLS + j * SUB
                all_ref[rows, pair * LANES : (pair + 1) * LANES] = ref[at : at + SUB]
        goes_to = (t_row // SUB) * ROWS + k * SUB + t_row % SUB
        spread = jnp.where(goes_to == t_col, 1.0, 0.0).astype(BF16)
        stats = stats + dot_n(ref[PAIRS * COLS :], spread)
    for pair in range(PAIRS):
        own_ref[:, pair * LANES : (pair + 1) * LANES] = x0_ref[pair * COLS : (pair + 1) * COLS]

    own = x0_ref[PAIRS * COLS :].astype(F32)
    own_inv = 1.0 / jnp.maximum(own[0:1] + own[1:2] + own[2:3], 1.0)
    usable = (own[3:4] + own[4:5])[:, 0:1]
    inv = 1.0 / jnp.maximum(stats[0:1] + stats[1:2] + stats[2:3], 1.0)
    inv_col = jnp.broadcast_to(inv, (LANES, FRAMES)).T

    tile = dot_t(all_ref[...], own_ref[...])
    tile = tile * (inv_col * (own_inv * usable))

    group = SUB // 2
    along = jnp.zeros((group, FRAMES), F32)
    row = lax.broadcasted_iota(jnp.int32, (LANES, LANES), 0)
    col = lax.broadcasted_iota(jnp.int32, (LANES, LANES), 1)
    for b in range(FRAMES // LANES):
        start = b * LANES
        width = FRAMES - start
        block = dot_t(all_ref[start : start + LANES], all_ref[start:])
        block = block * (inv_col[start : start + LANES, 0:1] * inv[:, start:])
        corner = jnp.where(col >= row, block[:, :LANES], 0.0)
        block = corner if width == LANES else jnp.concatenate([corner, block[:, LANES:]], axis=1)
        part = block[:group]
        for first in range(group, LANES, group):
            part = part + pltpu.roll(block[first : first + group], width - first, axis=1)
        if width < FRAMES:
            part = jnp.concatenate([part, jnp.zeros((group, start), F32)], axis=1)
        along = along + part
    place = lax.broadcasted_iota(jnp.int32, (group, FRAMES), 0)
    for step in (1, 2, 4):
        along = jnp.where((place & step) > 0, pltpu.roll(along, FRAMES - step, axis=1), along)
    lags = jnp.sum(along, axis=0, keepdims=True)
    remaining = (FRAMES - lax.broadcasted_iota(jnp.int32, (1, FRAMES), 1)).astype(F32)
    lags = lags * usable / remaining

    for i in range(N_TROW):
        out_ref[i, :ROWS] = tile[i * ROWS : (i + 1) * ROWS]
        for b in range(FRAMES // LANES):
            out_ref[i, ROWS + b : ROWS + b + 1] = lags[:, b * LANES : (b + 1) * LANES]
        out_ref[i, ROWS + 4 :] = jnp.zeros((4, LANES), F32)


def join_kernel(in_ref, tile_ref, lag_ref):
    for c in range(OWNED):
        both = in_ref[2 * c] + in_ref[2 * c + 1]
        tile_ref[c] = both[:ROWS]
        for b in range(FRAMES // LANES):
            lag_ref[c : c + 1, b * LANES : (b + 1) * LANES] = both[ROWS + b : ROWS + b + 1]


def call(body, out_shape, n_in, scalars=0, scratch=(), flops=0, size=0, source=pltpu.VMEM):
    vmem = pl.BlockSpec(memory_space=pltpu.VMEM)
    given = pl.BlockSpec(memory_space=source)
    smem = pl.BlockSpec(memory_space=pltpu.SMEM)
    many = isinstance(out_shape, tuple)
    return pl.pallas_call(
        body,
        out_shape=out_shape,
        in_specs=[smem] * scalars + [given] * n_in,
        out_specs=(vmem,) * len(out_shape) if many else vmem,
        scratch_shapes=list(scratch),
        compiler_params=pltpu.CompilerParams(vmem_limit_bytes=32 << 20),
        cost_estimate=pl.CostEstimate(flops=flops, bytes_accessed=size, transcendentals=0),
    )


def per_device(counts, labels, pixel_mask, dark_level, flat_field):
    turn = (lax.axis_index("pixel") & 1).astype(jnp.int32).reshape(1)
    me = lax.axis_index("tcol").astype(jnp.int32).reshape(1)
    payload = call(
        slot_kernel,
        jax.ShapeDtypeStruct((2 * CYCLES * MESSAGE, LANES), BF16),
        5,
        scalars=1,
        scratch=[
            pltpu.VMEM((1, PIX), jnp.int32),
            pltpu.VMEM((1, PIX), jnp.int32),
            pltpu.VMEM((1, PIX), F32),
            pltpu.VMEM((1, PIX), F32),
            pltpu.VMEM((SUB, PIX), jnp.int32),
        ]
        + [pltpu.SemaphoreType.DMA] * 5,
        flops=2 * CYCLES * SUB * CAP * PIX,
        size=1 << 20,
        source=pltpu.HBM,
    )(
        turn,
        *(
            pltpu.with_memory_space_constraint(x, pltpu.HBM)
            for x in (
                labels.reshape(1, PIX),
                pixel_mask.reshape(1, PIX),
                dark_level.reshape(1, PIX),
                flat_field.reshape(1, PIX),
                counts,
            )
        ),
    )
    arrived = lax.all_to_all(
        payload.reshape(2 * CYCLES, MESSAGE // 2, 2, LANES), ("pixel", "trow"), 0, 0, tiled=True
    )
    packed = call(
        pack_kernel,
        jax.ShapeDtypeStruct((PAIRS * COLS + SUB, LANES), BF16),
        1,
        flops=1 << 20,
        size=3 << 18,
    )(arrived.reshape(2 * CYCLES * MESSAGE, LANES))
    beside = lax.ppermute(packed, "tcol", [(k, k ^ 1) for k in range(N_TCOL)])
    across = lax.ppermute(packed, "tcol", [(k, k ^ 2) for k in range(N_TCOL)])
    corner = lax.ppermute(across, "tcol", [(k, k ^ 1) for k in range(N_TCOL)])
    depth = PAIRS * LANES
    sends = call(
        gram_kernel,
        jax.ShapeDtypeStruct((N_TROW, ROWS + 8, LANES), F32),
        4,
        scalars=1,
        scratch=[pltpu.VMEM((FRAMES, depth), BF16), pltpu.VMEM((COLS, depth), BF16)],
        flops=2 * FRAMES * FRAMES * depth,
        size=3 << 19,
    )(me, packed, beside, across, corner)
    gets = lax.all_to_all(sends, "trow", 0, 0, tiled=True)
    return call(
        join_kernel,
        (
            jax.ShapeDtypeStruct((OWNED, ROWS, COLS), F32),
            jax.ShapeDtypeStruct((OWNED, FRAMES), F32),
        ),
        1,
        flops=1 << 16,
        size=1 << 19,
    )(gets)


def solution(mesh):
    placed = (P(("trow", "tcol"), "pixel"), P("pixel", None), P("pixel"), P("pixel"), P("pixel"))
    return jax.shard_map(
        per_device,
        mesh=mesh,
        in_specs=placed,
        out_specs=(P("pixel", "trow", "tcol"), P("pixel", None)),
        check_vma=False,
    )
```

```python
import jax
import jax.numpy as jnp
from jax import lax
from jax.experimental import pallas as pl
from jax.experimental.pallas import tpu as pltpu
from jax.sharding import Mesh
from jax.sharding import PartitionSpec as P

CYCLES = 64
FRAMES = 512
CAP = 128
HALF = CAP // 2
PIX = 4096
N_PIXEL = 16
N_TROW = 8
N_TCOL = 4
N_Z = 2
SUB = 16
OWNED = CYCLES // N_PIXEL
COLS = N_TROW * SUB
PAIRS = N_PIXEL // 2
SEEN = N_TROW * N_Z * SUB
ROWS = N_TCOL * SUB
LANES = 128
MESSAGE = 10
FILLED = CYCLES // 2 * SUB
CHUNK = 512
RANK = 128
F32 = jnp.float32
BF16 = jnp.bfloat16


def dot_t(a, b):
    return lax.dot_general(a, b, (((1,), (1,)), ((), ())), preferred_element_type=F32)


def dot_n(a, b):
    return jnp.dot(a, b, preferred_element_type=F32)


def three_parts(x):
    hi = x.astype(BF16).astype(F32)
    rest = x - hi
    mid = rest.astype(BF16).astype(F32)
    return hi, mid, rest - mid


def slot_kernel(
    turn_ref,
    labels_hbm,
    mask_hbm,
    dark_hbm,
    flat_hbm,
    counts_hbm,
    out_ref,
    labels_ref,
    mask_ref,
    dark_ref,
    flat_ref,
    counts_ref,
    labels_sem,
    mask_sem,
    dark_sem,
    flat_sem,
    counts_sem,
):
    get_labels = pltpu.make_async_copy(labels_hbm, labels_ref, labels_sem)
    get_mask = pltpu.make_async_copy(mask_hbm, mask_ref, mask_sem)
    get_dark = pltpu.make_async_copy(dark_hbm, dark_ref, dark_sem)
    get_flat = pltpu.make_async_copy(flat_hbm, flat_ref, flat_sem)
    get_counts = pltpu.make_async_copy(counts_hbm, counts_ref, counts_sem)
    for get in (get_labels, get_mask, get_dark, get_flat, get_counts):
        get.start()
    turn = turn_ref[0]
    get_labels.wait()
    get_mask.wait()
    labels = labels_ref[...]
    live = mask_ref[...].astype(F32)

    before = lax.broadcasted_iota(jnp.int32, (RANK, RANK + LANES), 0)
    at = lax.broadcasted_iota(jnp.int32, (RANK, RANK + LANES), 1)
    ahead = jnp.where((before < at) | (at >= RANK), 1.0, 0.0).astype(BF16)
    cycle_of_row = lax.broadcasted_iota(jnp.int32, (CYCLES, RANK), 0)
    offset = jnp.zeros((CYCLES, LANES), F32)
    ranks = []
    for c in range(PIX // RANK):
        span = slice(c * RANK, (c + 1) * RANK)
        member = jnp.where(labels[:, span] == cycle_of_row, 1.0, 0.0)
        counted = dot_n(member.astype(BF16), ahead)
        place = counted[:, :RANK] + jnp.concatenate([offset] * (RANK // LANES), axis=1)
        ranks.append(jnp.sum(member * place, axis=0, keepdims=True))
        offset = offset + counted[:, RANK:]
    rank = jnp.concatenate(ranks, axis=1).astype(jnp.int32)
    slot = ((rank + turn * HALF) & (CAP - 1)) + (labels & 1) * CAP
    slot16 = slot.astype(F32).astype(BF16)
    pair16 = (labels >> 1).astype(F32).astype(BF16)

    get_dark.wait()
    get_flat.wait()
    get_counts.wait()
    frames = (
        flat_ref[...] * live * (counts_ref[...].astype(F32) - dark_ref[...])
    ).astype(BF16)
    live16 = live.astype(BF16)

    slots = jnp.zeros((FILLED + CYCLES // 2, 2 * CAP), F32)
    slot_of_row = lax.broadcasted_iota(jnp.int32, (2 * CAP, CHUNK), 0).astype(F32).astype(BF16)
    pairs = lax.broadcasted_iota(jnp.int32, (CYCLES // 2, CHUNK), 0).astype(F32).astype(BF16)
    one = jnp.ones((2 * CAP, CHUNK), BF16)
    none = jnp.zeros((SUB, CHUNK), BF16)
    for c in range(PIX // CHUNK):
        span = slice(c * CHUNK, (c + 1) * CHUNK)
        here = jnp.broadcast_to(pair16[:, span], (SUB, CHUNK))
        chunk = frames[:, span]
        usable = jnp.where(
            jnp.broadcast_to(pair16[:, span], (CYCLES // 2, CHUNK)) == pairs,
            jnp.broadcast_to(live16[:, span], (CYCLES // 2, CHUNK)),
            jnp.zeros((CYCLES // 2, CHUNK), BF16),
        )
        left = jnp.concatenate(
            [jnp.where(here == jnp.array(r, BF16), chunk, none) for r in range(CYCLES // 2)]
            + [usable],
            axis=0,
        )
        right = jnp.where(
            jnp.broadcast_to(slot16[:, span], (2 * CAP, CHUNK)) == slot_of_row,
            one,
            jnp.zeros_like(one),
        )
        slots = slots + dot_t(left, right)

    in_row = lax.broadcasted_iota(jnp.int32, (2 * CAP, 2 * CAP), 0) // CAP
    in_col = lax.broadcasted_iota(jnp.int32, (2 * CAP, 2 * CAP), 1) // CAP
    same = jnp.where(in_row == in_col, 1.0, 0.0).astype(BF16)
    sums = dot_n(slots.astype(BF16), same)
    counted = sums[FILLED:]
    sums = sums[:FILLED].reshape(CYCLES // 2, SUB, 2 * CAP)
    lane = lax.broadcasted_iota(jnp.int32, sums.shape, 2) % SUB
    sums = jnp.where(lane == lax.broadcasted_iota(jnp.int32, sums.shape, 1), sums, 0.0)
    hi, mid, lo = three_parts(jnp.sum(sums, axis=1))
    part = lax.broadcasted_iota(jnp.int32, (CYCLES // 2, 2 * CAP), 1) % CAP // SUB
    extra = jnp.where(part == 0, hi, jnp.where(part == 1, mid, jnp.where(part == 2, lo, counted)))
    shape = (CYCLES // 2, SUB // 2, LANES)
    extras = [
        jnp.broadcast_to(extra[:, b * LANES : (b + 1) * LANES][:, None, :], shape)
        for b in range(2)
    ]
    data = (lax.broadcasted_iota(jnp.int32, shape, 2) >= HALF) == (turn == 1)
    row = lax.broadcasted_iota(jnp.int32, shape, 1)
    slots = slots[:FILLED].reshape(CYCLES // 2, SUB, 2 * CAP)
    tiles = []
    for b in range(2):
        early = slots[:, : SUB // 2, b * CAP : (b + 1) * CAP]
        late = slots[:, SUB // 2 :, b * CAP : (b + 1) * CAP]
        tiles.append(jnp.where(data, early, pltpu.roll(late, HALF, axis=2)))
        tiles.append(jnp.where(data, pltpu.roll(early, HALF, axis=2), late))
    groups = []
    for b in range(2):
        extra, (lower, upper) = extras[b], tiles[2 * b : 2 * b + 2]
        second, third, fourth = (
            pltpu.roll(x, 2 * m, axis=1) for m, x in ((1, lower), (2, upper), (3, upper))
        )
        groups += [
            lower,
            jnp.where(row < 2, extra, second),
            jnp.where(row < 2, second, jnp.where(row < 4, extra, third)),
            jnp.where(row < 4, third, jnp.where(row < 6, extra, fourth)),
            jnp.where(row < 6, fourth, extra),
        ]
    out_ref[...] = (
        jnp.concatenate(groups, axis=1).reshape(4 * CYCLES * MESSAGE, LANES).astype(BF16)
    )


def pack_kernel(in_ref, out_ref):
    per_shard = N_TROW * N_Z * MESSAGE
    shape = (N_TROW * N_Z, SUB // 2, LANES)
    low = lax.broadcasted_iota(jnp.int32, shape, 2) < HALF
    row = lax.broadcasted_iota(jnp.int32, (SUB // 2, LANES), 0)
    lane = lax.broadcasted_iota(jnp.int32, (SUB // 2, LANES), 1)
    total = jnp.zeros((per_shard, LANES), F32)
    for pair in range(PAIRS):
        halves = []
        for shard in (2 * pair, 2 * pair + 1):
            rows = in_ref[shard * per_shard : (shard + 1) * per_shard].astype(F32)
            total = total + rows
            group = [rows[8 * i : 8 * i + 8] for i in range(per_shard // 8)]
            tiles = []
            for first in range(0, len(group), 5):
                g = group[first : first + 5]
                tiles.append(g[0])
                tiles.append(pltpu.roll(jnp.where(row < 2, g[2], g[1]), 6, axis=0))
                tiles.append(pltpu.roll(jnp.where(row < 4, g[3], g[2]), 4, axis=0))
                tiles.append(pltpu.roll(jnp.where(row < 6, g[4], g[3]), 2, axis=0))
            halves.append(jnp.concatenate(tiles, axis=0).reshape(shape))
        even, odd = halves
        early = jnp.where(low, even, odd)
        late = pltpu.roll(jnp.where(low, odd, even), HALF, axis=2)
        out_ref[pair * SEEN : (pair + 1) * SEEN] = (
            jnp.concatenate([early, late], axis=1).reshape(SEEN, LANES).astype(BF16)
        )
    tails = []
    for half in range(SEEN // LANES):
        sums = jnp.zeros((SUB // 2, LANES), F32)
        usable = jnp.zeros((SUB // 2, LANES), F32)
        for i in range(LANES // SUB):
            at = (half * LANES // SUB + i) * MESSAGE + SUB // 2
            extra = jnp.broadcast_to(total[at : at + 1], (SUB // 2, LANES))
            added = extra + pltpu.roll(extra, LANES - SUB, axis=1)
            added = added + pltpu.roll(extra, LANES - 2 * SUB, axis=1)
            here = lane // SUB == i
            sums = jnp.where(here, pltpu.roll(added, i * SUB, axis=1), sums)
            count = pltpu.roll(extra, (LANES - 3 * SUB + i * SUB) % LANES, axis=1)
            usable = jnp.where(here, count, usable)
        hi, mid, lo = three_parts(sums)
        n_hi, n_lo, _ = three_parts(usable)
        tail = jnp.zeros((SUB // 2, LANES), F32)
        for i, x in enumerate((hi, mid, lo, n_hi, n_lo)):
            tail = jnp.where(row == i, x, tail)
        tails.append(tail)
    out_ref[PAIRS * SEEN :] = jnp.concatenate(tails, axis=0).astype(BF16)


def gram_kernel(core_ref, z_ref, x0_ref, x1_ref, out_ref, all_ref, own_ref):
    me = core_ref[0]
    my_z = z_ref[0]
    t_row = lax.broadcasted_iota(jnp.int32, (LANES, FRAMES), 0)
    t_col = lax.broadcasted_iota(jnp.int32, (LANES, FRAMES), 1)
    stats = jnp.zeros((SUB // 2, FRAMES), F32)
    for d, ref in enumerate((x0_ref, x1_ref)):
        core = me ^ d
        for j in range(N_TROW):
            for z in range(N_Z):
                first = j * ROWS + z * 2 * SUB + core * SUB
                rows = pl.ds(pl.multiple_of(first, SUB), SUB)
                for pair in range(PAIRS):
                    at = pair * SEEN + (j * N_Z + z) * SUB
                    here = ref[at : at + SUB]
                    all_ref[rows, pair * LANES : (pair + 1) * LANES] = here
        tail = ref[PAIRS * SEEN :]
        for part in range(SEEN // LANES):
            group = t_row // SUB + part * LANES // SUB
            goes_to = group * 2 * SUB + core * SUB + t_row % SUB
            spread = jnp.where(goes_to == t_col, 1.0, 0.0).astype(BF16)
            stats = stats + dot_n(tail, spread)[part * SUB // 2 : (part + 1) * SUB // 2]

    inv = 1.0 / jnp.maximum(stats[0:1] + stats[1:2] + stats[2:3], 1.0)
    inv_col = jnp.broadcast_to(inv, (LANES, FRAMES)).T
    usable = (stats[3:4] + stats[4:5])[:, 0:1]

    group = SUB // 2
    along = jnp.zeros((group, FRAMES), F32)
    row = lax.broadcasted_iota(jnp.int32, (LANES, LANES), 0)
    col = lax.broadcasted_iota(jnp.int32, (LANES, LANES), 1)
    for b in range(FRAMES // LANES):
        start = b * LANES
        width = FRAMES - start
        block = dot_t(all_ref[start : start + LANES], all_ref[start:])
        block = block * (inv_col[start : start + LANES, 0:1] * inv[:, start:])
        corner = jnp.where(col >= row, block[:, :LANES], 0.0)
        block = corner if width == LANES else jnp.concatenate([corner, block[:, LANES:]], axis=1)
        part = block[:group]
        for first in range(group, LANES, group):
            part = part + pltpu.roll(block[first : first + group], width - first, axis=1)
        if width < FRAMES:
            part = jnp.concatenate([part, jnp.zeros((group, start), F32)], axis=1)
        along = along + part
    place = lax.broadcasted_iota(jnp.int32, (group, FRAMES), 0)
    for step in (1, 2, 4):
        along = jnp.where((place & step) > 0, pltpu.roll(along, FRAMES - step, axis=1), along)
    lags = jnp.sum(along, axis=0, keepdims=True)
    remaining = (FRAMES - lax.broadcasted_iota(jnp.int32, (1, FRAMES), 1)).astype(F32)
    lags = lags * usable / remaining
    tail = jnp.concatenate(
        [lags[:, b * LANES : (b + 1) * LANES] for b in range(FRAMES // LANES)]
        + [jnp.zeros((4, LANES), F32)],
        axis=0,
    )

    own_sums = x0_ref[PAIRS * SEEN :].astype(F32)
    own = jnp.zeros((SUB // 2, LANES), F32)
    for z in range(N_Z):
        pieces = []
        for j in range(N_TROW):
            at = (j * N_Z + z) * SUB
            half = at // LANES * (SUB // 2)
            pieces.append(own_sums[half : half + SUB // 2, at % LANES : at % LANES + SUB])
        own = jnp.where(my_z == z, jnp.concatenate(pieces, axis=1), own)
    own_inv = usable / jnp.maximum(own[0:1] + own[1:2] + own[2:3], 1.0)
    for j in range(N_TROW):
        for pair in range(PAIRS):
            at = pl.ds(pl.multiple_of(pair * SEEN + j * N_Z * SUB + my_z * SUB, SUB), SUB)
            own_ref[j * SUB : (j + 1) * SUB, pair * LANES : (pair + 1) * LANES] = x0_ref[at]
    tile = dot_t(all_ref[...], own_ref[...]) * (inv_col * own_inv)
    for i in range(N_TROW):
        out_ref[i, :ROWS] = tile[i * ROWS : (i + 1) * ROWS]
        out_ref[i, ROWS:] = tail


def join_kernel(in_ref, tile_ref, lag_ref):
    for c in range(OWNED):
        both = in_ref[2 * c] + in_ref[2 * c + 1]
        tile_ref[c] = both[:ROWS]
        for b in range(FRAMES // LANES):
            lag_ref[c : c + 1, b * LANES : (b + 1) * LANES] = both[ROWS + b : ROWS + b + 1]


def call(body, out_shape, n_in, scalars=0, scratch=(), flops=0, size=0, source=pltpu.VMEM):
    vmem = pl.BlockSpec(memory_space=pltpu.VMEM)
    given = pl.BlockSpec(memory_space=source)
    smem = pl.BlockSpec(memory_space=pltpu.SMEM)
    many = isinstance(out_shape, tuple)
    return pl.pallas_call(
        body,
        out_shape=out_shape,
        in_specs=[smem] * scalars + [given] * n_in,
        out_specs=(vmem,) * len(out_shape) if many else vmem,
        scratch_shapes=list(scratch),
        compiler_params=pltpu.CompilerParams(vmem_limit_bytes=32 << 20),
        cost_estimate=pl.CostEstimate(flops=flops, bytes_accessed=size, transcendentals=0),
    )


def per_device(counts, labels, pixel_mask, dark_level, flat_field):
    turn = (lax.axis_index("pixel") & 1).astype(jnp.int32).reshape(1)
    core = lax.axis_index("core").astype(jnp.int32).reshape(1)
    z = lax.axis_index("z").astype(jnp.int32).reshape(1)
    payload = call(
        slot_kernel,
        jax.ShapeDtypeStruct((4 * CYCLES * MESSAGE, LANES), BF16),
        5,
        scalars=1,
        scratch=[
            pltpu.VMEM((1, PIX), jnp.int32),
            pltpu.VMEM((1, PIX), jnp.int32),
            pltpu.VMEM((1, PIX), F32),
            pltpu.VMEM((1, PIX), F32),
            pltpu.VMEM((SUB, PIX), jnp.int32),
        ]
        + [pltpu.SemaphoreType.DMA] * 5,
        flops=2 * CYCLES * SUB * CAP * PIX,
        size=1 << 20,
        source=pltpu.HBM,
    )(
        turn,
        *(
            pltpu.with_memory_space_constraint(x, pltpu.HBM)
            for x in (
                labels.reshape(1, PIX),
                pixel_mask.reshape(1, PIX),
                dark_level.reshape(1, PIX),
                flat_field.reshape(1, PIX),
                counts,
            )
        ),
    )
    arrived = lax.all_to_all(
        payload.reshape(4 * CYCLES, MESSAGE // 2, 2, LANES),
        ("pixel", "trow", "z"),
        0,
        0,
        tiled=True,
    )
    packed = call(
        pack_kernel,
        jax.ShapeDtypeStruct((PAIRS * SEEN + SUB, LANES), BF16),
        1,
        flops=1 << 20,
        size=3 << 19,
    )(arrived.reshape(4 * CYCLES * MESSAGE, LANES))
    beside = lax.ppermute(packed, "core", [(0, 1), (1, 0)])
    depth = PAIRS * LANES
    sends = call(
        gram_kernel,
        jax.ShapeDtypeStruct((N_TROW, ROWS + 8, LANES), F32),
        2,
        scalars=2,
        scratch=[pltpu.VMEM((FRAMES, depth), BF16), pltpu.VMEM((COLS, depth), BF16)],
        flops=2 * FRAMES * FRAMES * depth,
        size=3 << 19,
    )(core, z, packed, beside)
    gets = lax.all_to_all(sends, "trow", 0, 0, tiled=True)
    return call(
        join_kernel,
        (
            jax.ShapeDtypeStruct((OWNED, ROWS, COLS), F32),
            jax.ShapeDtypeStruct((OWNED, FRAMES), F32),
        ),
        1,
        flops=1 << 16,
        size=1 << 19,
    )(gets)


def solution(mesh):
    fine = Mesh(
        mesh.devices.reshape(N_PIXEL, N_TROW, N_Z, 2), ("pixel", "trow", "z", "core")
    )
    frames = ("trow", "z", "core")
    placed = (P(frames, "pixel"), P("pixel", None), P("pixel"), P("pixel"), P("pixel"))
    return jax.shard_map(
        per_device,
        mesh=fine,
        in_specs=placed,
        out_specs=(P("pixel", "trow", ("z", "core")), P("pixel", None)),
        check_vma=False,
    )
```

```python
import jax
import jax.numpy as jnp
from jax import lax
from jax.experimental import pallas as pl
from jax.experimental.pallas import tpu as pltpu
from jax.sharding import Mesh
from jax.sharding import PartitionSpec as P

CYCLES = 64
FRAMES = 512
CAP = 128
HALF = CAP // 2
PIX = 4096
N_PIXEL = 16
N_TROW = 8
N_TCOL = 4
N_Z = 2
SUB = 16
OWNED = CYCLES // N_PIXEL
COLS = N_TROW * SUB
PAIRS = N_PIXEL // 2
SEEN = N_TROW * N_Z * SUB
ROWS = N_TCOL * SUB
LANES = 128
MESSAGE = 10
BLOCK = N_PIXEL * MESSAGE
FOUR = 4
FILLED = CYCLES // 2 * SUB
CHUNK = 512
RANK = 128
Y_ORDER = [4, 3, 5, 2, 6, 1, 7, 0]
F32 = jnp.float32
BF16 = jnp.bfloat16


def dot_t(a, b):
    return lax.dot_general(a, b, (((1,), (1,)), ((), ())), preferred_element_type=F32)


def dot_n(a, b):
    return jnp.dot(a, b, preferred_element_type=F32)


def block_of(y, z):
    return ((N_TROW - 1 - y) * N_Z + N_Z - 1 - z) * BLOCK


def three_parts(x):
    hi = x.astype(BF16).astype(F32)
    rest = x - hi
    mid = rest.astype(BF16).astype(F32)
    return hi, mid, rest - mid


def slot_kernel(
    turn_ref,
    labels_hbm,
    mask_hbm,
    dark_hbm,
    flat_hbm,
    counts_hbm,
    out_ref,
    labels_ref,
    mask_ref,
    dark_ref,
    flat_ref,
    counts_ref,
    labels_sem,
    mask_sem,
    dark_sem,
    flat_sem,
    counts_sem,
):
    get_labels = pltpu.make_async_copy(labels_hbm, labels_ref, labels_sem)
    get_mask = pltpu.make_async_copy(mask_hbm, mask_ref, mask_sem)
    get_dark = pltpu.make_async_copy(dark_hbm, dark_ref, dark_sem)
    get_flat = pltpu.make_async_copy(flat_hbm, flat_ref, flat_sem)
    get_counts = pltpu.make_async_copy(counts_hbm, counts_ref, counts_sem)
    for get in (get_labels, get_mask, get_dark, get_flat, get_counts):
        get.start()
    turn = turn_ref[0]
    get_labels.wait()
    get_mask.wait()
    labels = labels_ref[...]
    live = mask_ref[...].astype(F32)

    before = lax.broadcasted_iota(jnp.int32, (RANK, RANK + LANES), 0)
    at = lax.broadcasted_iota(jnp.int32, (RANK, RANK + LANES), 1)
    ahead = jnp.where((before < at) | (at >= RANK), 1.0, 0.0).astype(BF16)
    cycle_of_row = lax.broadcasted_iota(jnp.int32, (CYCLES, RANK), 0)
    offset = jnp.zeros((CYCLES, LANES), F32)
    ranks = []
    for c in range(PIX // RANK):
        span = slice(c * RANK, (c + 1) * RANK)
        member = jnp.where(labels[:, span] == cycle_of_row, 1.0, 0.0)
        counted = dot_n(member.astype(BF16), ahead)
        place = counted[:, :RANK] + jnp.concatenate([offset] * (RANK // LANES), axis=1)
        ranks.append(jnp.sum(member * place, axis=0, keepdims=True))
        offset = offset + counted[:, RANK:]
    rank = jnp.concatenate(ranks, axis=1).astype(jnp.int32)
    slot = ((rank + turn * HALF) & (CAP - 1)) + (labels & 1) * CAP
    slot16 = slot.astype(F32).astype(BF16)
    pair = ((labels >> 1) & 1) * N_PIXEL + N_PIXEL - 1 - labels // OWNED
    pair16 = pair.astype(F32).astype(BF16)

    get_dark.wait()
    get_flat.wait()
    get_counts.wait()
    frames = (
        flat_ref[...] * live * (counts_ref[...].astype(F32) - dark_ref[...])
    ).astype(BF16)
    live16 = live.astype(BF16)

    slots = jnp.zeros((FILLED + CYCLES // 2, 2 * CAP), F32)
    slot_of_row = lax.broadcasted_iota(jnp.int32, (2 * CAP, CHUNK), 0).astype(F32).astype(BF16)
    pairs = lax.broadcasted_iota(jnp.int32, (CYCLES // 2, CHUNK), 0).astype(F32).astype(BF16)
    one = jnp.ones((2 * CAP, CHUNK), BF16)
    none = jnp.zeros((SUB, CHUNK), BF16)
    for c in range(PIX // CHUNK):
        span = slice(c * CHUNK, (c + 1) * CHUNK)
        here = jnp.broadcast_to(pair16[:, span], (SUB, CHUNK))
        chunk = frames[:, span]
        usable = jnp.where(
            jnp.broadcast_to(pair16[:, span], (CYCLES // 2, CHUNK)) == pairs,
            jnp.broadcast_to(live16[:, span], (CYCLES // 2, CHUNK)),
            jnp.zeros((CYCLES // 2, CHUNK), BF16),
        )
        left = jnp.concatenate(
            [jnp.where(here == jnp.array(r, BF16), chunk, none) for r in range(CYCLES // 2)]
            + [usable],
            axis=0,
        )
        right = jnp.where(
            jnp.broadcast_to(slot16[:, span], (2 * CAP, CHUNK)) == slot_of_row,
            one,
            jnp.zeros_like(one),
        )
        slots = slots + dot_t(left, right)

    in_row = lax.broadcasted_iota(jnp.int32, (2 * CAP, 2 * CAP), 0) // CAP
    in_col = lax.broadcasted_iota(jnp.int32, (2 * CAP, 2 * CAP), 1) // CAP
    same = jnp.where(in_row == in_col, 1.0, 0.0).astype(BF16)
    sums = dot_n(slots.astype(BF16), same)
    counted = sums[FILLED:]
    sums = sums[:FILLED].reshape(CYCLES // 2, SUB, 2 * CAP)
    lane = lax.broadcasted_iota(jnp.int32, sums.shape, 2) % SUB
    sums = jnp.where(lane == lax.broadcasted_iota(jnp.int32, sums.shape, 1), sums, 0.0)
    hi, mid, lo = three_parts(jnp.sum(sums, axis=1))
    part = lax.broadcasted_iota(jnp.int32, (CYCLES // 2, 2 * CAP), 1) % CAP // SUB
    extra = jnp.where(part == 0, hi, jnp.where(part == 1, mid, jnp.where(part == 2, lo, counted)))
    shape = (CYCLES // 2, SUB // 2, LANES)
    extras = [
        jnp.broadcast_to(extra[:, b * LANES : (b + 1) * LANES][:, None, :], shape)
        for b in range(2)
    ]
    data = (lax.broadcasted_iota(jnp.int32, shape, 2) >= HALF) == (turn == 1)
    row = lax.broadcasted_iota(jnp.int32, (FOUR, SUB // 2, LANES), 1)
    slots = slots[:FILLED].reshape(CYCLES // 2, SUB, 2 * CAP)
    for b in range(2):
        early = slots[:, : SUB // 2, b * CAP : (b + 1) * CAP]
        late = slots[:, SUB // 2 :, b * CAP : (b + 1) * CAP]
        lower = jnp.where(data, early, pltpu.roll(late, HALF, axis=2))
        upper = jnp.where(data, pltpu.roll(early, HALF, axis=2), late)
        for high in range(2):
            mine = slice(high * N_PIXEL, (high + 1) * N_PIXEL)
            extra = extras[b][mine].reshape(FOUR, FOUR, SUB // 2, LANES)
            for half, tile in enumerate((lower, upper)):
                tile = tile[mine].reshape(FOUR, FOUR, SUB // 2, LANES)
                first = tile[:, 0]
                second, third, fourth = (pltpu.roll(tile[:, m], 2 * m, axis=1) for m in (1, 2, 3))
                groups = [
                    first,
                    jnp.where(row < 2, extra[:, 0], second),
                    jnp.where(row < 2, second, jnp.where(row < 4, extra[:, 1], third)),
                    jnp.where(row < 4, third, jnp.where(row < 6, extra[:, 2], fourth)),
                    jnp.where(row < 6, fourth, extra[:, 3]),
                ]
                block = jnp.concatenate(groups, axis=1).reshape(BLOCK, LANES).astype(BF16)
                y = (high * 2 + b) * 2 + half
                for z in range(N_Z):
                    at = block_of(y, z)
                    out_ref[at : at + BLOCK] = block


def pack_kernel(in_ref, out_ref):
    low = lax.broadcasted_iota(jnp.int32, (PAIRS, SUB // 2, LANES), 2) < HALF
    row = lax.broadcasted_iota(jnp.int32, (SUB // 2, LANES), 0)
    lane = lax.broadcasted_iota(jnp.int32, (SUB // 2, LANES), 1)
    totals = []
    for j in range(N_TROW):
        for z in range(N_Z):
            at = block_of(j, z)
            rows = in_ref[at : at + BLOCK].astype(F32)
            tiles = []
            total = jnp.zeros((FOUR * MESSAGE, LANES), F32)
            for first in range(0, BLOCK, FOUR * MESSAGE):
                part = rows[first : first + FOUR * MESSAGE]
                total = total + part
                g = [part[8 * i : 8 * i + 8] for i in range(5)]
                tiles.append(g[0])
                tiles.append(pltpu.roll(jnp.where(row < 2, g[2], g[1]), 6, axis=0))
                tiles.append(pltpu.roll(jnp.where(row < 4, g[3], g[2]), 4, axis=0))
                tiles.append(pltpu.roll(jnp.where(row < 6, g[4], g[3]), 2, axis=0))
            totals.append(sum(total[i : i + 1] for i in range(8, FOUR * MESSAGE, MESSAGE)))
            tiles = tiles[::-1]
            even = jnp.concatenate(tiles[0::2], axis=0).reshape(low.shape)
            odd = jnp.concatenate(tiles[1::2], axis=0).reshape(low.shape)
            early = jnp.where(low, even, odd)
            late = pltpu.roll(jnp.where(low, odd, even), HALF, axis=2)
            both = jnp.concatenate([early, late], axis=1).astype(BF16)
            for pair in range(PAIRS):
                to = pair * SEEN + (j * N_Z + z) * SUB
                out_ref[to : to + SUB] = both[pair]
    tails = []
    for half in range(SEEN // LANES):
        sums = jnp.zeros((SUB // 2, LANES), F32)
        usable = jnp.zeros((SUB // 2, LANES), F32)
        for i in range(LANES // SUB):
            extra = jnp.broadcast_to(totals[half * LANES // SUB + i], (SUB // 2, LANES))
            added = extra + pltpu.roll(extra, LANES - SUB, axis=1)
            added = added + pltpu.roll(extra, LANES - 2 * SUB, axis=1)
            here = lane // SUB == i
            sums = jnp.where(here, pltpu.roll(added, i * SUB, axis=1), sums)
            count = pltpu.roll(extra, (LANES - 3 * SUB + i * SUB) % LANES, axis=1)
            usable = jnp.where(here, count, usable)
        hi, mid, lo = three_parts(sums)
        n_hi, n_lo, _ = three_parts(usable)
        tail = jnp.zeros((SUB // 2, LANES), F32)
        for i, x in enumerate((hi, mid, lo, n_hi, n_lo)):
            tail = jnp.where(row == i, x, tail)
        tails.append(tail)
    out_ref[PAIRS * SEEN :] = jnp.concatenate(tails, axis=0).astype(BF16)


def gram_kernel(core_ref, z_ref, x0_ref, x1_ref, out_ref, all_ref, own_ref):
    me = core_ref[0]
    my_z = z_ref[0]
    t_row = lax.broadcasted_iota(jnp.int32, (LANES, FRAMES), 0)
    t_col = lax.broadcasted_iota(jnp.int32, (LANES, FRAMES), 1)
    stats = jnp.zeros((SUB // 2, FRAMES), F32)
    for d, ref in enumerate((x0_ref, x1_ref)):
        core = me ^ d
        for j in range(N_TROW):
            for z in range(N_Z):
                first = j * ROWS + z * 2 * SUB + core * SUB
                rows = pl.ds(pl.multiple_of(first, SUB), SUB)
                for pair in range(PAIRS):
                    at = pair * SEEN + (j * N_Z + z) * SUB
                    here = ref[at : at + SUB]
                    all_ref[rows, pair * LANES : (pair + 1) * LANES] = here
        tail = ref[PAIRS * SEEN :]
        for part in range(SEEN // LANES):
            group = t_row // SUB + part * LANES // SUB
            goes_to = group * 2 * SUB + core * SUB + t_row % SUB
            spread = jnp.where(goes_to == t_col, 1.0, 0.0).astype(BF16)
            stats = stats + dot_n(tail, spread)[part * SUB // 2 : (part + 1) * SUB // 2]

    inv = 1.0 / jnp.maximum(stats[0:1] + stats[1:2] + stats[2:3], 1.0)
    inv_col = jnp.broadcast_to(inv, (LANES, FRAMES)).T
    usable = (stats[3:4] + stats[4:5])[:, 0:1]

    group = SUB // 2
    along = jnp.zeros((group, FRAMES), F32)
    row = lax.broadcasted_iota(jnp.int32, (LANES, LANES), 0)
    col = lax.broadcasted_iota(jnp.int32, (LANES, LANES), 1)
    for b in range(FRAMES // LANES):
        start = b * LANES
        width = FRAMES - start
        block = dot_t(all_ref[start : start + LANES], all_ref[start:])
        block = block * (inv_col[start : start + LANES, 0:1] * inv[:, start:])
        corner = jnp.where(col >= row, block[:, :LANES], 0.0)
        block = corner if width == LANES else jnp.concatenate([corner, block[:, LANES:]], axis=1)
        part = block[:group]
        for first in range(group, LANES, group):
            part = part + pltpu.roll(block[first : first + group], width - first, axis=1)
        if width < FRAMES:
            part = jnp.concatenate([part, jnp.zeros((group, start), F32)], axis=1)
        along = along + part
    place = lax.broadcasted_iota(jnp.int32, (group, FRAMES), 0)
    for step in (1, 2, 4):
        along = jnp.where((place & step) > 0, pltpu.roll(along, FRAMES - step, axis=1), along)
    lags = jnp.sum(along, axis=0, keepdims=True)
    remaining = (FRAMES - lax.broadcasted_iota(jnp.int32, (1, FRAMES), 1)).astype(F32)
    lags = lags * usable / remaining
    tail = jnp.concatenate(
        [lags[:, b * LANES : (b + 1) * LANES] for b in range(FRAMES // LANES)]
        + [jnp.zeros((4, LANES), F32)],
        axis=0,
    )

    own_sums = x0_ref[PAIRS * SEEN :].astype(F32)
    own = jnp.zeros((SUB // 2, LANES), F32)
    for z in range(N_Z):
        pieces = []
        for j in range(N_TROW):
            at = (j * N_Z + z) * SUB
            half = at // LANES * (SUB // 2)
            pieces.append(own_sums[half : half + SUB // 2, at % LANES : at % LANES + SUB])
        own = jnp.where(my_z == z, jnp.concatenate(pieces, axis=1), own)
    own_inv = usable / jnp.maximum(own[0:1] + own[1:2] + own[2:3], 1.0)
    for j in range(N_TROW):
        for pair in range(PAIRS):
            at = pl.ds(pl.multiple_of(pair * SEEN + j * N_Z * SUB + my_z * SUB, SUB), SUB)
            own_ref[j * SUB : (j + 1) * SUB, pair * LANES : (pair + 1) * LANES] = x0_ref[at]
    tile = dot_t(all_ref[...], own_ref[...]) * (inv_col * own_inv)
    for i in range(N_TROW):
        at = Y_ORDER.index(i)
        out_ref[at, :ROWS] = tile[i * ROWS : (i + 1) * ROWS]
        out_ref[at, ROWS:] = tail


def join_kernel(in_ref, tile_ref, lag_ref):
    for c in range(OWNED):
        both = in_ref[Y_ORDER.index(2 * c)] + in_ref[Y_ORDER.index(2 * c + 1)]
        tile_ref[c] = both[:ROWS]
        for b in range(FRAMES // LANES):
            lag_ref[c : c + 1, b * LANES : (b + 1) * LANES] = both[ROWS + b : ROWS + b + 1]


def call(body, out_shape, n_in, scalars=0, scratch=(), flops=0, size=0, source=pltpu.VMEM):
    vmem = pl.BlockSpec(memory_space=pltpu.VMEM)
    given = pl.BlockSpec(memory_space=source)
    smem = pl.BlockSpec(memory_space=pltpu.SMEM)
    many = isinstance(out_shape, tuple)
    return pl.pallas_call(
        body,
        out_shape=out_shape,
        in_specs=[smem] * scalars + [given] * n_in,
        out_specs=(vmem,) * len(out_shape) if many else vmem,
        scratch_shapes=list(scratch),
        compiler_params=pltpu.CompilerParams(vmem_limit_bytes=32 << 20),
        cost_estimate=pl.CostEstimate(flops=flops, bytes_accessed=size, transcendentals=0),
    )


def per_device(counts, labels, pixel_mask, dark_level, flat_field):
    turn = (lax.axis_index("pixel") & 1).astype(jnp.int32).reshape(1)
    core = lax.axis_index("core").astype(jnp.int32).reshape(1)
    z = lax.axis_index("z").astype(jnp.int32).reshape(1)
    payload = call(
        slot_kernel,
        jax.ShapeDtypeStruct((4 * CYCLES * MESSAGE, LANES), BF16),
        5,
        scalars=1,
        scratch=[
            pltpu.VMEM((1, PIX), jnp.int32),
            pltpu.VMEM((1, PIX), jnp.int32),
            pltpu.VMEM((1, PIX), F32),
            pltpu.VMEM((1, PIX), F32),
            pltpu.VMEM((SUB, PIX), jnp.int32),
        ]
        + [pltpu.SemaphoreType.DMA] * 5,
        flops=2 * CYCLES * SUB * CAP * PIX,
        size=1 << 20,
        source=pltpu.HBM,
    )(
        turn,
        *(
            pltpu.with_memory_space_constraint(x, pltpu.HBM)
            for x in (
                labels.reshape(1, PIX),
                pixel_mask.reshape(1, PIX),
                dark_level.reshape(1, PIX),
                flat_field.reshape(1, PIX),
                counts,
            )
        ),
    )
    order = [
        (p * N_TROW + y) * N_Z + z
        for y in range(N_TROW)[::-1]
        for z in range(N_Z)[::-1]
        for p in range(N_PIXEL)[::-1]
    ]
    arrived = lax.all_to_all(
        payload.reshape(4 * CYCLES, MESSAGE // 2, 2, LANES),
        ("pixel", "trow", "z"),
        0,
        0,
        tiled=True,
        axis_index_groups=[order],
    )
    packed = call(
        pack_kernel,
        jax.ShapeDtypeStruct((PAIRS * SEEN + SUB, LANES), BF16),
        1,
        flops=1 << 20,
        size=3 << 19,
    )(arrived.reshape(4 * CYCLES * MESSAGE, LANES))
    beside = lax.ppermute(packed, "core", [(0, 1), (1, 0)])
    depth = PAIRS * LANES
    sends = call(
        gram_kernel,
        jax.ShapeDtypeStruct((N_TROW, ROWS + 8, LANES), F32),
        2,
        scalars=2,
        scratch=[pltpu.VMEM((FRAMES, depth), BF16), pltpu.VMEM((COLS, depth), BF16)],
        flops=2 * FRAMES * FRAMES * depth,
        size=3 << 19,
    )(core, z, packed, beside)
    gets = lax.all_to_all(
        sends, "trow", 0, 0, tiled=True, axis_index_groups=[Y_ORDER]
    )
    return call(
        join_kernel,
        (
            jax.ShapeDtypeStruct((OWNED, ROWS, COLS), F32),
            jax.ShapeDtypeStruct((OWNED, FRAMES), F32),
        ),
        1,
        flops=1 << 16,
        size=1 << 19,
    )(gets)


def solution(mesh):
    fine = Mesh(
        mesh.devices.reshape(N_PIXEL, N_TROW, N_Z, 2), ("pixel", "trow", "z", "core")
    )
    frames = ("trow", "z", "core")
    placed = (P(frames, "pixel"), P("pixel", None), P("pixel"), P("pixel"), P("pixel"))
    return jax.shard_map(
        per_device,
        mesh=fine,
        in_specs=placed,
        out_specs=(P("pixel", "trow", ("z", "core")), P("pixel", None)),
        check_vma=False,
    )
```

```python
import jax
import jax.numpy as jnp
from jax import lax
from jax.experimental import pallas as pl
from jax.experimental.pallas import tpu as pltpu
from jax.sharding import PartitionSpec as P

CYCLES = 64
FRAMES = 512
CAP = 128
HALF = CAP // 2
PIX = 4096
N_PIXEL = 16
N_TROW = 8
N_TCOL = 4
SUB = 16
OWNED = CYCLES // N_PIXEL
COLS = N_TROW * SUB
PAIRS = N_PIXEL // 2
ROWS = N_TCOL * SUB
LANES = 128
MESSAGE = 10
FILLED = CYCLES // 2 * SUB
CHUNK = 512
RANK = 128
Y_ORDER = [4, 3, 5, 2, 6, 1, 7, 0]
F32 = jnp.float32
BF16 = jnp.bfloat16


def dot_t(a, b):
    return lax.dot_general(a, b, (((1,), (1,)), ((), ())), preferred_element_type=F32)


def dot_n(a, b):
    return jnp.dot(a, b, preferred_element_type=F32)


def three_parts(x):
    hi = x.astype(BF16).astype(F32)
    rest = x - hi
    mid = rest.astype(BF16).astype(F32)
    return hi, mid, rest - mid


def slot_kernel(
    turn_ref,
    labels_hbm,
    mask_hbm,
    dark_hbm,
    flat_hbm,
    counts_hbm,
    out_ref,
    labels_ref,
    mask_ref,
    dark_ref,
    flat_ref,
    counts_ref,
    labels_sem,
    mask_sem,
    dark_sem,
    flat_sem,
    counts_sem,
):
    get_labels = pltpu.make_async_copy(labels_hbm, labels_ref, labels_sem)
    get_mask = pltpu.make_async_copy(mask_hbm, mask_ref, mask_sem)
    get_dark = pltpu.make_async_copy(dark_hbm, dark_ref, dark_sem)
    get_flat = pltpu.make_async_copy(flat_hbm, flat_ref, flat_sem)
    get_counts = pltpu.make_async_copy(counts_hbm, counts_ref, counts_sem)
    for get in (get_labels, get_mask, get_dark, get_flat, get_counts):
        get.start()
    turn = turn_ref[0]
    get_labels.wait()
    get_mask.wait()
    labels = labels_ref[...]
    live = mask_ref[...].astype(F32)

    before = lax.broadcasted_iota(jnp.int32, (RANK, RANK + LANES), 0)
    at = lax.broadcasted_iota(jnp.int32, (RANK, RANK + LANES), 1)
    ahead = jnp.where((before < at) | (at >= RANK), 1.0, 0.0).astype(BF16)
    cycle_of_row = lax.broadcasted_iota(jnp.int32, (CYCLES, RANK), 0)
    offset = jnp.zeros((CYCLES, LANES), F32)
    ranks = []
    for c in range(PIX // RANK):
        span = slice(c * RANK, (c + 1) * RANK)
        member = jnp.where(labels[:, span] == cycle_of_row, 1.0, 0.0)
        counted = dot_n(member.astype(BF16), ahead)
        place = counted[:, :RANK] + jnp.concatenate([offset] * (RANK // LANES), axis=1)
        ranks.append(jnp.sum(member * place, axis=0, keepdims=True))
        offset = offset + counted[:, RANK:]
    rank = jnp.concatenate(ranks, axis=1).astype(jnp.int32)
    back = CYCLES - 1 - labels
    slot = ((rank + turn * HALF) & (CAP - 1)) + (back & 1) * CAP
    slot16 = slot.astype(F32).astype(BF16)
    pair16 = (back >> 1).astype(F32).astype(BF16)

    get_dark.wait()
    get_flat.wait()
    get_counts.wait()
    frames = (
        flat_ref[...] * live * (counts_ref[...].astype(F32) - dark_ref[...])
    ).astype(BF16)
    live16 = live.astype(BF16)

    slots = jnp.zeros((FILLED + CYCLES // 2, 2 * CAP), F32)
    slot_of_row = lax.broadcasted_iota(jnp.int32, (2 * CAP, CHUNK), 0).astype(F32).astype(BF16)
    pairs = lax.broadcasted_iota(jnp.int32, (CYCLES // 2, CHUNK), 0).astype(F32).astype(BF16)
    one = jnp.ones((2 * CAP, CHUNK), BF16)
    none = jnp.zeros((SUB, CHUNK), BF16)
    for c in range(PIX // CHUNK):
        span = slice(c * CHUNK, (c + 1) * CHUNK)
        here = jnp.broadcast_to(pair16[:, span], (SUB, CHUNK))
        chunk = frames[:, span]
        usable = jnp.where(
            jnp.broadcast_to(pair16[:, span], (CYCLES // 2, CHUNK)) == pairs,
            jnp.broadcast_to(live16[:, span], (CYCLES // 2, CHUNK)),
            jnp.zeros((CYCLES // 2, CHUNK), BF16),
        )
        left = jnp.concatenate(
            [jnp.where(here == jnp.array(r, BF16), chunk, none) for r in range(CYCLES // 2)]
            + [usable],
            axis=0,
        )
        right = jnp.where(
            jnp.broadcast_to(slot16[:, span], (2 * CAP, CHUNK)) == slot_of_row,
            one,
            jnp.zeros_like(one),
        )
        slots = slots + dot_t(left, right)

    in_row = lax.broadcasted_iota(jnp.int32, (2 * CAP, 2 * CAP), 0) // CAP
    in_col = lax.broadcasted_iota(jnp.int32, (2 * CAP, 2 * CAP), 1) // CAP
    same = jnp.where(in_row == in_col, 1.0, 0.0).astype(BF16)
    sums = dot_n(slots.astype(BF16), same)
    counted = sums[FILLED:]
    sums = sums[:FILLED].reshape(CYCLES // 2, SUB, 2 * CAP)
    lane = lax.broadcasted_iota(jnp.int32, sums.shape, 2) % SUB
    sums = jnp.where(lane == lax.broadcasted_iota(jnp.int32, sums.shape, 1), sums, 0.0)
    hi, mid, lo = three_parts(jnp.sum(sums, axis=1))
    part = lax.broadcasted_iota(jnp.int32, (CYCLES // 2, 2 * CAP), 1) % CAP // SUB
    extra = jnp.where(part == 0, hi, jnp.where(part == 1, mid, jnp.where(part == 2, lo, counted)))
    shape = (CYCLES // 2, SUB // 2, LANES)
    extras = [
        jnp.broadcast_to(extra[:, b * LANES : (b + 1) * LANES][:, None, :], shape)
        for b in range(2)
    ]
    data = (lax.broadcasted_iota(jnp.int32, shape, 2) >= HALF) == (turn == 1)
    row = lax.broadcasted_iota(jnp.int32, shape, 1)
    slots = slots[:FILLED].reshape(CYCLES // 2, SUB, 2 * CAP)
    tiles = []
    for b in range(2):
        early = slots[:, : SUB // 2, b * CAP : (b + 1) * CAP]
        late = slots[:, SUB // 2 :, b * CAP : (b + 1) * CAP]
        tiles.append(jnp.where(data, pltpu.roll(early, HALF, axis=2), late))
        tiles.append(jnp.where(data, early, pltpu.roll(late, HALF, axis=2)))
    second, third, fourth = (pltpu.roll(tiles[m], 2 * m, axis=1) for m in (1, 2, 3))
    groups = [
        tiles[0],
        jnp.where(row < 2, extras[0], second),
        jnp.where(row < 2, second, jnp.where(row < 4, extras[0], third)),
        jnp.where(row < 4, third, jnp.where(row < 6, extras[1], fourth)),
        jnp.where(row < 6, fourth, extras[1]),
    ]
    out_ref[...] = (
        jnp.concatenate(groups, axis=1).reshape(2 * CYCLES * MESSAGE, LANES).astype(BF16)
    )


def pack_kernel(in_ref, out_ref):
    per_shard = N_TROW * MESSAGE
    shape = (N_TROW, SUB // 2, LANES)
    low = lax.broadcasted_iota(jnp.int32, shape, 2) < HALF
    row = lax.broadcasted_iota(jnp.int32, (SUB // 2, LANES), 0)
    lane = lax.broadcasted_iota(jnp.int32, (SUB // 2, LANES), 1)
    total = jnp.zeros((per_shard, LANES), F32)
    for pair in range(PAIRS):
        halves = []
        for shard in (N_PIXEL - 1 - 2 * pair, N_PIXEL - 2 - 2 * pair):
            rows = in_ref[shard * per_shard : (shard + 1) * per_shard].astype(F32)
            total = total + rows
            group = [rows[8 * i : 8 * i + 8] for i in range(per_shard // 8)]
            tiles = []
            for first in (0, 5):
                g = group[first : first + 5]
                tiles.append(g[0])
                tiles.append(pltpu.roll(jnp.where(row < 2, g[2], g[1]), 6, axis=0))
                tiles.append(pltpu.roll(jnp.where(row < 4, g[3], g[2]), 4, axis=0))
                tiles.append(pltpu.roll(jnp.where(row < 6, g[4], g[3]), 2, axis=0))
            halves.append(jnp.concatenate(tiles[::-1], axis=0).reshape(shape))
        even, odd = halves
        early = jnp.where(low, even, odd)
        late = pltpu.roll(jnp.where(low, odd, even), HALF, axis=2)
        out_ref[pair * COLS : (pair + 1) * COLS] = (
            jnp.concatenate([early, late], axis=1).reshape(COLS, LANES).astype(BF16)
        )
    sums = jnp.zeros((SUB // 2, LANES), F32)
    usable = jnp.zeros((SUB // 2, LANES), F32)
    for j in range(N_TROW):
        at = (N_TROW - 1 - j) * MESSAGE + SUB // 2
        extra = jnp.broadcast_to(total[at : at + 1], (SUB // 2, LANES))
        added = extra + pltpu.roll(extra, LANES - SUB, axis=1)
        added = added + pltpu.roll(extra, LANES - 2 * SUB, axis=1)
        here = lane // SUB == j
        sums = jnp.where(here, pltpu.roll(added, j * SUB, axis=1), sums)
        count = pltpu.roll(extra, (LANES - 3 * SUB + j * SUB) % LANES, axis=1)
        usable = jnp.where(here, count, usable)
    hi, mid, lo = three_parts(sums)
    n_hi, n_lo, _ = three_parts(usable)
    tail = jnp.zeros((SUB // 2, LANES), F32)
    for i, x in enumerate((hi, mid, lo, n_hi, n_lo)):
        tail = jnp.where(row == i, x, tail)
    out_ref[PAIRS * COLS :] = jnp.concatenate([tail, jnp.zeros_like(tail)], axis=0).astype(BF16)


def gram_kernel(me_ref, x0_ref, x1_ref, x2_ref, x3_ref, out_ref, all_ref, own_ref):
    me = me_ref[0]
    depth = PAIRS * LANES
    t_row = lax.broadcasted_iota(jnp.int32, (COLS, FRAMES), 0)
    t_col = lax.broadcasted_iota(jnp.int32, (COLS, FRAMES), 1)
    stats = jnp.zeros((SUB, FRAMES), F32)
    for d, ref in enumerate((x0_ref, x1_ref, x2_ref, x3_ref)):
        k = me ^ d
        for j in range(N_TROW):
            rows = pl.ds(pl.multiple_of(j * ROWS + k * SUB, SUB), SUB)
            for pair in range(PAIRS):
                at = pair * COLS + j * SUB
                all_ref[rows, pair * LANES : (pair + 1) * LANES] = ref[at : at + SUB]
        goes_to = (t_row // SUB) * ROWS + k * SUB + t_row % SUB
        spread = jnp.where(goes_to == t_col, 1.0, 0.0).astype(BF16)
        stats = stats + dot_n(ref[PAIRS * COLS :], spread)
    for pair in range(PAIRS):
        own_ref[:, pair * LANES : (pair + 1) * LANES] = x0_ref[pair * COLS : (pair + 1) * COLS]

    own = x0_ref[PAIRS * COLS :].astype(F32)
    own_inv = 1.0 / jnp.maximum(own[0:1] + own[1:2] + own[2:3], 1.0)
    usable = (own[3:4] + own[4:5])[:, 0:1]
    inv = 1.0 / jnp.maximum(stats[0:1] + stats[1:2] + stats[2:3], 1.0)
    inv_col = jnp.broadcast_to(inv, (LANES, FRAMES)).T

    tile = dot_t(all_ref[...], own_ref[...])
    tile = tile * (inv_col * (own_inv * usable))

    group = SUB // 2
    along = jnp.zeros((group, FRAMES), F32)
    row = lax.broadcasted_iota(jnp.int32, (LANES, LANES), 0)
    col = lax.broadcasted_iota(jnp.int32, (LANES, LANES), 1)
    for b in range(FRAMES // LANES):
        start = b * LANES
        width = FRAMES - start
        block = dot_t(all_ref[start : start + LANES], all_ref[start:])
        block = block * (inv_col[start : start + LANES, 0:1] * inv[:, start:])
        corner = jnp.where(col >= row, block[:, :LANES], 0.0)
        block = corner if width == LANES else jnp.concatenate([corner, block[:, LANES:]], axis=1)
        part = block[:group]
        for first in range(group, LANES, group):
            part = part + pltpu.roll(block[first : first + group], width - first, axis=1)
        if width < FRAMES:
            part = jnp.concatenate([part, jnp.zeros((group, start), F32)], axis=1)
        along = along + part
    place = lax.broadcasted_iota(jnp.int32, (group, FRAMES), 0)
    for step in (1, 2, 4):
        along = jnp.where((place & step) > 0, pltpu.roll(along, FRAMES - step, axis=1), along)
    lags = jnp.sum(along, axis=0, keepdims=True)
    remaining = (FRAMES - lax.broadcasted_iota(jnp.int32, (1, FRAMES), 1)).astype(F32)
    lags = lags * usable / remaining

    for i in range(N_TROW):
        at = Y_ORDER.index(i)
        out_ref[at, :ROWS] = tile[i * ROWS : (i + 1) * ROWS]
        for b in range(FRAMES // LANES):
            out_ref[at, ROWS + b : ROWS + b + 1] = lags[:, b * LANES : (b + 1) * LANES]
        out_ref[at, ROWS + 4 :] = jnp.zeros((4, LANES), F32)


def join_kernel(in_ref, tile_ref, lag_ref):
    for c in range(OWNED):
        both = in_ref[Y_ORDER.index(2 * c)] + in_ref[Y_ORDER.index(2 * c + 1)]
        tile_ref[c] = both[:ROWS]
        for b in range(FRAMES // LANES):
            lag_ref[c : c + 1, b * LANES : (b + 1) * LANES] = both[ROWS + b : ROWS + b + 1]


def call(body, out_shape, n_in, scalars=0, scratch=(), flops=0, size=0, source=pltpu.VMEM):
    vmem = pl.BlockSpec(memory_space=pltpu.VMEM)
    given = pl.BlockSpec(memory_space=source)
    smem = pl.BlockSpec(memory_space=pltpu.SMEM)
    many = isinstance(out_shape, tuple)
    return pl.pallas_call(
        body,
        out_shape=out_shape,
        in_specs=[smem] * scalars + [given] * n_in,
        out_specs=(vmem,) * len(out_shape) if many else vmem,
        scratch_shapes=list(scratch),
        compiler_params=pltpu.CompilerParams(vmem_limit_bytes=32 << 20),
        cost_estimate=pl.CostEstimate(flops=flops, bytes_accessed=size, transcendentals=0),
    )


def per_device(counts, labels, pixel_mask, dark_level, flat_field):
    turn = (lax.axis_index("pixel") & 1).astype(jnp.int32).reshape(1)
    me = lax.axis_index("tcol").astype(jnp.int32).reshape(1)
    payload = call(
        slot_kernel,
        jax.ShapeDtypeStruct((2 * CYCLES * MESSAGE, LANES), BF16),
        5,
        scalars=1,
        scratch=[
            pltpu.VMEM((1, PIX), jnp.int32),
            pltpu.VMEM((1, PIX), jnp.int32),
            pltpu.VMEM((1, PIX), F32),
            pltpu.VMEM((1, PIX), F32),
            pltpu.VMEM((SUB, PIX), jnp.int32),
        ]
        + [pltpu.SemaphoreType.DMA] * 5,
        flops=2 * CYCLES * SUB * CAP * PIX,
        size=1 << 20,
        source=pltpu.HBM,
    )(
        turn,
        *(
            pltpu.with_memory_space_constraint(x, pltpu.HBM)
            for x in (
                labels.reshape(1, PIX),
                pixel_mask.reshape(1, PIX),
                dark_level.reshape(1, PIX),
                flat_field.reshape(1, PIX),
                counts,
            )
        ),
    )
    arrived = lax.all_to_all(
        payload.reshape(2 * CYCLES, MESSAGE // 2, 2, LANES),
        ("pixel", "trow"),
        0,
        0,
        tiled=True,
        axis_index_groups=[list(range(N_PIXEL * N_TROW))[::-1]],
    )
    packed = call(
        pack_kernel,
        jax.ShapeDtypeStruct((PAIRS * COLS + SUB, LANES), BF16),
        1,
        flops=1 << 20,
        size=3 << 18,
    )(arrived.reshape(2 * CYCLES * MESSAGE, LANES))
    beside = lax.ppermute(packed, "tcol", [(k, k ^ 1) for k in range(N_TCOL)])
    across = lax.ppermute(packed, "tcol", [(k, k ^ 2) for k in range(N_TCOL)])
    corner = lax.ppermute(across, "tcol", [(k, k ^ 1) for k in range(N_TCOL)])
    depth = PAIRS * LANES
    sends = call(
        gram_kernel,
        jax.ShapeDtypeStruct((N_TROW, ROWS + 8, LANES), F32),
        4,
        scalars=1,
        scratch=[pltpu.VMEM((FRAMES, depth), BF16), pltpu.VMEM((COLS, depth), BF16)],
        flops=2 * FRAMES * FRAMES * depth,
        size=3 << 19,
    )(me, packed, beside, across, corner)
    gets = lax.all_to_all(sends, "trow", 0, 0, tiled=True, axis_index_groups=[Y_ORDER])
    return call(
        join_kernel,
        (
            jax.ShapeDtypeStruct((OWNED, ROWS, COLS), F32),
            jax.ShapeDtypeStruct((OWNED, FRAMES), F32),
        ),
        1,
        flops=1 << 16,
        size=1 << 19,
    )(gets)


def solution(mesh):
    placed = (P(("trow", "tcol"), "pixel"), P("pixel", None), P("pixel"), P("pixel"), P("pixel"))
    return jax.shard_map(
        per_device,
        mesh=mesh,
        in_specs=placed,
        out_specs=(P("pixel", "trow", "tcol"), P("pixel", None)),
        check_vma=False,
    )
```

```python
import jax
import jax.numpy as jnp
from jax import lax
from jax.experimental import pallas as pl
from jax.experimental.pallas import tpu as pltpu
from jax.sharding import PartitionSpec as P

CYCLES = 64
FRAMES = 512
CAP = 128
HALF = CAP // 2
PIX = 4096
N_PIXEL = 16
N_TROW = 8
N_TCOL = 4
SUB = 16
OWNED = CYCLES // N_PIXEL
COLS = N_TROW * SUB
PAIRS = N_PIXEL // 2
ROWS = N_TCOL * SUB
LANES = 128
MESSAGE = 10
FILLED = CYCLES // 2 * SUB
CHUNK = 512
RANK = 128
Y_ORDER = [4, 3, 5, 2, 6, 1, 7, 0]
FIRST_PIXEL, FIRST_Y = 10, 5
FIRST = FIRST_PIXEL * N_TROW + FIRST_Y
F32 = jnp.float32
BF16 = jnp.bfloat16


def dot_t(a, b):
    return lax.dot_general(a, b, (((1,), (1,)), ((), ())), preferred_element_type=F32)


def dot_n(a, b):
    return jnp.dot(a, b, preferred_element_type=F32)


def three_parts(x):
    hi = x.astype(BF16).astype(F32)
    rest = x - hi
    mid = rest.astype(BF16).astype(F32)
    return hi, mid, rest - mid


def slot_kernel(
    turn_ref,
    labels_hbm,
    mask_hbm,
    dark_hbm,
    flat_hbm,
    counts_hbm,
    out_ref,
    labels_ref,
    mask_ref,
    dark_ref,
    flat_ref,
    counts_ref,
    labels_sem,
    mask_sem,
    dark_sem,
    flat_sem,
    counts_sem,
):
    get_labels = pltpu.make_async_copy(labels_hbm, labels_ref, labels_sem)
    get_mask = pltpu.make_async_copy(mask_hbm, mask_ref, mask_sem)
    get_dark = pltpu.make_async_copy(dark_hbm, dark_ref, dark_sem)
    get_flat = pltpu.make_async_copy(flat_hbm, flat_ref, flat_sem)
    get_counts = pltpu.make_async_copy(counts_hbm, counts_ref, counts_sem)
    for get in (get_labels, get_mask, get_dark, get_flat, get_counts):
        get.start()
    turn = turn_ref[0]
    get_labels.wait()
    get_mask.wait()
    labels = labels_ref[...]
    live = mask_ref[...].astype(F32)

    before = lax.broadcasted_iota(jnp.int32, (RANK, RANK + LANES), 0)
    at = lax.broadcasted_iota(jnp.int32, (RANK, RANK + LANES), 1)
    ahead = jnp.where((before < at) | (at >= RANK), 1.0, 0.0).astype(BF16)
    cycle_of_row = lax.broadcasted_iota(jnp.int32, (CYCLES, RANK), 0)
    offset = jnp.zeros((CYCLES, LANES), F32)
    ranks = []
    for c in range(PIX // RANK):
        span = slice(c * RANK, (c + 1) * RANK)
        member = jnp.where(labels[:, span] == cycle_of_row, 1.0, 0.0)
        counted = dot_n(member.astype(BF16), ahead)
        place = counted[:, :RANK] + jnp.concatenate([offset] * (RANK // LANES), axis=1)
        ranks.append(jnp.sum(member * place, axis=0, keepdims=True))
        offset = offset + counted[:, RANK:]
    rank = jnp.concatenate(ranks, axis=1).astype(jnp.int32)
    back = labels ^ (FIRST // 2)
    slot = ((rank + turn * HALF) & (CAP - 1)) + (back & 1) * CAP
    slot16 = slot.astype(F32).astype(BF16)
    pair16 = (back >> 1).astype(F32).astype(BF16)

    get_dark.wait()
    get_flat.wait()
    get_counts.wait()
    frames = (
        flat_ref[...] * live * (counts_ref[...].astype(F32) - dark_ref[...])
    ).astype(BF16)
    live16 = live.astype(BF16)

    slots = jnp.zeros((FILLED + CYCLES // 2, 2 * CAP), F32)
    slot_of_row = lax.broadcasted_iota(jnp.int32, (2 * CAP, CHUNK), 0).astype(F32).astype(BF16)
    pairs = lax.broadcasted_iota(jnp.int32, (CYCLES // 2, CHUNK), 0).astype(F32).astype(BF16)
    one = jnp.ones((2 * CAP, CHUNK), BF16)
    none = jnp.zeros((SUB, CHUNK), BF16)
    for c in range(PIX // CHUNK):
        span = slice(c * CHUNK, (c + 1) * CHUNK)
        here = jnp.broadcast_to(pair16[:, span], (SUB, CHUNK))
        chunk = frames[:, span]
        usable = jnp.where(
            jnp.broadcast_to(pair16[:, span], (CYCLES // 2, CHUNK)) == pairs,
            jnp.broadcast_to(live16[:, span], (CYCLES // 2, CHUNK)),
            jnp.zeros((CYCLES // 2, CHUNK), BF16),
        )
        left = jnp.concatenate(
            [jnp.where(here == jnp.array(r, BF16), chunk, none) for r in range(CYCLES // 2)]
            + [usable],
            axis=0,
        )
        right = jnp.where(
            jnp.broadcast_to(slot16[:, span], (2 * CAP, CHUNK)) == slot_of_row,
            one,
            jnp.zeros_like(one),
        )
        slots = slots + dot_t(left, right)

    in_row = lax.broadcasted_iota(jnp.int32, (2 * CAP, 2 * CAP), 0) // CAP
    in_col = lax.broadcasted_iota(jnp.int32, (2 * CAP, 2 * CAP), 1) // CAP
    same = jnp.where(in_row == in_col, 1.0, 0.0).astype(BF16)
    sums = dot_n(slots.astype(BF16), same)
    counted = sums[FILLED:]
    sums = sums[:FILLED].reshape(CYCLES // 2, SUB, 2 * CAP)
    lane = lax.broadcasted_iota(jnp.int32, sums.shape, 2) % SUB
    sums = jnp.where(lane == lax.broadcasted_iota(jnp.int32, sums.shape, 1), sums, 0.0)
    hi, mid, lo = three_parts(jnp.sum(sums, axis=1))
    part = lax.broadcasted_iota(jnp.int32, (CYCLES // 2, 2 * CAP), 1) % CAP // SUB
    extra = jnp.where(part == 0, hi, jnp.where(part == 1, mid, jnp.where(part == 2, lo, counted)))
    shape = (CYCLES // 2, SUB // 2, LANES)
    extras = [
        jnp.broadcast_to(extra[:, b * LANES : (b + 1) * LANES][:, None, :], shape)
        for b in range(2)
    ]
    data = (lax.broadcasted_iota(jnp.int32, shape, 2) >= HALF) == (turn == 1)
    row = lax.broadcasted_iota(jnp.int32, shape, 1)
    slots = slots[:FILLED].reshape(CYCLES // 2, SUB, 2 * CAP)
    tiles = []
    for b in range(2):
        early = slots[:, : SUB // 2, b * CAP : (b + 1) * CAP]
        late = slots[:, SUB // 2 :, b * CAP : (b + 1) * CAP]
        lower = jnp.where(data, early, pltpu.roll(late, HALF, axis=2))
        upper = jnp.where(data, pltpu.roll(early, HALF, axis=2), late)
        tiles += [lower, upper] if FIRST % 2 == 0 else [upper, lower]
    second, third, fourth = (pltpu.roll(tiles[m], 2 * m, axis=1) for m in (1, 2, 3))
    groups = [
        tiles[0],
        jnp.where(row < 2, extras[0], second),
        jnp.where(row < 2, second, jnp.where(row < 4, extras[0], third)),
        jnp.where(row < 4, third, jnp.where(row < 6, extras[1], fourth)),
        jnp.where(row < 6, fourth, extras[1]),
    ]
    out_ref[...] = (
        jnp.concatenate(groups, axis=1).reshape(2 * CYCLES * MESSAGE, LANES).astype(BF16)
    )


def pack_kernel(in_ref, out_ref):
    per_shard = N_TROW * MESSAGE
    shape = (N_TROW, SUB // 2, LANES)
    low = lax.broadcasted_iota(jnp.int32, shape, 2) < HALF
    row = lax.broadcasted_iota(jnp.int32, (SUB // 2, LANES), 0)
    lane = lax.broadcasted_iota(jnp.int32, (SUB // 2, LANES), 1)
    total = jnp.zeros((per_shard, LANES), F32)
    for pair in range(PAIRS):
        halves = []
        for shard in ((2 * pair) ^ FIRST_PIXEL, (2 * pair + 1) ^ FIRST_PIXEL):
            rows = in_ref[shard * per_shard : (shard + 1) * per_shard].astype(F32)
            total = total + rows
            group = [rows[8 * i : 8 * i + 8] for i in range(per_shard // 8)]
            tiles = []
            for first in (0, 5):
                g = group[first : first + 5]
                tiles.append(g[0])
                tiles.append(pltpu.roll(jnp.where(row < 2, g[2], g[1]), 6, axis=0))
                tiles.append(pltpu.roll(jnp.where(row < 4, g[3], g[2]), 4, axis=0))
                tiles.append(pltpu.roll(jnp.where(row < 6, g[4], g[3]), 2, axis=0))
            tiles = [tiles[j ^ FIRST_Y] for j in range(N_TROW)]
            halves.append(jnp.concatenate(tiles, axis=0).reshape(shape))
        even, odd = halves
        early = jnp.where(low, even, odd)
        late = pltpu.roll(jnp.where(low, odd, even), HALF, axis=2)
        out_ref[pair * COLS : (pair + 1) * COLS] = (
            jnp.concatenate([early, late], axis=1).reshape(COLS, LANES).astype(BF16)
        )
    sums = jnp.zeros((SUB // 2, LANES), F32)
    usable = jnp.zeros((SUB // 2, LANES), F32)
    for j in range(N_TROW):
        at = (j ^ FIRST_Y) * MESSAGE + SUB // 2
        extra = jnp.broadcast_to(total[at : at + 1], (SUB // 2, LANES))
        added = extra + pltpu.roll(extra, LANES - SUB, axis=1)
        added = added + pltpu.roll(extra, LANES - 2 * SUB, axis=1)
        here = lane // SUB == j
        sums = jnp.where(here, pltpu.roll(added, j * SUB, axis=1), sums)
        count = pltpu.roll(extra, (LANES - 3 * SUB + j * SUB) % LANES, axis=1)
        usable = jnp.where(here, count, usable)
    hi, mid, lo = three_parts(sums)
    n_hi, n_lo, _ = three_parts(usable)
    tail = jnp.zeros((SUB // 2, LANES), F32)
    for i, x in enumerate((hi, mid, lo, n_hi, n_lo)):
        tail = jnp.where(row == i, x, tail)
    out_ref[PAIRS * COLS :] = jnp.concatenate([tail, jnp.zeros_like(tail)], axis=0).astype(BF16)


def gram_kernel(me_ref, x0_ref, x1_ref, x2_ref, x3_ref, out_ref, all_ref, own_ref):
    me = me_ref[0]
    depth = PAIRS * LANES
    t_row = lax.broadcasted_iota(jnp.int32, (COLS, FRAMES), 0)
    t_col = lax.broadcasted_iota(jnp.int32, (COLS, FRAMES), 1)
    stats = jnp.zeros((SUB, FRAMES), F32)
    for d, ref in enumerate((x0_ref, x1_ref, x2_ref, x3_ref)):
        k = me ^ d
        for j in range(N_TROW):
            rows = pl.ds(pl.multiple_of(j * ROWS + k * SUB, SUB), SUB)
            for pair in range(PAIRS):
                at = pair * COLS + j * SUB
                all_ref[rows, pair * LANES : (pair + 1) * LANES] = ref[at : at + SUB]
        goes_to = (t_row // SUB) * ROWS + k * SUB + t_row % SUB
        spread = jnp.where(goes_to == t_col, 1.0, 0.0).astype(BF16)
        stats = stats + dot_n(ref[PAIRS * COLS :], spread)
    for pair in range(PAIRS):
        own_ref[:, pair * LANES : (pair + 1) * LANES] = x0_ref[pair * COLS : (pair + 1) * COLS]

    own = x0_ref[PAIRS * COLS :].astype(F32)
    own_inv = 1.0 / jnp.maximum(own[0:1] + own[1:2] + own[2:3], 1.0)
    usable = (own[3:4] + own[4:5])[:, 0:1]
    inv = 1.0 / jnp.maximum(stats[0:1] + stats[1:2] + stats[2:3], 1.0)
    inv_col = jnp.broadcast_to(inv, (LANES, FRAMES)).T

    tile = dot_t(all_ref[...], own_ref[...])
    tile = tile * (inv_col * (own_inv * usable))

    group = SUB // 2
    along = jnp.zeros((group, FRAMES), F32)
    row = lax.broadcasted_iota(jnp.int32, (LANES, LANES), 0)
    col = lax.broadcasted_iota(jnp.int32, (LANES, LANES), 1)
    for b in range(FRAMES // LANES):
        start = b * LANES
        width = FRAMES - start
        block = dot_t(all_ref[start : start + LANES], all_ref[start:])
        block = block * (inv_col[start : start + LANES, 0:1] * inv[:, start:])
        corner = jnp.where(col >= row, block[:, :LANES], 0.0)
        block = corner if width == LANES else jnp.concatenate([corner, block[:, LANES:]], axis=1)
        part = block[:group]
        for first in range(group, LANES, group):
            part = part + pltpu.roll(block[first : first + group], width - first, axis=1)
        if width < FRAMES:
            part = jnp.concatenate([part, jnp.zeros((group, start), F32)], axis=1)
        along = along + part
    place = lax.broadcasted_iota(jnp.int32, (group, FRAMES), 0)
    for step in (1, 2, 4):
        along = jnp.where((place & step) > 0, pltpu.roll(along, FRAMES - step, axis=1), along)
    lags = jnp.sum(along, axis=0, keepdims=True)
    remaining = (FRAMES - lax.broadcasted_iota(jnp.int32, (1, FRAMES), 1)).astype(F32)
    lags = lags * usable / remaining

    for i in range(N_TROW):
        at = Y_ORDER.index(i)
        out_ref[at, :ROWS] = tile[i * ROWS : (i + 1) * ROWS]
        for b in range(FRAMES // LANES):
            out_ref[at, ROWS + b : ROWS + b + 1] = lags[:, b * LANES : (b + 1) * LANES]
        out_ref[at, ROWS + 4 :] = jnp.zeros((4, LANES), F32)


def join_kernel(in_ref, tile_ref, lag_ref):
    for c in range(OWNED):
        both = in_ref[Y_ORDER.index(2 * c)] + in_ref[Y_ORDER.index(2 * c + 1)]
        tile_ref[c] = both[:ROWS]
        for b in range(FRAMES // LANES):
            lag_ref[c : c + 1, b * LANES : (b + 1) * LANES] = both[ROWS + b : ROWS + b + 1]


def call(body, out_shape, n_in, scalars=0, scratch=(), flops=0, size=0, source=pltpu.VMEM):
    vmem = pl.BlockSpec(memory_space=pltpu.VMEM)
    given = pl.BlockSpec(memory_space=source)
    smem = pl.BlockSpec(memory_space=pltpu.SMEM)
    many = isinstance(out_shape, tuple)
    return pl.pallas_call(
        body,
        out_shape=out_shape,
        in_specs=[smem] * scalars + [given] * n_in,
        out_specs=(vmem,) * len(out_shape) if many else vmem,
        scratch_shapes=list(scratch),
        compiler_params=pltpu.CompilerParams(vmem_limit_bytes=32 << 20),
        cost_estimate=pl.CostEstimate(flops=flops, bytes_accessed=size, transcendentals=0),
    )


def per_device(counts, labels, pixel_mask, dark_level, flat_field):
    turn = (lax.axis_index("pixel") & 1).astype(jnp.int32).reshape(1)
    me = lax.axis_index("tcol").astype(jnp.int32).reshape(1)
    payload = call(
        slot_kernel,
        jax.ShapeDtypeStruct((2 * CYCLES * MESSAGE, LANES), BF16),
        5,
        scalars=1,
        scratch=[
            pltpu.VMEM((1, PIX), jnp.int32),
            pltpu.VMEM((1, PIX), jnp.int32),
            pltpu.VMEM((1, PIX), F32),
            pltpu.VMEM((1, PIX), F32),
            pltpu.VMEM((SUB, PIX), jnp.int32),
        ]
        + [pltpu.SemaphoreType.DMA] * 5,
        flops=2 * CYCLES * SUB * CAP * PIX,
        size=1 << 20,
        source=pltpu.HBM,
    )(
        turn,
        *(
            pltpu.with_memory_space_constraint(x, pltpu.HBM)
            for x in (
                labels.reshape(1, PIX),
                pixel_mask.reshape(1, PIX),
                dark_level.reshape(1, PIX),
                flat_field.reshape(1, PIX),
                counts,
            )
        ),
    )
    arrived = lax.all_to_all(
        payload.reshape(2 * CYCLES, MESSAGE // 2, 2, LANES),
        ("pixel", "trow"),
        0,
        0,
        tiled=True,
        axis_index_groups=[[m ^ FIRST for m in range(N_PIXEL * N_TROW)]],
    )
    packed = call(
        pack_kernel,
        jax.ShapeDtypeStruct((PAIRS * COLS + SUB, LANES), BF16),
        1,
        flops=1 << 20,
        size=3 << 18,
    )(arrived.reshape(2 * CYCLES * MESSAGE, LANES))
    beside = lax.ppermute(packed, "tcol", [(k, k ^ 1) for k in range(N_TCOL)])
    across = lax.ppermute(packed, "tcol", [(k, k ^ 2) for k in range(N_TCOL)])
    corner = lax.ppermute(across, "tcol", [(k, k ^ 1) for k in range(N_TCOL)])
    depth = PAIRS * LANES
    sends = call(
        gram_kernel,
        jax.ShapeDtypeStruct((N_TROW, ROWS + 8, LANES), F32),
        4,
        scalars=1,
        scratch=[pltpu.VMEM((FRAMES, depth), BF16), pltpu.VMEM((COLS, depth), BF16)],
        flops=2 * FRAMES * FRAMES * depth,
        size=3 << 19,
    )(me, packed, beside, across, corner)
    gets = lax.all_to_all(sends, "trow", 0, 0, tiled=True, axis_index_groups=[Y_ORDER])
    return call(
        join_kernel,
        (
            jax.ShapeDtypeStruct((OWNED, ROWS, COLS), F32),
            jax.ShapeDtypeStruct((OWNED, FRAMES), F32),
        ),
        1,
        flops=1 << 16,
        size=1 << 19,
    )(gets)


def solution(mesh):
    placed = (P(("trow", "tcol"), "pixel"), P("pixel", None), P("pixel"), P("pixel"), P("pixel"))
    return jax.shard_map(
        per_device,
        mesh=mesh,
        in_specs=placed,
        out_specs=(P("pixel", "trow", "tcol"), P("pixel", None)),
        check_vma=False,
    )
```

```python
import jax
import jax.numpy as jnp
from jax import lax
from jax.experimental import pallas as pl
from jax.experimental.pallas import tpu as pltpu
from jax.sharding import Mesh
from jax.sharding import PartitionSpec as P

CYCLES = 64
FRAMES = 512
CAP = 128
HALF = CAP // 2
PIX = 4096
N_PIXEL = 16
N_TROW = 8
N_TCOL = 4
N_Z = 2
SUB = 16
OWNED = CYCLES // N_PIXEL
COLS = N_TROW * SUB
PAIRS = N_PIXEL // 2
SEEN = N_TROW * N_Z * SUB
ROWS = N_TCOL * SUB
LANES = 128
MESSAGE = 10
BLOCK = N_PIXEL * MESSAGE
FOUR = 4
FILLED = CYCLES // 2 * SUB
CHUNK = 512
RANK = 128
Y_ORDER = [4, 3, 5, 2, 6, 1, 7, 0]
FIRST_PIXEL, FIRST_Y = 10, 5
F32 = jnp.float32
BF16 = jnp.bfloat16


def dot_t(a, b):
    return lax.dot_general(a, b, (((1,), (1,)), ((), ())), preferred_element_type=F32)


def dot_n(a, b):
    return jnp.dot(a, b, preferred_element_type=F32)


def block_of(y, z):
    return ((y ^ FIRST_Y) * N_Z + z) * BLOCK


def three_parts(x):
    hi = x.astype(BF16).astype(F32)
    rest = x - hi
    mid = rest.astype(BF16).astype(F32)
    return hi, mid, rest - mid


def slot_kernel(
    turn_ref,
    labels_hbm,
    mask_hbm,
    dark_hbm,
    flat_hbm,
    counts_hbm,
    out_ref,
    labels_ref,
    mask_ref,
    dark_ref,
    flat_ref,
    counts_ref,
    labels_sem,
    mask_sem,
    dark_sem,
    flat_sem,
    counts_sem,
):
    get_labels = pltpu.make_async_copy(labels_hbm, labels_ref, labels_sem)
    get_mask = pltpu.make_async_copy(mask_hbm, mask_ref, mask_sem)
    get_dark = pltpu.make_async_copy(dark_hbm, dark_ref, dark_sem)
    get_flat = pltpu.make_async_copy(flat_hbm, flat_ref, flat_sem)
    get_counts = pltpu.make_async_copy(counts_hbm, counts_ref, counts_sem)
    for get in (get_labels, get_mask, get_dark, get_flat, get_counts):
        get.start()
    turn = turn_ref[0]
    get_labels.wait()
    get_mask.wait()
    labels = labels_ref[...]
    live = mask_ref[...].astype(F32)

    before = lax.broadcasted_iota(jnp.int32, (RANK, RANK + LANES), 0)
    at = lax.broadcasted_iota(jnp.int32, (RANK, RANK + LANES), 1)
    ahead = jnp.where((before < at) | (at >= RANK), 1.0, 0.0).astype(BF16)
    cycle_of_row = lax.broadcasted_iota(jnp.int32, (CYCLES, RANK), 0)
    offset = jnp.zeros((CYCLES, LANES), F32)
    ranks = []
    for c in range(PIX // RANK):
        span = slice(c * RANK, (c + 1) * RANK)
        member = jnp.where(labels[:, span] == cycle_of_row, 1.0, 0.0)
        counted = dot_n(member.astype(BF16), ahead)
        place = counted[:, :RANK] + jnp.concatenate([offset] * (RANK // LANES), axis=1)
        ranks.append(jnp.sum(member * place, axis=0, keepdims=True))
        offset = offset + counted[:, RANK:]
    rank = jnp.concatenate(ranks, axis=1).astype(jnp.int32)
    slot = ((rank + turn * HALF) & (CAP - 1)) + (labels & 1) * CAP
    slot16 = slot.astype(F32).astype(BF16)
    pair = ((labels >> 1) & 1) * N_PIXEL + ((labels // OWNED) ^ FIRST_PIXEL)
    pair16 = pair.astype(F32).astype(BF16)

    get_dark.wait()
    get_flat.wait()
    get_counts.wait()
    frames = (
        flat_ref[...] * live * (counts_ref[...].astype(F32) - dark_ref[...])
    ).astype(BF16)
    live16 = live.astype(BF16)

    slots = jnp.zeros((FILLED + CYCLES // 2, 2 * CAP), F32)
    slot_of_row = lax.broadcasted_iota(jnp.int32, (2 * CAP, CHUNK), 0).astype(F32).astype(BF16)
    pairs = lax.broadcasted_iota(jnp.int32, (CYCLES // 2, CHUNK), 0).astype(F32).astype(BF16)
    one = jnp.ones((2 * CAP, CHUNK), BF16)
    none = jnp.zeros((SUB, CHUNK), BF16)
    for c in range(PIX // CHUNK):
        span = slice(c * CHUNK, (c + 1) * CHUNK)
        here = jnp.broadcast_to(pair16[:, span], (SUB, CHUNK))
        chunk = frames[:, span]
        usable = jnp.where(
            jnp.broadcast_to(pair16[:, span], (CYCLES // 2, CHUNK)) == pairs,
            jnp.broadcast_to(live16[:, span], (CYCLES // 2, CHUNK)),
            jnp.zeros((CYCLES // 2, CHUNK), BF16),
        )
        left = jnp.concatenate(
            [jnp.where(here == jnp.array(r, BF16), chunk, none) for r in range(CYCLES // 2)]
            + [usable],
            axis=0,
        )
        right = jnp.where(
            jnp.broadcast_to(slot16[:, span], (2 * CAP, CHUNK)) == slot_of_row,
            one,
            jnp.zeros_like(one),
        )
        slots = slots + dot_t(left, right)

    in_row = lax.broadcasted_iota(jnp.int32, (2 * CAP, 2 * CAP), 0) // CAP
    in_col = lax.broadcasted_iota(jnp.int32, (2 * CAP, 2 * CAP), 1) // CAP
    same = jnp.where(in_row == in_col, 1.0, 0.0).astype(BF16)
    sums = dot_n(slots.astype(BF16), same)
    counted = sums[FILLED:]
    sums = sums[:FILLED].reshape(CYCLES // 2, SUB, 2 * CAP)
    lane = lax.broadcasted_iota(jnp.int32, sums.shape, 2) % SUB
    sums = jnp.where(lane == lax.broadcasted_iota(jnp.int32, sums.shape, 1), sums, 0.0)
    hi, mid, lo = three_parts(jnp.sum(sums, axis=1))
    part = lax.broadcasted_iota(jnp.int32, (CYCLES // 2, 2 * CAP), 1) % CAP // SUB
    extra = jnp.where(part == 0, hi, jnp.where(part == 1, mid, jnp.where(part == 2, lo, counted)))
    shape = (CYCLES // 2, SUB // 2, LANES)
    extras = [
        jnp.broadcast_to(extra[:, b * LANES : (b + 1) * LANES][:, None, :], shape)
        for b in range(2)
    ]
    data = (lax.broadcasted_iota(jnp.int32, shape, 2) >= HALF) == (turn == 1)
    row = lax.broadcasted_iota(jnp.int32, (FOUR, SUB // 2, LANES), 1)
    slots = slots[:FILLED].reshape(CYCLES // 2, SUB, 2 * CAP)
    for b in range(2):
        early = slots[:, : SUB // 2, b * CAP : (b + 1) * CAP]
        late = slots[:, SUB // 2 :, b * CAP : (b + 1) * CAP]
        lower = jnp.where(data, early, pltpu.roll(late, HALF, axis=2))
        upper = jnp.where(data, pltpu.roll(early, HALF, axis=2), late)
        for high in range(2):
            mine = slice(high * N_PIXEL, (high + 1) * N_PIXEL)
            extra = extras[b][mine].reshape(FOUR, FOUR, SUB // 2, LANES)
            for half, tile in enumerate((lower, upper)):
                tile = tile[mine].reshape(FOUR, FOUR, SUB // 2, LANES)
                first = tile[:, 0]
                second, third, fourth = (pltpu.roll(tile[:, m], 2 * m, axis=1) for m in (1, 2, 3))
                groups = [
                    first,
                    jnp.where(row < 2, extra[:, 0], second),
                    jnp.where(row < 2, second, jnp.where(row < 4, extra[:, 1], third)),
                    jnp.where(row < 4, third, jnp.where(row < 6, extra[:, 2], fourth)),
                    jnp.where(row < 6, fourth, extra[:, 3]),
                ]
                block = jnp.concatenate(groups, axis=1).reshape(BLOCK, LANES).astype(BF16)
                y = (high * 2 + b) * 2 + half
                for z in range(N_Z):
                    at = block_of(y, z)
                    out_ref[at : at + BLOCK] = block


def pack_kernel(in_ref, out_ref):
    low = lax.broadcasted_iota(jnp.int32, (PAIRS, SUB // 2, LANES), 2) < HALF
    row = lax.broadcasted_iota(jnp.int32, (SUB // 2, LANES), 0)
    lane = lax.broadcasted_iota(jnp.int32, (SUB // 2, LANES), 1)
    totals = []
    for j in range(N_TROW):
        for z in range(N_Z):
            at = block_of(j, z)
            rows = in_ref[at : at + BLOCK].astype(F32)
            tiles = []
            total = jnp.zeros((FOUR * MESSAGE, LANES), F32)
            for first in range(0, BLOCK, FOUR * MESSAGE):
                part = rows[first : first + FOUR * MESSAGE]
                total = total + part
                g = [part[8 * i : 8 * i + 8] for i in range(5)]
                tiles.append(g[0])
                tiles.append(pltpu.roll(jnp.where(row < 2, g[2], g[1]), 6, axis=0))
                tiles.append(pltpu.roll(jnp.where(row < 4, g[3], g[2]), 4, axis=0))
                tiles.append(pltpu.roll(jnp.where(row < 6, g[4], g[3]), 2, axis=0))
            totals.append(sum(total[i : i + 1] for i in range(8, FOUR * MESSAGE, MESSAGE)))
            tiles = [tiles[p ^ FIRST_PIXEL] for p in range(N_PIXEL)]
            even = jnp.concatenate(tiles[0::2], axis=0).reshape(low.shape)
            odd = jnp.concatenate(tiles[1::2], axis=0).reshape(low.shape)
            early = jnp.where(low, even, odd)
            late = pltpu.roll(jnp.where(low, odd, even), HALF, axis=2)
            both = jnp.concatenate([early, late], axis=1).astype(BF16)
            for pair in range(PAIRS):
                to = pair * SEEN + (j * N_Z + z) * SUB
                out_ref[to : to + SUB] = both[pair]
    tails = []
    for half in range(SEEN // LANES):
        sums = jnp.zeros((SUB // 2, LANES), F32)
        usable = jnp.zeros((SUB // 2, LANES), F32)
        for i in range(LANES // SUB):
            extra = jnp.broadcast_to(totals[half * LANES // SUB + i], (SUB // 2, LANES))
            added = extra + pltpu.roll(extra, LANES - SUB, axis=1)
            added = added + pltpu.roll(extra, LANES - 2 * SUB, axis=1)
            here = lane // SUB == i
            sums = jnp.where(here, pltpu.roll(added, i * SUB, axis=1), sums)
            count = pltpu.roll(extra, (LANES - 3 * SUB + i * SUB) % LANES, axis=1)
            usable = jnp.where(here, count, usable)
        hi, mid, lo = three_parts(sums)
        n_hi, n_lo, _ = three_parts(usable)
        tail = jnp.zeros((SUB // 2, LANES), F32)
        for i, x in enumerate((hi, mid, lo, n_hi, n_lo)):
            tail = jnp.where(row == i, x, tail)
        tails.append(tail)
    out_ref[PAIRS * SEEN :] = jnp.concatenate(tails, axis=0).astype(BF16)


def gram_kernel(core_ref, z_ref, x0_ref, x1_ref, out_ref, all_ref, own_ref):
    me = core_ref[0]
    my_z = z_ref[0]
    t_row = lax.broadcasted_iota(jnp.int32, (LANES, FRAMES), 0)
    t_col = lax.broadcasted_iota(jnp.int32, (LANES, FRAMES), 1)
    stats = jnp.zeros((SUB // 2, FRAMES), F32)
    for d, ref in enumerate((x0_ref, x1_ref)):
        core = me ^ d
        for j in range(N_TROW):
            for z in range(N_Z):
                first = j * ROWS + z * 2 * SUB + core * SUB
                rows = pl.ds(pl.multiple_of(first, SUB), SUB)
                for pair in range(PAIRS):
                    at = pair * SEEN + (j * N_Z + z) * SUB
                    here = ref[at : at + SUB]
                    all_ref[rows, pair * LANES : (pair + 1) * LANES] = here
        tail = ref[PAIRS * SEEN :]
        for part in range(SEEN // LANES):
            group = t_row // SUB + part * LANES // SUB
            goes_to = group * 2 * SUB + core * SUB + t_row % SUB
            spread = jnp.where(goes_to == t_col, 1.0, 0.0).astype(BF16)
            stats = stats + dot_n(tail, spread)[part * SUB // 2 : (part + 1) * SUB // 2]

    inv = 1.0 / jnp.maximum(stats[0:1] + stats[1:2] + stats[2:3], 1.0)
    inv_col = jnp.broadcast_to(inv, (LANES, FRAMES)).T
    usable = (stats[3:4] + stats[4:5])[:, 0:1]

    group = SUB // 2
    along = jnp.zeros((group, FRAMES), F32)
    row = lax.broadcasted_iota(jnp.int32, (LANES, LANES), 0)
    col = lax.broadcasted_iota(jnp.int32, (LANES, LANES), 1)
    for b in range(FRAMES // LANES):
        start = b * LANES
        width = FRAMES - start
        block = dot_t(all_ref[start : start + LANES], all_ref[start:])
        block = block * (inv_col[start : start + LANES, 0:1] * inv[:, start:])
        corner = jnp.where(col >= row, block[:, :LANES], 0.0)
        block = corner if width == LANES else jnp.concatenate([corner, block[:, LANES:]], axis=1)
        part = block[:group]
        for first in range(group, LANES, group):
            part = part + pltpu.roll(block[first : first + group], width - first, axis=1)
        if width < FRAMES:
            part = jnp.concatenate([part, jnp.zeros((group, start), F32)], axis=1)
        along = along + part
    place = lax.broadcasted_iota(jnp.int32, (group, FRAMES), 0)
    for step in (1, 2, 4):
        along = jnp.where((place & step) > 0, pltpu.roll(along, FRAMES - step, axis=1), along)
    lags = jnp.sum(along, axis=0, keepdims=True)
    remaining = (FRAMES - lax.broadcasted_iota(jnp.int32, (1, FRAMES), 1)).astype(F32)
    lags = lags * usable / remaining
    tail = jnp.concatenate(
        [lags[:, b * LANES : (b + 1) * LANES] for b in range(FRAMES // LANES)]
        + [jnp.zeros((4, LANES), F32)],
        axis=0,
    )

    own_sums = x0_ref[PAIRS * SEEN :].astype(F32)
    own = jnp.zeros((SUB // 2, LANES), F32)
    for z in range(N_Z):
        pieces = []
        for j in range(N_TROW):
            at = (j * N_Z + z) * SUB
            half = at // LANES * (SUB // 2)
            pieces.append(own_sums[half : half + SUB // 2, at % LANES : at % LANES + SUB])
        own = jnp.where(my_z == z, jnp.concatenate(pieces, axis=1), own)
    own_inv = usable / jnp.maximum(own[0:1] + own[1:2] + own[2:3], 1.0)
    for j in range(N_TROW):
        for pair in range(PAIRS):
            at = pl.ds(pl.multiple_of(pair * SEEN + j * N_Z * SUB + my_z * SUB, SUB), SUB)
            own_ref[j * SUB : (j + 1) * SUB, pair * LANES : (pair + 1) * LANES] = x0_ref[at]
    tile = dot_t(all_ref[...], own_ref[...]) * (inv_col * own_inv)
    for i in range(N_TROW):
        at = Y_ORDER.index(i)
        out_ref[at, :ROWS] = tile[i * ROWS : (i + 1) * ROWS]
        out_ref[at, ROWS:] = tail


def join_kernel(in_ref, tile_ref, lag_ref):
    for c in range(OWNED):
        both = in_ref[Y_ORDER.index(2 * c)] + in_ref[Y_ORDER.index(2 * c + 1)]
        tile_ref[c] = both[:ROWS]
        for b in range(FRAMES // LANES):
            lag_ref[c : c + 1, b * LANES : (b + 1) * LANES] = both[ROWS + b : ROWS + b + 1]


def call(body, out_shape, n_in, scalars=0, scratch=(), flops=0, size=0, source=pltpu.VMEM):
    vmem = pl.BlockSpec(memory_space=pltpu.VMEM)
    given = pl.BlockSpec(memory_space=source)
    smem = pl.BlockSpec(memory_space=pltpu.SMEM)
    many = isinstance(out_shape, tuple)
    return pl.pallas_call(
        body,
        out_shape=out_shape,
        in_specs=[smem] * scalars + [given] * n_in,
        out_specs=(vmem,) * len(out_shape) if many else vmem,
        scratch_shapes=list(scratch),
        compiler_params=pltpu.CompilerParams(vmem_limit_bytes=32 << 20),
        cost_estimate=pl.CostEstimate(flops=flops, bytes_accessed=size, transcendentals=0),
    )


def per_device(counts, labels, pixel_mask, dark_level, flat_field):
    turn = (lax.axis_index("pixel") & 1).astype(jnp.int32).reshape(1)
    core = lax.axis_index("core").astype(jnp.int32).reshape(1)
    z = lax.axis_index("z").astype(jnp.int32).reshape(1)
    payload = call(
        slot_kernel,
        jax.ShapeDtypeStruct((4 * CYCLES * MESSAGE, LANES), BF16),
        5,
        scalars=1,
        scratch=[
            pltpu.VMEM((1, PIX), jnp.int32),
            pltpu.VMEM((1, PIX), jnp.int32),
            pltpu.VMEM((1, PIX), F32),
            pltpu.VMEM((1, PIX), F32),
            pltpu.VMEM((SUB, PIX), jnp.int32),
        ]
        + [pltpu.SemaphoreType.DMA] * 5,
        flops=2 * CYCLES * SUB * CAP * PIX,
        size=1 << 20,
        source=pltpu.HBM,
    )(
        turn,
        *(
            pltpu.with_memory_space_constraint(x, pltpu.HBM)
            for x in (
                labels.reshape(1, PIX),
                pixel_mask.reshape(1, PIX),
                dark_level.reshape(1, PIX),
                flat_field.reshape(1, PIX),
                counts,
            )
        ),
    )
    order = [
        ((p ^ FIRST_PIXEL) * N_TROW + (y ^ FIRST_Y)) * N_Z + z
        for y in range(N_TROW)
        for z in range(N_Z)
        for p in range(N_PIXEL)
    ]
    arrived = lax.all_to_all(
        payload.reshape(4 * CYCLES, MESSAGE // 2, 2, LANES),
        ("pixel", "trow", "z"),
        0,
        0,
        tiled=True,
        axis_index_groups=[order],
    )
    packed = call(
        pack_kernel,
        jax.ShapeDtypeStruct((PAIRS * SEEN + SUB, LANES), BF16),
        1,
        flops=1 << 20,
        size=3 << 19,
    )(arrived.reshape(4 * CYCLES * MESSAGE, LANES))
    beside = lax.ppermute(packed, "core", [(0, 1), (1, 0)])
    depth = PAIRS * LANES
    sends = call(
        gram_kernel,
        jax.ShapeDtypeStruct((N_TROW, ROWS + 8, LANES), F32),
        2,
        scalars=2,
        scratch=[pltpu.VMEM((FRAMES, depth), BF16), pltpu.VMEM((COLS, depth), BF16)],
        flops=2 * FRAMES * FRAMES * depth,
        size=3 << 19,
    )(core, z, packed, beside)
    gets = lax.all_to_all(
        sends, "trow", 0, 0, tiled=True, axis_index_groups=[Y_ORDER]
    )
    return call(
        join_kernel,
        (
            jax.ShapeDtypeStruct((OWNED, ROWS, COLS), F32),
            jax.ShapeDtypeStruct((OWNED, FRAMES), F32),
        ),
        1,
        flops=1 << 16,
        size=1 << 19,
    )(gets)


def solution(mesh):
    fine = Mesh(
        mesh.devices.reshape(N_PIXEL, N_TROW, N_Z, 2), ("pixel", "trow", "z", "core")
    )
    frames = ("trow", "z", "core")
    placed = (P(frames, "pixel"), P("pixel", None), P("pixel"), P("pixel"), P("pixel"))
    return jax.shard_map(
        per_device,
        mesh=fine,
        in_specs=placed,
        out_specs=(P("pixel", "trow", ("z", "core")), P("pixel", None)),
        check_vma=False,
    )
```

```python
import jax
import jax.numpy as jnp
from jax import lax
from jax.experimental import pallas as pl
from jax.experimental.pallas import tpu as pltpu
from jax.sharding import PartitionSpec as P

CYCLES = 64
FRAMES = 512
CAP = 128
HALF = CAP // 2
PIX = 4096
N_PIXEL = 16
N_TROW = 8
N_TCOL = 4
SUB = 16
OWNED = CYCLES // N_PIXEL
COLS = N_TROW * SUB
PAIRS = N_PIXEL // 2
ROWS = N_TCOL * SUB
LANES = 128
MESSAGE = 10
FILLED = CYCLES // 2 * SUB
CHUNK = 512
RANK = 128
Y_ORDER = [4, 3, 5, 2, 6, 1, 7, 0]
FIRST_PIXEL, FIRST_Y = 10, 5
FIRST = FIRST_PIXEL * N_TROW + FIRST_Y
F32 = jnp.float32
BF16 = jnp.bfloat16


def dot_t(a, b):
    return lax.dot_general(a, b, (((1,), (1,)), ((), ())), preferred_element_type=F32)


def dot_n(a, b):
    return jnp.dot(a, b, preferred_element_type=F32)


def three_parts(x):
    hi = x.astype(BF16).astype(F32)
    rest = x - hi
    mid = rest.astype(BF16).astype(F32)
    return hi, mid, rest - mid


def slot_kernel(
    turn_ref,
    labels_hbm,
    mask_hbm,
    dark_hbm,
    flat_hbm,
    counts_hbm,
    out_ref,
    labels_ref,
    mask_ref,
    dark_ref,
    flat_ref,
    counts_ref,
    labels_sem,
    mask_sem,
    dark_sem,
    flat_sem,
    counts_sem,
):
    get_labels = pltpu.make_async_copy(labels_hbm, labels_ref, labels_sem)
    get_mask = pltpu.make_async_copy(mask_hbm, mask_ref, mask_sem)
    get_dark = pltpu.make_async_copy(dark_hbm, dark_ref, dark_sem)
    get_flat = pltpu.make_async_copy(flat_hbm, flat_ref, flat_sem)
    get_counts = pltpu.make_async_copy(counts_hbm, counts_ref, counts_sem)
    for get in (get_labels, get_mask, get_dark, get_flat, get_counts):
        get.start()
    turn = turn_ref[0]
    get_labels.wait()
    get_mask.wait()
    labels = labels_ref[...]
    live = mask_ref[...].astype(F32)

    before = lax.broadcasted_iota(jnp.int32, (RANK, RANK + LANES), 0)
    at = lax.broadcasted_iota(jnp.int32, (RANK, RANK + LANES), 1)
    ahead = jnp.where((before < at) | (at >= RANK), 1.0, 0.0).astype(BF16)
    cycle_of_row = lax.broadcasted_iota(jnp.int32, (CYCLES, RANK), 0)
    offset = jnp.zeros((CYCLES, LANES), F32)
    ranks = []
    for c in range(PIX // RANK):
        span = slice(c * RANK, (c + 1) * RANK)
        member = jnp.where(labels[:, span] == cycle_of_row, 1.0, 0.0)
        counted = dot_n(member.astype(BF16), ahead)
        place = counted[:, :RANK] + jnp.concatenate([offset] * (RANK // LANES), axis=1)
        ranks.append(jnp.sum(member * place, axis=0, keepdims=True))
        offset = offset + counted[:, RANK:]
    rank = jnp.concatenate(ranks, axis=1).astype(jnp.int32)
    back = labels ^ (FIRST // 2)
    slot = ((rank + turn * HALF) & (CAP - 1)) + (back & 1) * CAP
    slot16 = slot.astype(F32).astype(BF16)
    pair16 = (back >> 1).astype(F32).astype(BF16)

    get_dark.wait()
    get_flat.wait()
    get_counts.wait()
    frames = (
        flat_ref[...] * live * (counts_ref[...].astype(F32) - dark_ref[...])
    ).astype(BF16)
    live16 = live.astype(BF16)

    slots = jnp.zeros((FILLED + CYCLES // 2, 2 * CAP), F32)
    slot_of_row = lax.broadcasted_iota(jnp.int32, (2 * CAP, CHUNK), 0).astype(F32).astype(BF16)
    pairs = lax.broadcasted_iota(jnp.int32, (CYCLES // 2, CHUNK), 0).astype(F32).astype(BF16)
    one = jnp.ones((2 * CAP, CHUNK), BF16)
    none = jnp.zeros((SUB, CHUNK), BF16)
    for c in range(PIX // CHUNK):
        span = slice(c * CHUNK, (c + 1) * CHUNK)
        here = jnp.broadcast_to(pair16[:, span], (SUB, CHUNK))
        chunk = frames[:, span]
        usable = jnp.where(
            jnp.broadcast_to(pair16[:, span], (CYCLES // 2, CHUNK)) == pairs,
            jnp.broadcast_to(live16[:, span], (CYCLES // 2, CHUNK)),
            jnp.zeros((CYCLES // 2, CHUNK), BF16),
        )
        left = jnp.concatenate(
            [jnp.where(here == jnp.array(r, BF16), chunk, none) for r in range(CYCLES // 2)]
            + [usable],
            axis=0,
        )
        right = jnp.where(
            jnp.broadcast_to(slot16[:, span], (2 * CAP, CHUNK)) == slot_of_row,
            one,
            jnp.zeros_like(one),
        )
        slots = slots + dot_t(left, right)

    in_row = lax.broadcasted_iota(jnp.int32, (2 * CAP, 2 * CAP), 0) // CAP
    in_col = lax.broadcasted_iota(jnp.int32, (2 * CAP, 2 * CAP), 1) // CAP
    same = jnp.where(in_row == in_col, 1.0, 0.0).astype(BF16)
    sums = dot_n(slots.astype(BF16), same)
    counted = sums[FILLED:]
    sums = sums[:FILLED].reshape(CYCLES // 2, SUB, 2 * CAP)
    lane = lax.broadcasted_iota(jnp.int32, sums.shape, 2) % SUB
    sums = jnp.where(lane == lax.broadcasted_iota(jnp.int32, sums.shape, 1), sums, 0.0)
    hi, mid, lo = three_parts(jnp.sum(sums, axis=1))
    part = lax.broadcasted_iota(jnp.int32, (CYCLES // 2, 2 * CAP), 1) % CAP // SUB
    extra = jnp.where(part == 0, hi, jnp.where(part == 1, mid, jnp.where(part == 2, lo, counted)))
    shape = (CYCLES // 2, SUB // 2, LANES)
    extras = [
        jnp.broadcast_to(extra[:, b * LANES : (b + 1) * LANES][:, None, :], shape)
        for b in range(2)
    ]
    data = (lax.broadcasted_iota(jnp.int32, shape, 2) >= HALF) == (turn == 1)
    row = lax.broadcasted_iota(jnp.int32, shape, 1)
    slots = slots[:FILLED].reshape(CYCLES // 2, SUB, 2 * CAP)
    tiles = []
    for b in range(2):
        early = slots[:, : SUB // 2, b * CAP : (b + 1) * CAP]
        late = slots[:, SUB // 2 :, b * CAP : (b + 1) * CAP]
        lower = jnp.where(data, early, pltpu.roll(late, HALF, axis=2))
        upper = jnp.where(data, pltpu.roll(early, HALF, axis=2), late)
        tiles += [lower, upper] if FIRST % 2 == 0 else [upper, lower]
    second, third, fourth = (pltpu.roll(tiles[m], 2 * m, axis=1) for m in (1, 2, 3))
    groups = [
        tiles[0],
        jnp.where(row < 2, extras[0], second),
        jnp.where(row < 2, second, jnp.where(row < 4, extras[0], third)),
        jnp.where(row < 4, third, jnp.where(row < 6, extras[1], fourth)),
        jnp.where(row < 6, fourth, extras[1]),
    ]
    out_ref[...] = (
        jnp.concatenate(groups, axis=1).reshape(2 * CYCLES * MESSAGE, LANES).astype(BF16)
    )


def pack_kernel(in_ref, out_ref):
    per_shard = N_TROW * MESSAGE
    shape = (N_TROW, SUB // 2, LANES)
    low = lax.broadcasted_iota(jnp.int32, shape, 2) < HALF
    row = lax.broadcasted_iota(jnp.int32, (SUB // 2, LANES), 0)
    lane = lax.broadcasted_iota(jnp.int32, (SUB // 2, LANES), 1)
    total = jnp.zeros((per_shard, LANES), F32)
    for pair in range(PAIRS):
        halves = []
        for shard in ((2 * pair) ^ FIRST_PIXEL, (2 * pair + 1) ^ FIRST_PIXEL):
            rows = in_ref[shard * per_shard : (shard + 1) * per_shard].astype(F32)
            total = total + rows
            group = [rows[8 * i : 8 * i + 8] for i in range(per_shard // 8)]
            tiles = []
            for first in (0, 5):
                g = group[first : first + 5]
                tiles.append(g[0])
                tiles.append(pltpu.roll(jnp.where(row < 2, g[2], g[1]), 6, axis=0))
                tiles.append(pltpu.roll(jnp.where(row < 4, g[3], g[2]), 4, axis=0))
                tiles.append(pltpu.roll(jnp.where(row < 6, g[4], g[3]), 2, axis=0))
            tiles = [tiles[j ^ FIRST_Y] for j in range(N_TROW)]
            halves.append(jnp.concatenate(tiles, axis=0).reshape(shape))
        even, odd = halves
        early = jnp.where(low, even, odd)
        late = pltpu.roll(jnp.where(low, odd, even), HALF, axis=2)
        out_ref[pair * COLS : (pair + 1) * COLS] = (
            jnp.concatenate([early, late], axis=1).reshape(COLS, LANES).astype(BF16)
        )
    sums = jnp.zeros((SUB // 2, LANES), F32)
    usable = jnp.zeros((SUB // 2, LANES), F32)
    for j in range(N_TROW):
        at = (j ^ FIRST_Y) * MESSAGE + SUB // 2
        extra = jnp.broadcast_to(total[at : at + 1], (SUB // 2, LANES))
        added = extra + pltpu.roll(extra, LANES - SUB, axis=1)
        added = added + pltpu.roll(extra, LANES - 2 * SUB, axis=1)
        here = lane // SUB == j
        sums = jnp.where(here, pltpu.roll(added, j * SUB, axis=1), sums)
        count = pltpu.roll(extra, (LANES - 3 * SUB + j * SUB) % LANES, axis=1)
        usable = jnp.where(here, count, usable)
    hi, mid, lo = three_parts(sums)
    n_hi, n_lo, _ = three_parts(usable)
    tail = jnp.zeros((SUB // 2, LANES), F32)
    for i, x in enumerate((hi, mid, lo, n_hi, n_lo)):
        tail = jnp.where(row == i, x, tail)
    out_ref[PAIRS * COLS :] = jnp.concatenate([tail, jnp.zeros_like(tail)], axis=0).astype(BF16)


def gram_kernel(me_ref, x0_ref, x1_ref, x2_ref, x3_ref, out_ref, all_ref, own_ref):
    me = me_ref[0]
    depth = PAIRS * LANES
    t_row = lax.broadcasted_iota(jnp.int32, (COLS, FRAMES), 0)
    t_col = lax.broadcasted_iota(jnp.int32, (COLS, FRAMES), 1)
    stats = jnp.zeros((SUB, FRAMES), F32)
    for d, ref in enumerate((x0_ref, x1_ref, x2_ref, x3_ref)):
        k = me ^ d
        for j in range(N_TROW):
            rows = pl.ds(pl.multiple_of(j * ROWS + k * SUB, SUB), SUB)
            for pair in range(PAIRS):
                at = pair * COLS + j * SUB
                all_ref[rows, pair * LANES : (pair + 1) * LANES] = ref[at : at + SUB]
        goes_to = (t_row // SUB) * ROWS + k * SUB + t_row % SUB
        spread = jnp.where(goes_to == t_col, 1.0, 0.0).astype(BF16)
        stats = stats + dot_n(ref[PAIRS * COLS :], spread)
    for pair in range(PAIRS):
        own_ref[:, pair * LANES : (pair + 1) * LANES] = x0_ref[pair * COLS : (pair + 1) * COLS]

    own = x0_ref[PAIRS * COLS :].astype(F32)
    own_inv = 1.0 / jnp.maximum(own[0:1] + own[1:2] + own[2:3], 1.0)
    usable = (own[3:4] + own[4:5])[:, 0:1]
    inv = 1.0 / jnp.maximum(stats[0:1] + stats[1:2] + stats[2:3], 1.0)
    inv_col = jnp.broadcast_to(inv, (LANES, FRAMES)).T

    tile = dot_t(all_ref[...], own_ref[...])
    tile = tile * (inv_col * (own_inv * usable))

    group = SUB // 2
    along = jnp.zeros((group, FRAMES), F32)
    row = lax.broadcasted_iota(jnp.int32, (LANES, LANES), 0)
    col = lax.broadcasted_iota(jnp.int32, (LANES, LANES), 1)
    for b in range(FRAMES // LANES):
        start = b * LANES
        width = FRAMES - start
        block = dot_t(all_ref[start : start + LANES], all_ref[start:])
        block = block * (inv_col[start : start + LANES, 0:1] * inv[:, start:])
        corner = jnp.where(col >= row, block[:, :LANES], 0.0)
        block = corner if width == LANES else jnp.concatenate([corner, block[:, LANES:]], axis=1)
        part = block[:group]
        for first in range(group, LANES, group):
            part = part + pltpu.roll(block[first : first + group], width - first, axis=1)
        if width < FRAMES:
            part = jnp.concatenate([part, jnp.zeros((group, start), F32)], axis=1)
        along = along + part
    place = lax.broadcasted_iota(jnp.int32, (group, FRAMES), 0)
    for step in (1, 2, 4):
        along = jnp.where((place & step) > 0, pltpu.roll(along, FRAMES - step, axis=1), along)
    lags = jnp.sum(along, axis=0, keepdims=True)
    remaining = (FRAMES - lax.broadcasted_iota(jnp.int32, (1, FRAMES), 1)).astype(F32)
    lags = lags * usable / remaining

    for i in range(N_TROW):
        at = Y_ORDER.index(i)
        out_ref[at, :ROWS] = tile[i * ROWS : (i + 1) * ROWS]
        for b in range(FRAMES // LANES):
            out_ref[at, ROWS + b : ROWS + b + 1] = lags[:, b * LANES : (b + 1) * LANES]
        out_ref[at, ROWS + 4 :] = jnp.zeros((4, LANES), F32)


def join_kernel(in_ref, tile_hbm, lag_ref, tile_ref, sems):
    puts = []
    for c in range(OWNED):
        both = in_ref[Y_ORDER.index(2 * c)] + in_ref[Y_ORDER.index(2 * c + 1)]
        tile_ref[c] = both[:ROWS]
        put = pltpu.make_async_copy(tile_ref.at[c], tile_hbm.at[c], sems.at[c])
        put.start()
        puts.append(put)
        for b in range(FRAMES // LANES):
            lag_ref[c : c + 1, b * LANES : (b + 1) * LANES] = both[ROWS + b : ROWS + b + 1]
    for put in puts:
        put.wait()


def call(body, out_shape, n_in, scalars=0, scratch=(), flops=0, size=0, source=pltpu.VMEM, first_out=pltpu.VMEM):
    vmem = pl.BlockSpec(memory_space=pltpu.VMEM)
    given = pl.BlockSpec(memory_space=source)
    smem = pl.BlockSpec(memory_space=pltpu.SMEM)
    many = isinstance(out_shape, tuple)
    return pl.pallas_call(
        body,
        out_shape=out_shape,
        in_specs=[smem] * scalars + [given] * n_in,
        out_specs=(pl.BlockSpec(memory_space=first_out), vmem) if many else vmem,
        scratch_shapes=list(scratch),
        compiler_params=pltpu.CompilerParams(vmem_limit_bytes=32 << 20),
        cost_estimate=pl.CostEstimate(flops=flops, bytes_accessed=size, transcendentals=0),
    )


def per_device(counts, labels, pixel_mask, dark_level, flat_field):
    turn = (lax.axis_index("pixel") & 1).astype(jnp.int32).reshape(1)
    me = lax.axis_index("tcol").astype(jnp.int32).reshape(1)
    payload = call(
        slot_kernel,
        jax.ShapeDtypeStruct((2 * CYCLES * MESSAGE, LANES), BF16),
        5,
        scalars=1,
        scratch=[
            pltpu.VMEM((1, PIX), jnp.int32),
            pltpu.VMEM((1, PIX), jnp.int32),
            pltpu.VMEM((1, PIX), F32),
            pltpu.VMEM((1, PIX), F32),
            pltpu.VMEM((SUB, PIX), jnp.int32),
        ]
        + [pltpu.SemaphoreType.DMA] * 5,
        flops=2 * CYCLES * SUB * CAP * PIX,
        size=1 << 20,
        source=pltpu.HBM,
    )(
        turn,
        *(
            pltpu.with_memory_space_constraint(x, pltpu.HBM)
            for x in (
                labels.reshape(1, PIX),
                pixel_mask.reshape(1, PIX),
                dark_level.reshape(1, PIX),
                flat_field.reshape(1, PIX),
                counts,
            )
        ),
    )
    arrived = lax.all_to_all(
        payload.reshape(2 * CYCLES, MESSAGE // 2, 2, LANES),
        ("pixel", "trow"),
        0,
        0,
        tiled=True,
        axis_index_groups=[[m ^ FIRST for m in range(N_PIXEL * N_TROW)]],
    )
    packed = call(
        pack_kernel,
        jax.ShapeDtypeStruct((PAIRS * COLS + SUB, LANES), BF16),
        1,
        flops=1 << 20,
        size=3 << 18,
    )(arrived.reshape(2 * CYCLES * MESSAGE, LANES))
    beside = lax.ppermute(packed, "tcol", [(k, k ^ 1) for k in range(N_TCOL)])
    across = lax.ppermute(packed, "tcol", [(k, k ^ 2) for k in range(N_TCOL)])
    corner = lax.ppermute(across, "tcol", [(k, k ^ 1) for k in range(N_TCOL)])
    depth = PAIRS * LANES
    sends = call(
        gram_kernel,
        jax.ShapeDtypeStruct((N_TROW, ROWS + 8, LANES), F32),
        4,
        scalars=1,
        scratch=[pltpu.VMEM((FRAMES, depth), BF16), pltpu.VMEM((COLS, depth), BF16)],
        flops=2 * FRAMES * FRAMES * depth,
        size=3 << 19,
    )(me, packed, beside, across, corner)
    gets = lax.all_to_all(sends, "trow", 0, 0, tiled=True, axis_index_groups=[Y_ORDER])
    return call(
        join_kernel,
        (
            jax.ShapeDtypeStruct((OWNED, ROWS, COLS), F32),
            jax.ShapeDtypeStruct((OWNED, FRAMES), F32),
        ),
        1,
        scratch=[pltpu.VMEM((OWNED, ROWS, COLS), F32), pltpu.SemaphoreType.DMA((OWNED,))],
        first_out=pltpu.HBM,
        flops=1 << 16,
        size=1 << 19,
    )(gets)


def solution(mesh):
    placed = (P(("trow", "tcol"), "pixel"), P("pixel", None), P("pixel"), P("pixel"), P("pixel"))
    return jax.shard_map(
        per_device,
        mesh=mesh,
        in_specs=placed,
        out_specs=(P("pixel", "trow", "tcol"), P("pixel", None)),
        check_vma=False,
    )
```
